32 devices in a mesh: batch: 8 (over z, y), seq: 4 (over x, core).
Axes of the slice: x: 2, y: 2, z: 4, core: 2. Of those that a mesh axis runs over, the one named last changes fastest.
Arguments:
- tokens: bfloat16 [16384, 768], P(('batch', 'seq')), may hold values from -6 to 6
- segment_ids: int32 [16384], P(('batch', 'seq')), may hold values from 0 to 2047, as said below
- cotangent: bfloat16 [16384, 768], P(('batch', 'seq')), may hold values from -6 to 6
- w_q: bfloat16 [768, 768], replicated, may hold values from -0.21875 to 0.21875
- w_k: bfloat16 [768, 768], replicated, may hold values from -0.21875 to 0.21875
- w_v: bfloat16 [768, 768], replicated, may hold values from -0.21875 to 0.21875
- conv_weight: float32 [3, 3, 768], replicated, may hold values from -3 to 3
- w_o: bfloat16 [768, 768], replicated, may hold values from -0.875 to 0.875
- gain_one: float32 [768], replicated, may hold values from 0.5 to 1.5
- bias_one: float32 [768], replicated, may hold values from -1.5 to 1.5
- gain_two: float32 [768], replicated, may hold values from 0.5 to 1.5
- bias_two: float32 [768], replicated, may hold values from -1.5 to 1.5
- w_up: bfloat16 [768, 3072], replicated, may hold values from -0.21875 to 0.21875
- w_down: bfloat16 [3072, 768], replicated, may hold values from -0.109375 to 0.109375
Outputs:
- mixed: bfloat16 [16384, 768], P(('batch', 'seq'))
- d_tokens: bfloat16 [16384, 768], P(('batch', 'seq'))
- grad_w_q: float32 [768, 768], P(None, ('batch', 'seq'))
- grad_w_k: float32 [768, 768], P(None, ('batch', 'seq'))
- grad_w_v: float32 [768, 768], P(None, ('batch', 'seq'))
- grad_conv: float32 [3, 3, 768], P(None, None, ('batch', 'seq'))
- grad_w_o: float32 [768, 768], P(None, ('batch', 'seq'))
- grad_gain_one: float32 [768], P(('batch', 'seq'))
- grad_bias_one: float32 [768], P(('batch', 'seq'))
- grad_gain_two: float32 [768], P(('batch', 'seq'))
- grad_bias_two: float32 [768], P(('batch', 'seq'))
- grad_w_up: float32 [768, 3072], P(None, ('batch', 'seq'))
- grad_w_down: float32 [3072, 768], P(None, ('batch', 'seq'))
The draws below stay inside these ranges and needn't reach their ends.
Inputs may be any that keep to these rules, and one draw needn't show every extreme that they name: `segment_ids`: within each packed sequence of 2048 rows the ids never fall, each equals the position in the sequence of its document's first row, one document starts within the first 512 rows after row 0 and ends within the last 512 rows, and the last row starts a document of its own.
All inputs are finite; a program needn't handle non-finite values.
Results may differ from the reference program's by a relative error of at most 0.015.
The reference program's roundings to bfloat16 on the way count: a program that leaves them out, or rounds other values in their place, can miss the bound.
Values may be sent and summed in bfloat16 or wider, within the bound.
No kernel may reach another device: no remote copies, remote signals or barrier semaphores. Data moves between devices by JAX's collectives and lax.ppermute only.
A program may use at most 256 MiB of HBM per device.

```python
import jax
import jax.numpy as jnp
from jax import lax

D = 768
HEADS = 12
HEAD_DIM = 64
FF = 3072
ROWS = 512
LEN = 2048
GROUPS = 8
TOKENS = 16384


def draw_segment_ids(key, part):
    key = jax.random.fold_in(key, 11)
    key_flags, key_begin, key_end = jax.random.split(key, 3)
    positions = jnp.arange(LEN, dtype=jnp.int32)[None, :]
    boundary = (jax.random.randint(key_flags, (GROUPS, LEN), 0, 48) == 0).astype(jnp.int32)
    long_begin = jax.random.randint(key_begin, (GROUPS, 1), 1, ROWS)
    long_end = jax.random.randint(key_end, (GROUPS, 1), LEN - ROWS, LEN - 1)
    inside = (positions > long_begin) & (positions <= long_end)
    boundary = jnp.where(inside, 0, boundary)
    marked = (positions == long_begin) | (positions == long_end + 1) | (positions == 0) | (positions == LEN - 1)
    boundary = jnp.where(marked, 1, boundary)
    starts = lax.cummax(boundary * positions, axis=1)
    return starts.reshape(-1).astype(jnp.int32)


def with_spikes(entries, stream_key, source, target, parts, factor):
    owner, partner = [(jnp.arange(entries.shape[dim]) // (entries.shape[dim] // parts)).reshape([-1 if axis == dim else 1 for axis in range(entries.ndim)]) for dim in (source, target)]
    chosen = jax.random.permutation(stream_key, parts)[partner]
    strong = (owner == chosen) | (owner == (partner + parts // 2) % parts)
    return jnp.where(strong, factor * entries, entries)


def block_levels(rng, extent, cuts, smallest, largest):
    def one(dim, parts):
        draws = jax.random.uniform(jax.random.fold_in(jax.random.fold_in(rng, 6), dim), (parts,), jnp.float32, smallest / len(cuts), largest / len(cuts))
        return jnp.repeat(jnp.exp(draws), extent[dim] // parts).reshape((-1,) + (1,) * (len(extent) - dim - 1))

    level = one(*cuts[0])
    for cut in cuts[1:]:
        level = level * one(*cut)
    return level


def normal_values(stream_key, shape, scale, reach, cuts=(), kind=jnp.bfloat16):
    drawn = jax.random.normal(stream_key, shape, jnp.float32) * scale
    if len(cuts) > 0:
        drawn = block_levels(stream_key, shape, cuts, -0.22, 0.18) * drawn
    return jnp.clip(drawn, min=-reach, max=reach).astype(kind)


def bell_draw_with(rng, shape, width, bound, cuts, heavy, kind=jnp.bfloat16):
    values = width * jax.random.normal(rng, shape, jnp.float32)
    if cuts:
        values = values * block_levels(rng, shape, cuts, -0.22, 0.18)
    return jnp.clip(with_spikes(values, jax.random.fold_in(rng, 3), *heavy), -bound, bound).astype(kind)


def setup_inputs(seed: int = 0) -> dict:
    key_of = jax.random.split(jax.random.key(seed), 15)
    tokens = normal_values(key_of[0], (TOKENS, D), 1.0, 6.0, ((0, 32),))
    segment_ids = draw_segment_ids(jax.random.fold_in(key_of[14], 71), 0)
    cotangent = bell_draw_with(key_of[2], (TOKENS, D), 1.0, 6.0, ((0, 32),), (0, 1, 32, 2.75))
    w_q = normal_values(key_of[3], (D, D), D ** -0.5, 0.21875)
    w_k = normal_values(key_of[4], (D, D), D ** -0.5, 0.21875)
    w_v = normal_values(key_of[5], (D, D), D ** -0.5, 0.21875)
    conv_weight = normal_values(key_of[6], (3, 3, D), 0.7, 3.0, (), jnp.float32)
    w_o = normal_values(key_of[7], (D, D), (D // 16) ** -0.5, 0.875)
    gain_one = jnp.clip(1.0 + 0.1 * jax.random.normal(key_of[8], (D,), jnp.float32), 0.5, 1.5)
    bias_one = normal_values(key_of[9], (D,), 0.3, 1.5, (), jnp.float32)
    gain_two = jnp.clip(1.0 + 0.1 * jax.random.normal(key_of[10], (D,), jnp.float32), 0.5, 1.5)
    bias_two = normal_values(key_of[11], (D,), 0.3, 1.5, (), jnp.float32)
    w_up = normal_values(key_of[12], (D, FF), D ** -0.5, 0.21875)
    w_down = normal_values(key_of[13], (FF, D), FF ** -0.5, 0.109375)
    return dict(tokens=tokens, segment_ids=segment_ids, cotangent=cotangent, w_q=w_q, w_k=w_k, w_v=w_v, conv_weight=conv_weight, w_o=w_o, gain_one=gain_one, bias_one=bias_one, gain_two=gain_two, bias_two=bias_two, w_up=w_up, w_down=w_down)


HIGH = lax.Precision.HIGHEST

@jax.custom_vjp
def low(v):
    return lax.optimization_barrier(v.astype(jnp.bfloat16)).astype(jnp.float32)

@jax.custom_vjp
def low_back(v):
    return v

def low_keep(v):
    return (low(v), None)

def low_pass(kept, grad):
    return (grad,)

def back_keep(v):
    return (v, None)

def back_low(kept, grad):
    return (low(grad),)
low.defvjp(low_keep, low_pass)
low_back.defvjp(back_keep, back_low)

def norm_rows(values, gain, bias):
    centred = values - lax.optimization_barrier(jnp.mean(values, axis=-1, keepdims=True))
    variance = lax.optimization_barrier(jnp.mean(centred * centred, axis=-1, keepdims=True))
    return centred * lax.rsqrt(variance + 1e-05) * gain + bias

def causal_conv(values, conv_taps, doc_starts):
    result = conv_taps[0] * values
    for offset in (1, 2):
        earlier = jnp.concatenate([jnp.full((offset,), -1, jnp.int32), doc_starts[:-offset]])
        moved = jnp.concatenate([jnp.zeros((offset, values.shape[1]), values.dtype), values[:-offset]], 0)
        result = result + conv_taps[offset] * jnp.where((earlier == doc_starts)[:, None], moved, 0.0)
    return result

def attention(queries, keys_all, values_all, doc_starts):
    length = queries.shape[0]
    block_rows = min(512, length)
    positions = jnp.arange(length).astype(jnp.int32)

    def one_block(block_start):
        query_block = lax.dynamic_slice_in_dim(queries, block_start, block_rows, 0)
        row_pos = block_start + jnp.arange(block_rows).astype(jnp.int32)
        doc_block = lax.dynamic_slice_in_dim(doc_starts, block_start, block_rows, 0)
        allowed = (positions[None, :] <= row_pos[:, None]) & (doc_block[:, None] == doc_starts[None, :])
        scores = jnp.einsum('qhd,khd->hqk', query_block, keys_all, precision=HIGH) * HEAD_DIM ** (-0.5)
        scores = jnp.where(allowed[None], low_back(scores), -1e+30)
        probability = jax.nn.softmax(scores, axis=-1)
        return jnp.einsum('hqk,khd->qhd', low(probability), values_all, precision=HIGH)
    starts = (jnp.arange(length // block_rows) * block_rows).astype(jnp.int32)
    blocks = lax.map(jax.checkpoint(one_block), starts)
    return blocks.reshape(queries.shape)

def primer_layer(inputs, doc_starts, w_q, w_k, w_v, conv_weight, w_o, gain_one, bias_one, gain_two, bias_two, w_up, w_down):
    normed_in = low(norm_rows(inputs, gain_one, bias_one))
    query_rows = low_back(low(jnp.dot(normed_in, w_q, precision=HIGH)))
    key_rows = low_back(low(jnp.dot(normed_in, w_k, precision=HIGH)))
    value_rows = low_back(low(jnp.dot(normed_in, w_v, precision=HIGH)))
    query_conv = low(causal_conv(query_rows, conv_weight[0], doc_starts))
    key_conv = low(causal_conv(key_rows, conv_weight[1], doc_starts))
    value_conv = low(causal_conv(value_rows, conv_weight[2], doc_starts))
    split_shape = (inputs.shape[0], HEADS, HEAD_DIM)
    attended = attention(query_conv.reshape(split_shape), key_conv.reshape(split_shape), value_conv.reshape(split_shape), doc_starts)
    attended = low_back(low(attended.reshape(inputs.shape)))
    middle = inputs + low_back(jnp.dot(attended, w_o, precision=HIGH))
    normed_mid = low(norm_rows(middle, gain_two, bias_two))
    hidden_pre = low_back(jnp.dot(normed_mid, w_up, precision=HIGH))
    hidden = low(jnp.square(jnp.maximum(hidden_pre, 0.0)))
    return middle + low_back(jnp.dot(hidden, w_down, precision=HIGH))

def reference(tokens, segment_ids, cotangent, w_q, w_k, w_v, conv_weight, w_o, gain_one, bias_one, gain_two, bias_two, w_up, w_down):
    params = tuple((p.astype(jnp.float32) for p in (w_q, w_k, w_v, conv_weight, w_o, gain_one, bias_one, gain_two, bias_two, w_up, w_down)))
    inputs_all = tokens.astype(jnp.float32).reshape(GROUPS, LEN, D)
    starts_all = segment_ids.reshape(GROUPS, LEN)
    cotan_all = cotangent.astype(jnp.float32).reshape(GROUPS, LEN, D)

    def one_group(running, element):
        inputs, doc_starts, cotan = element

        def layer_of(values, *weights):
            return primer_layer(values, doc_starts, *weights)
        result, pullback = jax.vjp(layer_of, inputs, *params)
        gradients = pullback(cotan)
        running = tuple((a + b for a, b in zip(running, gradients[1:])))
        return (running, (result.astype(jnp.bfloat16), gradients[0].astype(jnp.bfloat16)))
    zeros_init = tuple((jnp.zeros(p.shape, jnp.float32) for p in params))
    totals, (results, input_grads) = lax.scan(one_group, zeros_init, (inputs_all, starts_all, cotan_all))
    return (results.reshape(TOKENS, D), input_grads.reshape(TOKENS, D), totals[0], totals[1], totals[2], totals[3], totals[4], totals[5], totals[6], totals[7], totals[8], totals[9], totals[10])
```

```python
import functools
import math

import jax
import jax.numpy as jnp
from jax import lax
from jax.experimental import pallas as pl
from jax.experimental.pallas import tpu as pltpu
from jax.sharding import PartitionSpec as P

HEAD_DIM = 64
EPS = 1e-05
NEG_FILL = -1e30
LONG = 512
LOG2E = math.log2(math.e)
BF = jnp.bfloat16
F32 = jnp.float32
VMEM_LIMIT = 60 * 1024 * 1024


def nn(first, second):
    return lax.dot_general(first, second, (((1,), (0,)), ((), ())), preferred_element_type=F32)


def nt(first, second):
    return lax.dot_general(first, second, (((1,), (1,)), ((), ())), preferred_element_type=F32)


def tn(first, second):
    return lax.dot_general(first, second, (((0,), (0,)), ((), ())), preferred_element_type=F32)


def norm_stats(values):
    centred = values - jnp.mean(values, axis=-1, keepdims=True)
    variance = jnp.mean(centred * centred, axis=-1, keepdims=True)
    inv_scale = lax.rsqrt(variance + EPS)
    return (centred * inv_scale, inv_scale)


def norm_back(grad_out, normed, inv_scale, gain):
    grad_norm = grad_out * gain
    projected = (
        grad_norm
        - jnp.mean(grad_norm, -1, keepdims=True)
        - normed * jnp.mean(grad_norm * normed, -1, keepdims=True)
    )
    return (projected * inv_scale, jnp.sum(grad_out * normed, 0, keepdims=True), jnp.sum(grad_out, 0, keepdims=True))


def lag_mask(starts, positions, lag):
    return positions - lag >= starts


def project_kernel(ns, place, *refs):
    toks, ids = (refs[:ns], refs[ns : 2 * ns])
    gain, bias, weights, taps = refs[2 * ns : 2 * ns + 4]
    raw, conv, normed_out, starts_out = refs[2 * ns + 4 :]
    rows = toks[0].shape[0]
    for k in range(ns):
        begin = pl.multiple_of((place[0] ^ k) * rows, rows)
        normed, _ = norm_stats(toks[k][...].astype(F32))
        low = (normed * gain[...] + bias[...]).astype(BF)
        normed_out[pl.ds(begin, rows), :] = low
        raw[:, pl.ds(begin, rows)] = nt(weights[...], low).astype(BF)
        starts_out[:, pl.ds(begin, rows)] = ids[k][...]
    starts = starts_out[...]
    positions = lax.broadcasted_iota(jnp.int32, starts.shape, 1)
    step = HEAD_DIM
    for r in range(0, raw.shape[0], step):
        values = raw[r : r + step, :].astype(F32)
        result = taps[r : r + step, 0:1] * values
        for lag in (1, 2):
            moved = jnp.where(lag_mask(starts, positions, lag), pltpu.roll(values, lag, 1), 0.0)
            result = result + taps[r : r + step, lag : lag + 1] * moved
        conv[r : r + step, :] = result.astype(BF)


def masked_scores(scores, starts, key_begin, query_begin, length):
    keys, queries = scores.shape
    diagonal = key_begin + keys > query_begin
    inside = key_begin >= LONG and query_begin + queries <= length - LONG
    if inside and not diagonal:
        return scores
    key_pos = key_begin + lax.broadcasted_iota(jnp.int32, scores.shape, 0)
    allowed = None
    if not inside:
        allowed = key_pos >= starts
    if diagonal:
        query_pos = query_begin + lax.broadcasted_iota(jnp.int32, scores.shape, 1)
        causal = key_pos <= query_pos
        allowed = causal if allowed is None else allowed & causal
    return jnp.where(allowed, scores, NEG_FILL)


def attend_kernel(ns, block, place, starts_ref, qkv, *outs):
    pieces, out_full, lse_out = (outs[:ns], outs[ns], outs[ns + 1])
    length = qkv.shape[1]
    rows = length // ns
    keys = jnp.transpose(qkv[HEAD_DIM : 2 * HEAD_DIM, :])
    factor = LOG2E * HEAD_DIM ** (-0.5)
    for q in range(0, length, block):
        queries = qkv[0:HEAD_DIM, q : q + block]
        starts = starts_ref[:, q : q + block]
        scores = [
            masked_scores(nn(keys[u : u + block], queries), starts, u, q, length) * factor
            for u in range(0, q + block, block)
        ]
        top = scores[0]
        for one in scores[1:]:
            top = jnp.maximum(top, one)
        top = jnp.max(top, 0, keepdims=True)
        total = jnp.zeros((8, block), F32)
        result = jnp.zeros((HEAD_DIM, block), F32)
        for index, one in enumerate(scores):
            prob = jnp.exp2(one - top)
            total = total + jnp.sum(prob.reshape(block // 8, 8, block), 0)
            values = qkv[2 * HEAD_DIM :, index * block : (index + 1) * block]
            result = result + nn(values, prob.astype(BF))
        total = jnp.sum(total, 0, keepdims=True)
        lse_out[:, q : q + block] = top + jnp.log2(total)
        out_full[:, q : q + block] = result / total
    for k in range(ns):
        begin = pl.multiple_of((place[0] ^ k) * rows, rows)
        pieces[k][...] = out_full[:, pl.ds(begin, rows)].astype(BF)


def attend_back_kernel(ns, block, place, starts_ref, conv, raw, taps, normed, out_full, lse, *refs):
    grads_in, grads_out, grad_w = (refs[:ns], refs[ns : 2 * ns], refs[2 * ns])
    grad_attn, grad_conv, grad_raw = refs[2 * ns + 1 :]
    length = conv.shape[1]
    rows = length // ns
    head_scale = HEAD_DIM ** (-0.5)
    factor = LOG2E * head_scale
    for k in range(ns):
        begin = pl.multiple_of((place[0] ^ k) * rows, rows)
        grad_attn[:, pl.ds(begin, rows)] = grads_in[k][...]
    delta = jnp.sum(grad_attn[...].astype(F32) * out_full[...], 0, keepdims=True)
    keys = jnp.transpose(conv[HEAD_DIM : 2 * HEAD_DIM, :])
    values = jnp.transpose(conv[2 * HEAD_DIM :, :])
    grad_conv[HEAD_DIM:, :] = jnp.zeros((2 * HEAD_DIM, length), F32)
    for q in range(0, length, block):
        queries = conv[0:HEAD_DIM, q : q + block]
        grad_block = grad_attn[:, q : q + block]
        starts = starts_ref[:, q : q + block]
        grad_query = jnp.zeros((HEAD_DIM, block), F32)
        for u in range(0, q + block, block):
            scores = masked_scores(nn(keys[u : u + block], queries), starts, u, q, length)
            prob = jnp.exp2(scores * factor - lse[:, q : q + block])
            grad_prob = nn(values[u : u + block], grad_block)
            grad_scores = (prob * (grad_prob - delta[:, q : q + block])).astype(BF)
            grad_query = grad_query + nn(conv[HEAD_DIM : 2 * HEAD_DIM, u : u + block], grad_scores)
            grad_conv[HEAD_DIM : 2 * HEAD_DIM, u : u + block] += nt(queries, grad_scores)
            grad_conv[2 * HEAD_DIM :, u : u + block] += nt(grad_block, prob.astype(BF))
        grad_conv[0:HEAD_DIM, q : q + block] = grad_query
    starts = starts_ref[...]
    positions = lax.broadcasted_iota(jnp.int32, starts.shape, 1)
    tap_columns = []
    for part in range(3):
        at = slice(part * HEAD_DIM, (part + 1) * HEAD_DIM)
        grad = grad_conv[at, :] * (head_scale if part < 2 else 1.0)
        inputs = raw[at, :].astype(F32)
        result = taps[at, 0:1] * grad
        sums = [jnp.sum(grad * inputs, 1, keepdims=True)]
        for lag in (1, 2):
            kept = jnp.where(lag_mask(starts, positions, lag), grad, 0.0)
            result = result + taps[at, lag : lag + 1] * pltpu.roll(kept, length - lag, 1)
            sums.append(jnp.sum(kept * pltpu.roll(inputs, lag, 1), 1, keepdims=True))
        grad_raw[at, :] = result.astype(BF)
        lane = lax.broadcasted_iota(jnp.int32, (HEAD_DIM, 128), 1)
        tap_columns.append(
            jnp.where(lane == 0, sums[0], jnp.where(lane == 1, sums[1], jnp.where(lane == 2, sums[2], 0.0)))
        )
    width = normed.shape[1]
    grad_w[:, :width] = nn(grad_raw[...], normed[...]).astype(BF)
    for part in range(3):
        grad_w[part * HEAD_DIM : (part + 1) * HEAD_DIM, width:] = tap_columns[part].astype(BF)
    for k in range(ns):
        begin = pl.multiple_of((place[0] ^ k) * rows, rows)
        grads_out[k][...] = grad_raw[:, pl.ds(begin, rows)]


def middle_kernel(ns, heads, place, *refs):
    count = ns * heads
    pieces = refs[:count]
    tokens, w_o, cotangent, gain, bias, w_up, w_down = refs[count : count + 7]
    outs = refs[count + 7 : count + 15 + ns]
    mixed, grad_middle, grad_low, hidden_out, grad_pre_out, normed_low, attn_out, sums = outs[:8]
    grad_attn = outs[8:]
    middle, normed_two, grad_normed = refs[count + 15 + ns :]
    step = pl.program_id(0)
    head_rows = heads * HEAD_DIM

    @pl.when(step == 0)
    def _():
        for k in range(ns):
            for h in range(heads):
                begin = pl.multiple_of((place[0] ^ k) * head_rows + h * HEAD_DIM, HEAD_DIM)
                attn_out[pl.ds(begin, HEAD_DIM), :] = pieces[h * ns + k][...]
        value = tokens[...].astype(F32) + tn(attn_out[...], w_o[...])
        normed, _ = norm_stats(value)
        middle[...] = value
        normed_two[...] = normed
        normed_low[...] = (normed * gain[...] + bias[...]).astype(BF)
        grad_normed[...] = jnp.zeros_like(grad_normed)

    positive = jnp.maximum(nn(normed_low[...], w_up[...]), 0.0)
    hidden = (positive * positive).astype(BF)
    hidden_out[...] = hidden
    grad_pre = (nt(cotangent[...], w_down[...]) * (2.0 * positive)).astype(BF)
    grad_pre_out[...] = grad_pre
    middle[...] += nn(hidden, w_down[...])
    grad_normed[...] += nt(grad_pre, w_up[...])

    @pl.when(step == pl.num_programs(0) - 1)
    def _():
        mixed[...] = middle[...].astype(BF)
        value = tokens[...].astype(F32) + tn(attn_out[...], w_o[...])
        _, inv_scale = norm_stats(value)
        back, grad_gain, grad_bias = norm_back(grad_normed[...], normed_two[...], inv_scale, gain[...])
        total = cotangent[...].astype(F32) + back
        grad_middle[...] = total
        low = total.astype(BF)
        grad_low[...] = low
        row = lax.broadcasted_iota(jnp.int32, sums.shape, 0)
        sums[...] = jnp.where(row == 0, grad_gain, jnp.where(row == 1, grad_bias, 0.0))
        for k in range(ns):
            begin = pl.multiple_of((place[0] ^ k) * head_rows, head_rows)
            grad_attn[k][...] = nt(w_o[pl.ds(begin, head_rows), :], low).astype(BF)


def weight_kernel(cotangent, hidden, grad_pre, normed_low, grad_low, attn, sums, grad_down, grad_rest, grad_up, flipped):
    @pl.when(pl.program_id(0) == 0)
    def _():
        flipped[...] = jnp.transpose(cotangent[...])
        width = attn.shape[0]
        grad_rest[:, :width] = nt(jnp.transpose(grad_low[...]), attn[...]).astype(BF)
        filled = jnp.concatenate([sums[...], jnp.zeros((128 - sums.shape[0], width), F32)], 0)
        grad_rest[:, width:] = jnp.transpose(filled).astype(BF)

    grad_down[...] = nn(flipped[...], hidden[...]).astype(BF)
    grad_up[...] = nn(jnp.transpose(grad_pre[...]), normed_low[...]).astype(BF)


def final_kernel(ns, heads, place, *refs):
    count = ns * heads
    pieces = refs[:count]
    weights, tokens, gain, grad_middle = refs[count : count + 4]
    d_tokens, sums, stacked = refs[count + 4 :]
    part = 3 * HEAD_DIM
    for k in range(ns):
        for h in range(heads):
            begin = pl.multiple_of(((place[0] ^ k) * heads + h) * part, part)
            stacked[pl.ds(begin, part), :] = pieces[h * ns + k][...]
    grad_normed = tn(stacked[...], weights[...])
    normed, inv_scale = norm_stats(tokens[...].astype(F32))
    back, grad_gain, grad_bias = norm_back(grad_normed, normed, inv_scale, gain[...])
    d_tokens[...] = (grad_middle[...] + back).astype(BF)
    row = lax.broadcasted_iota(jnp.int32, sums.shape, 0)
    sums[...] = jnp.where(row == 0, grad_gain, jnp.where(row == 1, grad_bias, 0.0))


def whole(shape):
    return pl.BlockSpec(shape, lambda *_: (0,) * len(shape))


def shaped(shape, dtype):
    return jax.ShapeDtypeStruct(shape, dtype)


def call(kernel, grid, in_specs, out_specs, out_shape, scratch, flops, moved, name):
    return pl.pallas_call(
        kernel,
        grid_spec=pltpu.PrefetchScalarGridSpec(
            num_scalar_prefetch=1, grid=grid, in_specs=in_specs, out_specs=out_specs, scratch_shapes=scratch
        ),
        out_shape=out_shape,
        compiler_params=pltpu.CompilerParams(vmem_limit_bytes=VMEM_LIMIT),
        cost_estimate=pl.CostEstimate(flops=flops, bytes_accessed=moved, transcendentals=0),
        name=name,
    )


def swap(values, axis, count, mask):
    return lax.ppermute(values, axis, [(i, i ^ mask) for i in range(count)])


def add_all(first, others):
    total = first.astype(F32)
    for one in others:
        total = total + one.astype(F32)
    return total


def reduce_over(values, dim, axis, low, size):
    count = lax.axis_size(axis)
    while size > 4:
        values, size, low = (reduce_over(values, dim, axis, low, 4), size // 4, low * 4)
    if size == 1:
        return values
    mine = (lax.axis_index(axis) // low) % size
    block = values.shape[dim] // size

    def part(m):
        return lax.dynamic_slice_in_dim(values, (mine ^ m) * block, block, dim)

    others = [swap(part(m), axis, count, m * low) for m in range(1, size)]
    return add_all(part(0), others).astype(BF)


def digits(index, low, size):
    place = 0
    while size > 4:
        place, size, low = (place * 4 + (index // low) % 4, size // 4, low * 4)
    return place * size + (index // low) % size


def local(tokens, segment_ids, cotangent, w_q, w_k, w_v, conv_weight, w_o, gain_one, bias_one, gain_two, bias_two, w_up, w_down):
    ns, nb = (lax.axis_size("seq"), lax.axis_size("batch"))
    seq_index = lax.axis_index("seq")
    rows, width = tokens.shape
    units = w_up.shape[1]
    heads_all = width // HEAD_DIM
    heads = heads_all // ns
    length = rows * ns
    part = 3 * HEAD_DIM
    place = seq_index.astype(jnp.int32).reshape(1)
    gain_one, bias_one, gain_two, bias_two = (v.reshape(1, width) for v in (gain_one, bias_one, gain_two, bias_two))

    def exchange(pieces):
        return [pieces[0]] + [swap(pieces[k], "seq", ns, k) for k in range(1, ns)]

    toks = [tokens]
    ids = [segment_ids.reshape(1, rows)]
    ids = ids + [swap(ids[0], "seq", ns, k) for k in range(1, ns)]
    bit = ns // 2
    pieces = {0: tokens}
    while bit >= 1:
        for k in list(pieces):
            pieces[k | bit] = swap(pieces[k], "seq", ns, bit)
        bit //= 2
    toks = [pieces[k] for k in range(ns)]

    w_all = jnp.stack([w.T.reshape(heads_all, HEAD_DIM, width) for w in (w_q, w_k, w_v)], 1).reshape(3 * width, width)
    taps = jnp.transpose(
        lax.dynamic_slice_in_dim(conv_weight, seq_index * heads * HEAD_DIM, heads * HEAD_DIM, 2).reshape(
            3, 3, heads, HEAD_DIM
        ),
        (2, 0, 3, 1),
    ).reshape(heads * part, 3)

    raw, conv, normed_in, starts = call(
        functools.partial(project_kernel, ns),
        (1,),
        [whole((rows, width))] * ns
        + [whole((1, rows))] * ns
        + [
            whole((1, width)),
            whole((1, width)),
            pl.BlockSpec((heads * part, width), lambda i, place: (place[0], 0)),
            whole((heads * part, 3)),
        ],
        [whole((heads * part, length)), whole((heads * part, length)), whole((length, width)), whole((1, length))],
        [
            shaped((heads * part, length), BF),
            shaped((heads * part, length), BF),
            shaped((length, width), BF),
            shaped((1, length), jnp.int32),
        ],
        [],
        2 * length * width * heads * part,
        4 * length * width * 2,
        "project",
    )(place, *toks, *ids, gain_one, bias_one, w_all, taps)

    block = 256
    attn_pieces, outs, lses = ([], [], [])
    for h in range(heads):
        results = call(
            functools.partial(attend_kernel, ns, block),
            (1,),
            [whole((1, length)), pl.BlockSpec((part, length), lambda i, place, h=h: (h, 0))],
            [whole((HEAD_DIM, rows))] * ns + [whole((HEAD_DIM, length)), whole((1, length))],
            [shaped((HEAD_DIM, rows), BF)] * ns + [shaped((HEAD_DIM, length), F32), shaped((1, length), F32)],
            [],
            2 * length * length * HEAD_DIM * 4,
            part * length * 4,
            "attend",
        )(place, starts, conv)
        attn_pieces += exchange(results[:ns])
        outs.append(results[ns])
        lses.append(results[ns + 1])

    chunk = 512
    results = call(
        functools.partial(middle_kernel, ns, heads),
        (units // chunk,),
        [whole((HEAD_DIM, rows))] * (ns * heads)
        + [
            whole((rows, width)),
            whole((width, width)),
            whole((rows, width)),
            whole((1, width)),
            whole((1, width)),
            pl.BlockSpec((width, chunk), lambda i, place: (0, i)),
            pl.BlockSpec((chunk, width), lambda i, place: (i, 0)),
        ],
        [
            whole((rows, width)),
            whole((rows, width)),
            whole((rows, width)),
            pl.BlockSpec((rows, chunk), lambda i, place: (0, i)),
            pl.BlockSpec((rows, chunk), lambda i, place: (0, i)),
            whole((rows, width)),
            whole((width, rows)),
            whole((8, width)),
        ]
        + [whole((heads * HEAD_DIM, rows))] * ns,
        [
            shaped((rows, width), BF),
            shaped((rows, width), F32),
            shaped((rows, width), BF),
            shaped((rows, units), BF),
            shaped((rows, units), BF),
            shaped((rows, width), BF),
            shaped((width, rows), BF),
            shaped((8, width), F32),
        ]
        + [shaped((heads * HEAD_DIM, rows), BF)] * ns,
        [pltpu.VMEM((rows, width), F32)] * 3,
        8 * rows * width * units + 4 * rows * width * width,
        4 * width * units,
        "middle",
    )(place, *attn_pieces, tokens, w_o, cotangent, gain_two, bias_two, w_up, w_down)
    mixed, grad_middle, grad_low, hidden, grad_pre, normed_mid, attn, sums_two = results[:8]
    grad_pieces = exchange(results[8:])

    chunk = 768
    rest = width + 128
    grad_down, grad_rest, grad_up = call(
        lambda place, *refs: weight_kernel(*refs),
        (units // chunk,),
        [
            whole((rows, width)),
            pl.BlockSpec((rows, chunk), lambda i, place: (0, i)),
            pl.BlockSpec((rows, chunk), lambda i, place: (0, i)),
            whole((rows, width)),
            whole((rows, width)),
            whole((width, rows)),
            whole((8, width)),
        ],
        [
            pl.BlockSpec((width, chunk), lambda i, place: (0, i)),
            whole((width, rest)),
            pl.BlockSpec((chunk, width), lambda i, place: (i, 0)),
        ],
        [shaped((width, units), BF), shaped((width, rest), BF), shaped((units, width), BF)],
        [pltpu.VMEM((width, rows), BF)],
        4 * rows * width * units + 2 * rows * width * width,
        8 * width * units,
        "weight_grads",
    )(place, cotangent, hidden, grad_pre, normed_mid, grad_low, attn, sums_two)

    y_size = 2 if nb % 2 == 0 else 1
    z_size = nb // y_size
    cores = 2 if ns % 2 == 0 else 1
    x_size = ns // cores
    half_down = reduce_over(grad_down, 0, "seq", 1, cores)
    half_up = reduce_over(grad_up, 0, "seq", 1, cores)
    half_rest = reduce_over(grad_rest, 0, "seq", 1, cores)
    steps_first = lambda v: reduce_over(
        reduce_over(reduce_over(v, 0, "batch", 1, y_size), 0, "batch", y_size, z_size), 0, "seq", cores, x_size
    )
    steps_second = lambda v: reduce_over(
        reduce_over(reduce_over(v, 0, "batch", y_size, z_size), 0, "batch", 1, y_size), 0, "seq", cores, x_size
    )
    owner_first, owner_second = ([], [])
    for device in range(nb * ns):
        b, s = (device // ns, device % ns)
        c, x, y = (digits(s, 1, cores), digits(s, cores, x_size), digits(b, 1, y_size))
        z = digits(b, y_size, z_size)
        owner_first.append((device, ((c * y_size + y) * z_size + z) * x_size + x))
        owner_second.append((device, ((c * z_size + z) * y_size + y) * x_size + x))
    everywhere = ("batch", "seq")
    got_down = lax.ppermute(steps_first(half_down), everywhere, owner_first).astype(F32)
    got_rest = lax.ppermute(steps_first(half_rest), everywhere, owner_first).astype(F32)
    got_up = lax.ppermute(steps_second(half_up), everywhere, owner_second).astype(F32)

    back_pieces, weight_parts = ([], [])
    for h in range(heads):
        results = call(
            functools.partial(attend_back_kernel, ns, block),
            (1,),
            [
                whole((1, length)),
                pl.BlockSpec((part, length), lambda i, place, h=h: (h, 0)),
                pl.BlockSpec((part, length), lambda i, place, h=h: (h, 0)),
                pl.BlockSpec((part, 3), lambda i, place, h=h: (h, 0)),
                whole((length, width)),
                whole((HEAD_DIM, length)),
                whole((1, length)),
            ]
            + [pl.BlockSpec((HEAD_DIM, rows), lambda i, place, h=h: (h, 0))] * ns,
            [whole((part, rows))] * ns + [whole((part, rest))],
            [shaped((part, rows), BF)] * ns + [shaped((part, rest), BF)],
            [pltpu.VMEM((HEAD_DIM, length), BF), pltpu.VMEM((part, length), F32), pltpu.VMEM((part, length), BF)],
            2 * length * length * HEAD_DIM * 10,
            length * width * 2,
            "attend_back",
        )(place, starts, conv, raw, taps, normed_in, outs[h], lses[h], *grad_pieces)
        back_pieces += exchange(results[:ns])
        weight_parts.append(results[ns])

    d_tokens, sums_one = call(
        functools.partial(final_kernel, ns, heads),
        (1,),
        [whole((part, rows))] * (ns * heads)
        + [whole((3 * width, width)), whole((rows, width)), whole((1, width)), whole((rows, width))],
        [whole((rows, width)), whole((8, width))],
        [shaped((rows, width), BF), shaped((8, width), F32)],
        [pltpu.VMEM((3 * width, rows), BF)],
        6 * rows * width * width,
        8 * width * width,
        "final",
    )(place, *back_pieces, w_all, tokens, gain_one, grad_middle)

    grad_qkv = jnp.stack([w.reshape(3, HEAD_DIM, rest) for w in weight_parts], 1).reshape(3, heads * HEAD_DIM, rest)
    grad_qkv = reduce_over(reduce_over(grad_qkv, 1, "batch", 1, y_size), 1, "batch", y_size, z_size)
    owner = []
    for device in range(nb * ns):
        b, s = (device // ns, device % ns)
        owner.append((device, s * nb + digits(b, 1, y_size) * z_size + digits(b, y_size, z_size)))
    grad_qkv = lax.ppermute(grad_qkv, everywhere, owner).astype(F32)
    sums_one = lax.psum_scatter(sums_one[:2], everywhere, scatter_dimension=1, tiled=True)
    flat = jnp.swapaxes(grad_qkv[:, :, :width], 1, 2)
    return (
        mixed,
        d_tokens,
        flat[0],
        flat[1],
        flat[2],
        jnp.swapaxes(grad_qkv[:, :, width : width + 3], 1, 2),
        got_rest[:, :width].T,
        sums_one[0],
        sums_one[1],
        got_rest[:, width],
        got_rest[:, width + 1],
        got_up.T,
        got_down.T,
    )


def solution(mesh):
    split = ("batch", "seq")
    in_specs = (P(split, None), P(split), P(split, None)) + (P(),) * 11
    out_specs = (
        P(split, None),
        P(split, None),
        P(None, split),
        P(None, split),
        P(None, split),
        P(None, None, split),
        P(None, split),
        P(split),
        P(split),
        P(split),
        P(split),
        P(None, split),
        P(None, split),
    )
    return jax.shard_map(local, mesh=mesh, in_specs=in_specs, out_specs=out_specs, check_vma=False)
```

```python
import functools
import math

import jax
import jax.numpy as jnp
from jax import lax
from jax.experimental import pallas as pl
from jax.experimental.pallas import tpu as pltpu
from jax.sharding import PartitionSpec as P

HEAD_DIM = 64
EPS = 1e-05
NEG_FILL = -1e30
LONG = 512
ID_ROWS = 16
LOG2E = math.log2(math.e)
BF = jnp.bfloat16
F32 = jnp.float32
VMEM_LIMIT = 60 * 1024 * 1024


def nn(first, second):
    return lax.dot_general(first, second, (((1,), (0,)), ((), ())), preferred_element_type=F32)


def nt(first, second):
    return lax.dot_general(first, second, (((1,), (1,)), ((), ())), preferred_element_type=F32)


def tn(first, second):
    return lax.dot_general(first, second, (((0,), (0,)), ((), ())), preferred_element_type=F32)


def norm_stats(values):
    centred = values - jnp.mean(values, axis=-1, keepdims=True)
    variance = jnp.mean(centred * centred, axis=-1, keepdims=True)
    inv_scale = lax.rsqrt(variance + EPS)
    return (centred * inv_scale, inv_scale)


def norm_back(grad_out, normed, inv_scale, gain):
    grad_norm = grad_out * gain
    projected = (
        grad_norm
        - jnp.mean(grad_norm, -1, keepdims=True)
        - normed * jnp.mean(grad_norm * normed, -1, keepdims=True)
    )
    return (projected * inv_scale, jnp.sum(grad_out * normed, 0, keepdims=True), jnp.sum(grad_out, 0, keepdims=True))


def lag_mask(starts, positions, lag):
    return positions - lag >= starts


def project_rows(tok, gain, bias, flipped):
    normed, _ = norm_stats(tok.astype(F32))
    low = (normed * gain + bias).astype(BF)
    return (low, nn(flipped, jnp.transpose(low)).astype(BF))


def near_kernel(heads, place, own, other, gain, bias, w_q, w_k, w_v, flipped, low_own, low_other, raw_own, raw_other):
    rows = low_own.shape[0]
    for h in range(heads):
        for part, weights in enumerate((w_q, w_k, w_v)):
            row = (h * 3 + part) * HEAD_DIM
            flipped[row : row + HEAD_DIM, :] = jnp.transpose(weights[:, h * HEAD_DIM : (h + 1) * HEAD_DIM])
    low_own[...], raw_own[...] = project_rows(own[:rows, :], gain[...], bias[...], flipped[...])
    low_other[...], raw_other[...] = project_rows(other[:rows, :], gain[...], bias[...], flipped[...])


def far_kernel(ns, place, *refs):
    near, toks = (refs[:4], refs[4 : 4 + ns])
    gain, bias, flipped, taps, raw, conv, normed_out, starts_out = refs[4 + ns :]
    rows = near[0].shape[0]

    def offset(k):
        return pl.multiple_of((place[0] ^ k) * rows, rows)

    for k in range(ns):
        codes = toks[k][rows : rows + ID_ROWS, :rows].astype(F32)
        starts_out[:, pl.ds(offset(k), rows)] = (codes[0:1, :] * 256.0 + codes[1:2, :]).astype(jnp.int32)
        if k < 2:
            normed_out[pl.ds(offset(k), rows), :] = near[k][...]
            raw[:, pl.ds(offset(k), rows)] = near[2 + k][...]
        else:
            low, projected = project_rows(toks[k][:rows, :], gain[...], bias[...], flipped[...])
            normed_out[pl.ds(offset(k), rows), :] = low
            raw[:, pl.ds(offset(k), rows)] = projected
    starts = starts_out[...]
    positions = lax.broadcasted_iota(jnp.int32, starts.shape, 1)
    step = HEAD_DIM
    for r in range(0, raw.shape[0], step):
        values = raw[r : r + step, :].astype(F32)
        result = taps[r : r + step, 0:1] * values
        for lag in (1, 2):
            moved = jnp.where(lag_mask(starts, positions, lag), pltpu.roll(values, lag, 1), 0.0)
            result = result + taps[r : r + step, lag : lag + 1] * moved
        conv[r : r + step, :] = result.astype(BF)


def masked_scores(scores, starts, key_begin, query_begin, length):
    keys, queries = scores.shape
    diagonal = key_begin + keys > query_begin
    inside = key_begin >= LONG and query_begin + queries <= length - LONG
    if inside and not diagonal:
        return scores
    key_pos = key_begin + lax.broadcasted_iota(jnp.int32, scores.shape, 0)
    allowed = None
    if not inside:
        allowed = key_pos >= starts
    if diagonal:
        query_pos = query_begin + lax.broadcasted_iota(jnp.int32, scores.shape, 1)
        causal = key_pos <= query_pos
        allowed = causal if allowed is None else allowed & causal
    return jnp.where(allowed, scores, NEG_FILL)


def attend_kernel(ns, block, place, starts_ref, qkv, *outs):
    pieces, out_full, lse_out = (outs[:ns], outs[ns], outs[ns + 1])
    length = qkv.shape[1]
    rows = length // ns
    keys = jnp.transpose(qkv[HEAD_DIM : 2 * HEAD_DIM, :])
    factor = LOG2E * HEAD_DIM ** (-0.5)
    for q in range(0, length, block):
        queries = qkv[0:HEAD_DIM, q : q + block]
        starts = starts_ref[:, q : q + block]
        scores = [
            masked_scores(nn(keys[u : u + block], queries), starts, u, q, length) * factor
            for u in range(0, q + block, block)
        ]
        top = scores[0]
        for one in scores[1:]:
            top = jnp.maximum(top, one)
        top = jnp.max(top, 0, keepdims=True)
        total = jnp.zeros((8, block), F32)
        result = jnp.zeros((HEAD_DIM, block), F32)
        for index, one in enumerate(scores):
            prob = jnp.exp2(one - top)
            total = total + jnp.sum(prob.reshape(block // 8, 8, block), 0)
            values = qkv[2 * HEAD_DIM :, index * block : (index + 1) * block]
            result = result + nn(values, prob.astype(BF))
        total = jnp.sum(total, 0, keepdims=True)
        lse_out[0, :, q : q + block] = top + jnp.log2(total)
        out_full[:, q : q + block] = result / total
    for k in range(ns):
        begin = pl.multiple_of((place[0] ^ k) * rows, rows)
        pieces[k][...] = out_full[:, pl.ds(begin, rows)].astype(BF)


def attend_back_kernel(ns, block, place, starts_ref, conv, raw, taps, flipped, gain, bias, normed, out_full, lse, *refs):
    grads_in, grads_out, grad_w, norm_sums = (refs[:ns], refs[ns : 2 * ns], refs[2 * ns], refs[2 * ns + 1])
    grad_attn, grad_conv, grad_raw = refs[2 * ns + 2 :]
    length = conv.shape[1]
    rows = length // ns
    head_scale = HEAD_DIM ** (-0.5)
    factor = LOG2E * head_scale
    for k in range(ns):
        begin = pl.multiple_of((place[0] ^ k) * rows, rows)
        grad_attn[:, pl.ds(begin, rows)] = grads_in[k][...]
    delta = jnp.sum(grad_attn[...].astype(F32) * out_full[...], 0, keepdims=True)
    keys = jnp.transpose(conv[HEAD_DIM : 2 * HEAD_DIM, :])
    values = jnp.transpose(conv[2 * HEAD_DIM :, :])
    grad_conv[HEAD_DIM:, :] = jnp.zeros((2 * HEAD_DIM, length), F32)
    for q in range(0, length, block):
        queries = conv[0:HEAD_DIM, q : q + block]
        grad_block = grad_attn[:, q : q + block]
        starts = starts_ref[:, q : q + block]
        grad_query = jnp.zeros((HEAD_DIM, block), F32)
        for u in range(0, q + block, block):
            scores = masked_scores(nn(keys[u : u + block], queries), starts, u, q, length)
            prob = jnp.exp2(scores * factor - lse[0, :, q : q + block])
            grad_prob = nn(values[u : u + block], grad_block)
            grad_scores = (prob * (grad_prob - delta[:, q : q + block])).astype(BF)
            grad_query = grad_query + nn(conv[HEAD_DIM : 2 * HEAD_DIM, u : u + block], grad_scores)
            grad_conv[HEAD_DIM : 2 * HEAD_DIM, u : u + block] += nt(queries, grad_scores)
            grad_conv[2 * HEAD_DIM :, u : u + block] += nt(grad_block, prob.astype(BF))
        grad_conv[0:HEAD_DIM, q : q + block] = grad_query
    starts = starts_ref[...]
    positions = lax.broadcasted_iota(jnp.int32, starts.shape, 1)
    tap_columns = []
    for part in range(3):
        at = slice(part * HEAD_DIM, (part + 1) * HEAD_DIM)
        grad = grad_conv[at, :] * (head_scale if part < 2 else 1.0)
        inputs = raw[at, :].astype(F32)
        result = taps[at, 0:1] * grad
        sums = [jnp.sum(grad * inputs, 1, keepdims=True)]
        for lag in (1, 2):
            kept = jnp.where(lag_mask(starts, positions, lag), grad, 0.0)
            result = result + taps[at, lag : lag + 1] * pltpu.roll(kept, length - lag, 1)
            sums.append(jnp.sum(kept * pltpu.roll(inputs, lag, 1), 1, keepdims=True))
        grad_raw[at, :] = result.astype(BF)
        lane = lax.broadcasted_iota(jnp.int32, (HEAD_DIM, 128), 1)
        tap_columns.append(
            jnp.where(lane == 0, sums[0], jnp.where(lane == 1, sums[1], jnp.where(lane == 2, sums[2], 0.0)))
        )
    width = normed.shape[1]
    grads = nn(grad_raw[...], normed[...])
    grad_w[:, :width] = grads.astype(BF)
    weights = flipped[...].astype(F32)
    column = jnp.sum(grad_raw[...].astype(F32), 1, keepdims=True)
    norm_sums[0, 0:1, :] = jnp.sum(weights * (grads - bias[...] * column), 0, keepdims=True) / gain[...]
    norm_sums[0, 1:2, :] = jnp.sum(weights * column, 0, keepdims=True)
    for part in range(3):
        grad_w[part * HEAD_DIM : (part + 1) * HEAD_DIM, width:] = tap_columns[part].astype(BF)
    for k in range(ns):
        begin = pl.multiple_of((place[0] ^ k) * rows, rows)
        grads_out[k][...] = grad_raw[:, pl.ds(begin, rows)]


def middle_kernel(ns, heads, groups, place, *refs):
    count = ns * len(groups)
    pieces = refs[:count]
    tokens, w_o, cotangent, gain, bias, w_up, w_down = refs[count : count + 7]
    outs = refs[count + 7 : count + 15 + ns]
    mixed, grad_middle, grad_low, sent, kept, normed_low, attn_out, sums = outs[:8]
    grad_attn = outs[8:]
    middle, normed_two, grad_normed, scale = refs[count + 15 + ns :]
    step = pl.program_id(0)
    steps = pl.num_programs(0)
    head_rows = heads * HEAD_DIM

    @pl.when(step == 0)
    def _():
        for k in range(ns):
            for g, (first, size) in enumerate(groups):
                begin = pl.multiple_of((place[0] ^ k) * head_rows + first * HEAD_DIM, HEAD_DIM)
                attn_out[pl.ds(begin, size * HEAD_DIM), :] = pieces[g * ns + k][...]
        value = tokens[...].astype(F32) + tn(attn_out[...], w_o[...])
        normed, inv_scale = norm_stats(value)
        middle[...] = value
        normed_two[...] = normed
        scale[...] = jnp.broadcast_to(inv_scale, scale.shape)
        normed_low[...] = (normed * gain[...] + bias[...]).astype(BF)
        grad_normed[...] = jnp.zeros_like(grad_normed)

    positive = jnp.maximum(nn(normed_low[...], w_up[...]), 0.0)
    hidden = (positive * positive).astype(BF)
    grad_pre = (nt(cotangent[...], w_down[...]) * (2.0 * positive)).astype(BF)

    @pl.when(step < steps // 2)
    def _():
        sent[0] = hidden
        sent[1] = grad_pre

    @pl.when(step >= steps // 2)
    def _():
        kept[0] = hidden
        kept[1] = grad_pre

    middle[...] += nn(hidden, w_down[...])
    grad_normed[...] += nt(grad_pre, w_up[...])

    @pl.when(step == steps - 1)
    def _():
        mixed[...] = middle[...].astype(BF)
        back, grad_gain, grad_bias = norm_back(grad_normed[...], normed_two[...], scale[:, 0:1], gain[...])
        total = cotangent[...].astype(F32) + back
        grad_middle[...] = total
        low = total.astype(BF)
        grad_low[...] = low
        row = lax.broadcasted_iota(jnp.int32, sums.shape, 0)
        sums[...] = jnp.where(row == 0, grad_gain, jnp.where(row == 1, grad_bias, 0.0))
        for k in range(ns):
            begin = pl.multiple_of((place[0] ^ k) * head_rows, head_rows)
            grad_attn[k][...] = nt(w_o[pl.ds(begin, head_rows), :], low).astype(BF)


def own_kernel(place, cotangent, hidden, pre_low, pre_high, normed, grad_low, attn_sent, attn_kept, sums, *refs):
    grad_down, grad_up, rest_sent, rest_kept, flipped = refs

    @pl.when(pl.program_id(0) == 0)
    def _():
        flipped[...] = jnp.transpose(cotangent[...])
        columns = jnp.transpose(grad_low[...])
        width = columns.shape[0]
        filled = jnp.transpose(jnp.concatenate([sums[...], jnp.zeros((128 - sums.shape[0], width), F32)], 0)).astype(BF)
        for attn, rest in ((attn_sent, rest_sent), (attn_kept, rest_kept)):
            half = attn.shape[0]
            rest[:, :half] = nt(columns, attn[...]).astype(BF)
            rest[:, half:] = filled

    grad_down[...] = nn(flipped[...], hidden[0]).astype(BF)
    half = normed.shape[1]
    grad_up[:, :half] = nn(jnp.transpose(pre_low[0]), normed[...]).astype(BF)
    grad_up[:, half:] = nn(jnp.transpose(pre_high[0]), normed[...]).astype(BF)


def other_kernel(place, cotangent, hidden, pre_low, pre_high, normed, own_down, own_up, rest_one, rest_two, *refs):
    grad_down, grad_up, rest, flipped = refs

    @pl.when(pl.program_id(0) == 0)
    def _():
        flipped[...] = jnp.transpose(cotangent[...])
        rest[...] = (rest_one[...].astype(F32) + rest_two[...].astype(F32)).astype(BF)

    grad_down[...] = (own_down[...].astype(F32) + nn(flipped[...], hidden[0])).astype(BF)
    half = normed.shape[1]
    low = nn(jnp.transpose(pre_low[0]), normed[...])
    grad_up[:, :half] = (own_up[:, :half].astype(F32) + low).astype(BF)
    high = nn(jnp.transpose(pre_high[0]), normed[...])
    grad_up[:, half:] = (own_up[:, half:].astype(F32) + high).astype(BF)


def pass_kernel(place, values, result):
    pass


def final_kernel(ns, heads, groups, place, *refs):
    count = ns * len(groups)
    pieces = refs[:count]
    weights, (tokens, gain, grad_middle, d_tokens, stacked) = (refs[count : count + 3], refs[count + 3 :])
    for k in range(ns):
        for g, (first, size) in enumerate(groups):
            for h in range(size):
                begin = pl.multiple_of(((place[0] ^ k) * heads + first + h) * HEAD_DIM, HEAD_DIM)
                for part in range(3):
                    row = (h * 3 + part) * HEAD_DIM
                    stacked[part, pl.ds(begin, HEAD_DIM), :] = pieces[g * ns + k][row : row + HEAD_DIM, :]
    grad_normed = nt(jnp.transpose(stacked[0]), weights[0][...])
    for part in (1, 2):
        grad_normed = grad_normed + nt(jnp.transpose(stacked[part]), weights[part][...])
    normed, inv_scale = norm_stats(tokens[...].astype(F32))
    back, _, _ = norm_back(grad_normed, normed, inv_scale, gain[...])
    d_tokens[...] = (grad_middle[...] + back).astype(BF)


def whole(shape):
    return pl.BlockSpec(shape, lambda *_: (0,) * len(shape))


def shaped(shape, dtype):
    return jax.ShapeDtypeStruct(shape, dtype)


def call(kernel, grid, inputs, outputs, scratch, flops, moved, name, place, ties=()):
    count = len(inputs)

    def body(place, *refs):
        kernel(place, *refs[:count], *refs[count + len(ties) :])

    return pl.pallas_call(
        body,
        grid_spec=pltpu.PrefetchScalarGridSpec(
            num_scalar_prefetch=1,
            grid=grid,
            in_specs=[spec for _, spec in inputs] + [pl.BlockSpec(memory_space=pl.ANY)] * len(ties),
            out_specs=[spec for _, _, spec in outputs],
            scratch_shapes=scratch,
        ),
        out_shape=[jax.ShapeDtypeStruct(shape, dtype) for shape, dtype, _ in outputs],
        compiler_params=pltpu.CompilerParams(vmem_limit_bytes=VMEM_LIMIT),
        cost_estimate=pl.CostEstimate(flops=flops, bytes_accessed=moved, transcendentals=0),
        name=name,
    )(place, *[array for array, _ in inputs], *ties)


def full(array):
    return (array, whole(array.shape))


def out(shape, dtype):
    return (shape, dtype, whole(shape))


def swap(values, axis, count, mask):
    return lax.ppermute(values, axis, [(i, i ^ mask) for i in range(count)])


def add_all(terms):
    total = terms[0].astype(F32)
    for one in terms[1:]:
        total = total + one.astype(F32)
    return total


def after(values, tie, place):
    anywhere = pl.BlockSpec(memory_space=pl.ANY)
    return pl.pallas_call(
        lambda place, values, tie, result: None,
        in_specs=[pl.BlockSpec(memory_space=pltpu.SMEM), anywhere, anywhere],
        out_specs=anywhere,
        out_shape=jax.ShapeDtypeStruct(values.shape, values.dtype),
        input_output_aliases={1: 0},
        name="after",
    )(place, values, tie)


class Chain:
    def __init__(self, terms, dims):
        self.terms, self.dims = (terms, dims)

    def step(self, name):
        sent = []
        for dim, axis, low in self.dims[name]:
            size = self.terms[0].shape[dim]
            count = lax.axis_size(axis)
            mine = (lax.axis_index(axis) // low) % size
            cut = lambda m: [lax.dynamic_slice_in_dim(t, mine ^ m, 1, dim) for t in self.terms]
            moved = [add_all(cut(m)).astype(BF) for m in range(1, size)]
            sent += moved
            self.terms = cut(0) + [swap(v, axis, count, (i + 1) * low) for i, v in enumerate(moved)]
        return sent

    def value(self):
        return add_all(self.terms)


def join(chains, dim):
    values = jnp.concatenate([c.value().astype(BF) for c in chains], dim)
    return Chain([values], chains[0].dims)


def regroup(pieces, targets, slots):
    count = len(pieces)
    devices = len(targets[0])
    edges = [(d, targets[i][d], i, slots[i][d]) for d in range(devices) for i in range(count)]
    colors = color_edges(edges, count)
    tables = [[0] * devices for _ in range(2 * count)]
    perms = [[] for _ in range(count)]
    for e, (source, target, piece, slot) in enumerate(edges):
        perms[colors[e]].append((source, target))
        tables[colors[e]][source] = piece
        tables[count + slot][target] = colors[e]
    device = lax.axis_index("batch") * lax.axis_size("seq") + lax.axis_index("seq")
    column = lax.dynamic_slice_in_dim(jnp.asarray(tables, jnp.int32), device, 1, 1)

    def choose(arrays, row):
        result = arrays[0]
        for i in range(1, count):
            result = jnp.where(column[row, 0] == i, arrays[i], result)
        return result

    got = [lax.ppermute(choose(pieces, c), ("batch", "seq"), perms[c]) for c in range(count)]
    return [choose(got, count + j) for j in range(count)]


def color_edges(edges, degree):
    colors = {}
    left = list(range(len(edges)))
    for color in range(degree):
        match = {}
        by_source = {}
        for e in left:
            by_source.setdefault(edges[e][0], []).append(e)

        def place(source, seen):
            for e in by_source[source]:
                target = edges[e][1]
                if target in seen:
                    continue
                seen.add(target)
                if target not in match or place(edges[match[target]][0], seen):
                    match[target] = e
                    return True
            return False

        for source in by_source:
            place(source, set())
        for e in match.values():
            colors[e] = color
        left = [e for e in left if e not in colors]
    return colors


def local(tokens, segment_ids, cotangent, w_q, w_k, w_v, conv_weight, w_o, gain_one, bias_one, gain_two, bias_two, w_up, w_down):
    ns, nb = (lax.axis_size("seq"), lax.axis_size("batch"))
    s_index, b_index = (lax.axis_index("seq"), lax.axis_index("batch"))
    cores, y_size = (2, 2)
    x_size, z_size = (ns // cores, nb // y_size)
    rows, width = tokens.shape
    units = w_up.shape[1]
    heads = width // HEAD_DIM // ns
    length = rows * ns
    part = 3 * HEAD_DIM
    mine = heads * HEAD_DIM
    core = s_index % cores
    place = jnp.stack([s_index, core]).astype(jnp.int32)
    gain_one, bias_one, gain_two, bias_two = (v.reshape(1, width) for v in (gain_one, bias_one, gain_two, bias_two))
    groups = [(0, heads - 1), (heads - 1, 1)]

    def exchange(pieces):
        return [pieces[0]] + [swap(pieces[k], "seq", ns, k) for k in range(1, ns)]

    def to_core(values):
        return swap(values, "seq", ns, 1)

    codes = jnp.stack([segment_ids // 256, segment_ids % 256]).astype(BF)
    codes = jnp.pad(codes, ((0, ID_ROWS - 2), (0, width - rows)))
    coded = jnp.concatenate([tokens, codes], 0)
    toks = [coded] + [None] * (ns - 1)
    for k in range(2, ns, 2):
        toks[k] = swap(coded, "seq", ns, k)
    toks[1] = to_core(coded)
    cotangent_other = to_core(cotangent)

    own = [lax.dynamic_slice_in_dim(w, s_index * mine, mine, 1) for w in (w_q, w_k, w_v)]
    taps = jnp.transpose(
        lax.dynamic_slice_in_dim(conv_weight, s_index * mine, mine, 2).reshape(3, 3, heads, HEAD_DIM), (2, 0, 3, 1)
    ).reshape(heads * part, 3)

    near = call(
        functools.partial(near_kernel, heads),
        (1,),
        [full(v) for v in (coded, toks[1], gain_one, bias_one, *own)],
        [
            out((heads * part, width), BF),
            out((rows, width), BF),
            out((rows, width), BF),
            out((heads * part, rows), BF),
            out((heads * part, rows), BF),
        ],
        [],
        4 * rows * width * heads * part,
        8 * rows * width,
        "near",
        place,
    )
    flipped = near[0]
    for k in range(2, ns, 2):
        toks[k] = after(toks[k], near[4], place)
        toks[k + 1] = to_core(toks[k])
    raw, conv, normed_in, starts = call(
        functools.partial(far_kernel, ns),
        (1,),
        [full(v) for v in (*near[1:], *toks, gain_one, bias_one, flipped, taps)],
        [
            out((heads * part, length), BF),
            out((heads * part, length), BF),
            out((length, width), BF),
            out((1, length), jnp.int32),
        ],
        [],
        4 * rows * width * heads * part,
        8 * length * width,
        "far",
        place,
    )

    block = 256

    def by_head(array, first, columns):
        return (array, pl.BlockSpec((array.shape[0] // heads, columns), lambda i, place: (first + i, 0)))

    def per_head(size, height, columns, dtype):
        return ((size * height, columns), dtype, pl.BlockSpec((height, columns), lambda i, place: (i, 0)))

    attn_pieces, attended = ([], [])
    for first, size in groups:
        results = call(
            functools.partial(attend_kernel, ns, block),
            (size,),
            [full(starts), by_head(conv, first, length)],
            [per_head(size, HEAD_DIM, rows, BF)] * ns
            + [
                per_head(size, HEAD_DIM, length, F32),
                ((size, 1, length), F32, pl.BlockSpec((1, 1, length), lambda i, place: (i, 0, 0))),
            ],
            [],
            2 * length * length * HEAD_DIM * 4 * size,
            part * length * 4,
            "attend",
            place,
        )
        attn_pieces += exchange(results[:ns])
        attended.append(results[ns:])

    chunk = 512
    half = units // 2
    steps = half // chunk

    def unit_block(i, place):
        return jnp.where(i < steps, 1 - place[1], place[1]) * steps + lax.rem(i, steps)

    pair = (2, rows, half)
    results = call(
        functools.partial(middle_kernel, ns, heads, groups),
        (2 * steps,),
        [full(v) for v in (*attn_pieces, tokens, w_o, cotangent, gain_two, bias_two)]
        + [
            (w_up, pl.BlockSpec((width, chunk), lambda i, place: (0, unit_block(i, place)))),
            (w_down, pl.BlockSpec((chunk, width), lambda i, place: (unit_block(i, place), 0))),
        ],
        [
            out((rows, width), BF),
            out((rows, width), F32),
            out((rows, width), BF),
            (pair, BF, pl.BlockSpec((2, rows, chunk), lambda i, place: (0, 0, jnp.minimum(i, steps - 1)))),
            (pair, BF, pl.BlockSpec((2, rows, chunk), lambda i, place: (0, 0, jnp.maximum(i - steps, 0)))),
            out((rows, width), BF),
            out((width, rows), BF),
            out((8, width), F32),
        ]
        + [out((mine, rows), BF)] * ns,
        [pltpu.VMEM((rows, width), F32)] * 3 + [pltpu.VMEM((rows, 128), F32)],
        8 * rows * width * units + 4 * rows * width * width,
        4 * width * units,
        "middle",
        place,
    )
    mixed, grad_middle, grad_low, sent, kept, normed_mid, attn, sums_two = results[:8]
    grad_pieces = exchange(results[8:])
    normed_other = to_core(normed_mid)
    got = to_core(sent)

    flip = [pltpu.VMEM((width, rows), BF)]
    quarter = chunk // 2

    def unit_inputs(array):
        return [
            (array, pl.BlockSpec((1, rows, chunk), lambda i, place: (0, 0, i))),
            (array, pl.BlockSpec((1, rows, quarter), lambda i, place: (1, 0, i))),
            (array, pl.BlockSpec((1, rows, quarter), lambda i, place: (1, 0, steps + i))),
        ]

    unit_grads = [
        (width, half),
        BF,
        pl.BlockSpec((width, chunk), lambda i, place: (0, i)),
    ], [
        (half // 2, 2 * width),
        BF,
        pl.BlockSpec((quarter, 2 * width), lambda i, place: (i, 0)),
    ]
    rest = width // 2 + 128
    own_down, own_up, rest_sent, rest_kept = call(
        own_kernel,
        (steps,),
        [full(cotangent)]
        + unit_inputs(kept)
        + [full(normed_mid), full(grad_low)]
        + [
            (attn, pl.BlockSpec((width // 2, rows), lambda i, place: (1 - place[1], 0))),
            (attn, pl.BlockSpec((width // 2, rows), lambda i, place: (place[1], 0))),
            full(sums_two),
        ],
        [*unit_grads, out((width, rest), BF), out((width, rest), BF)],
        flip,
        2 * rows * width * units + 2 * rows * width * width,
        3 * width * units,
        "own_rows",
        place,
    )
    grad_down, grad_up, grad_rest = call(
        other_kernel,
        (steps,),
        [full(cotangent_other)]
        + unit_inputs(got)
        + [
            full(normed_other),
            (own_down, unit_grads[0][2]),
            (own_up, unit_grads[1][2]),
            full(rest_kept),
            full(to_core(rest_sent)),
        ],
        [*unit_grads, out((width, rest), BF)],
        flip,
        2 * rows * width * units,
        5 * width * units,
        "other_rows",
        place,
    )

    z_dims, left = ([], z_size)
    while left > 4:
        z_dims, left = (z_dims + [4], left // 4)
    z_dims = [left] + z_dims
    z_steps = []
    low = y_size * z_size
    for i, size in enumerate(z_dims):
        low //= size
        z_steps.append((i, "batch", low))
    chips = nb * x_size
    lead = (*z_dims, y_size, x_size)
    steps_of = {"z": z_steps, "y": [(len(z_dims), "batch", 1)], "x": [(len(z_dims) + 1, "seq", cores)]}
    split = lambda v: Chain([v.reshape(*lead, v.shape[0] // chips, v.shape[1])], steps_of)
    ups, downs, rests = (split(grad_up), split(grad_down), split(grad_rest))

    lanes = width + 128
    head_rows = HEAD_DIM // nb
    head_lead = (3, *z_dims, y_size, head_rows, lanes)
    head_steps = {
        "z": [(d + 2, axis, low) for d, axis, low in z_steps],
        "y": [(len(z_dims) + 2, "batch", 1)],
    }
    back_pieces, weight_chains, sums_heads = ([], [], [])

    def back(g, ties):
        first, size = groups[g]
        out_full, lse = attended[g]
        results = call(
            functools.partial(attend_back_kernel, ns, block),
            (size,),
            [
                full(starts),
                by_head(conv, first, length),
                by_head(raw, first, length),
                by_head(taps, first, 3),
                by_head(flipped, first, width),
                full(gain_one),
                full(bias_one),
                full(normed_in),
                (out_full, pl.BlockSpec((HEAD_DIM, length), lambda i, place: (i, 0))),
                (lse, pl.BlockSpec((1, 1, length), lambda i, place: (i, 0, 0))),
            ]
            + [by_head(v, first, rows) for v in grad_pieces],
            [per_head(size, part, rows, BF)] * ns
            + [
                per_head(size, part, lanes, BF),
                ((size, 2, width), F32, pl.BlockSpec((1, 2, width), lambda i, place: (i, 0, 0))),
            ],
            [pltpu.VMEM((HEAD_DIM, length), BF), pltpu.VMEM((part, length), F32), pltpu.VMEM((part, length), BF)],
            2 * length * length * HEAD_DIM * 10 * size,
            length * width * 2,
            "attend_back",
            place,
            ties,
        )
        back_pieces.extend(exchange(results[:ns]))
        weight_chains.append(Chain([results[ns].reshape(size, *head_lead)], head_steps))
        sums_heads.append(results[ns + 1])

    ties = ups.step("x") + downs.step("y") + rests.step("z")
    back(0, ties)
    ties = ups.step("y") + downs.step("x") + rests.step("y") + weight_chains[0].step("y")
    back(1, ties)
    total = jnp.sum(jnp.concatenate(sums_heads, 0), 0)
    total = jnp.transpose(total.reshape(2, nb, ns, 3, head_rows), (3, 1, 4, 0, 2)).reshape(1, 3, HEAD_DIM, 2 * ns)
    total = jnp.pad(total, ((0, 0), (0, 0), (0, 0), (width + 3, lanes - width - 3 - 2 * ns)))
    weight_chains[1].terms.append(total.reshape(1, *head_lead))
    weight_chains[1].step("y")
    both = join([ups, downs], len(lead) + 1)
    ties = both.step("z") + rests.step("x") + weight_chains[0].step("z")
    weight_chains[1].step("z")

    (d_tokens,) = call(
        functools.partial(final_kernel, ns, heads, groups),
        (1,),
        [full(v) for v in (*back_pieces, w_q, w_k, w_v, tokens, gain_one, grad_middle)],
        [out((rows, width), BF)],
        [pltpu.VMEM((3, width, rows), BF)],
        6 * rows * width * width,
        8 * width * width,
        "final",
        place,
        ties,
    )

    devices = [(d // ns, d % ns) for d in range(nb * ns)]

    per_granule = [c.value().reshape(-1, 3, head_rows, lanes) for c in weight_chains]
    granules = [v[i] for v in per_granule for i in range(v.shape[0])]
    last = granules[-1][:, :, width + 3 : width + 3 + 2 * ns].reshape(3, head_rows, 2, ns)
    take = lambda k: lax.dynamic_index_in_dim(last, s_index ^ k, 3, keepdims=False)
    sums_one = add_all([take(0)] + [swap(take(k), "seq", ns, k) for k in range(1, ns)]).reshape(-1, 2)
    number = lambda h, b, s: (s * heads + h) * nb + b
    pieces = regroup(
        [v.astype(BF) for v in granules],
        [[number(h, b, s) // heads for b, s in devices] for h in range(heads)],
        [[number(h, b, s) % heads for b, s in devices] for h in range(heads)],
    )
    grad_qkv = jnp.concatenate(pieces, 1).astype(F32)

    value = both.value().astype(BF)
    value = value.reshape(value.shape[-2:])
    piece = half // 2 // chips
    begin = lambda p, b, s: (s % cores) * half + p * (half // 2) + (b * x_size + s // cores) * piece
    got_up = regroup(
        [value[:, :width], value[:, width : 2 * width]],
        [[begin(p, b, s) // (2 * piece) for b, s in devices] for p in range(2)],
        [[begin(p, b, s) % (2 * piece) // piece for b, s in devices] for p in range(2)],
    )
    got_up = jnp.concatenate(got_up, 0).astype(F32)

    value = jnp.concatenate([value[:, 2 * width :], rests.value().astype(BF).reshape(value.shape[0], rest)], 1)
    size = value.shape[0] // cores
    here = lax.dynamic_slice_in_dim(value, core * size, size, 0)
    there = to_core(lax.dynamic_slice_in_dim(value, (1 - core) * size, size, 0))
    by_core = [jnp.where(core == 0, here, there).astype(F32), jnp.where(core == 0, there, here).astype(F32)]
    got_down = jnp.concatenate([v[:, :half] for v in by_core], 1)
    got_rest = jnp.concatenate([v[:, half : half + width // 2] for v in by_core], 1)
    sums_two = here[:, half + width // 2 : half + width // 2 + 2].astype(F32)

    flat = jnp.swapaxes(grad_qkv[:, :, :width], 1, 2)
    return (
        mixed,
        d_tokens,
        flat[0],
        flat[1],
        flat[2],
        jnp.swapaxes(grad_qkv[:, :, width : width + 3], 1, 2),
        got_rest.T,
        sums_one[:, 0],
        sums_one[:, 1],
        sums_two[:, 0],
        sums_two[:, 1],
        got_up.T,
        got_down.T,
    )


def solution(mesh):
    split = ("batch", "seq")
    in_specs = (P(split, None), P(split), P(split, None)) + (P(),) * 11
    out_specs = (
        P(split, None),
        P(split, None),
        P(None, split),
        P(None, split),
        P(None, split),
        P(None, None, split),
        P(None, split),
        P(split),
        P(split),
        P(split),
        P(split),
        P(None, split),
        P(None, split),
    )
    return jax.shard_map(local, mesh=mesh, in_specs=in_specs, out_specs=out_specs, check_vma=False)
```

```python
import functools
import math

import jax
import jax.numpy as jnp
from jax import lax
from jax.experimental import pallas as pl
from jax.experimental.pallas import tpu as pltpu
from jax.sharding import PartitionSpec as P

HEAD_DIM = 64
EPS = 1e-05
NEG_FILL = -1e30
LONG = 512
ID_ROWS = 16
COST = 1
LOG2E = math.log2(math.e)
BF = jnp.bfloat16
F32 = jnp.float32
VMEM_LIMIT = 60 * 1024 * 1024


def nn(first, second):
    return lax.dot_general(first, second, (((1,), (0,)), ((), ())), preferred_element_type=F32)


def nt(first, second):
    return lax.dot_general(first, second, (((1,), (1,)), ((), ())), preferred_element_type=F32)


def tn(first, second):
    return lax.dot_general(first, second, (((0,), (0,)), ((), ())), preferred_element_type=F32)


def norm_stats(values):
    centred = values - jnp.mean(values, axis=-1, keepdims=True)
    variance = jnp.mean(centred * centred, axis=-1, keepdims=True)
    inv_scale = lax.rsqrt(variance + EPS)
    return (centred * inv_scale, inv_scale)


def norm_back(grad_out, normed, inv_scale, gain):
    grad_norm = grad_out * gain
    projected = (
        grad_norm
        - jnp.mean(grad_norm, -1, keepdims=True)
        - normed * jnp.mean(grad_norm * normed, -1, keepdims=True)
    )
    return (projected * inv_scale, jnp.sum(grad_out * normed, 0, keepdims=True), jnp.sum(grad_out, 0, keepdims=True))


def lag_mask(starts, positions, lag):
    return positions - lag >= starts


def project_rows(tok, gain, bias, flipped):
    normed, _ = norm_stats(tok.astype(F32))
    low = (normed * gain + bias).astype(BF)
    return (low, nn(flipped, jnp.transpose(low)).astype(BF))


def near_kernel(heads, place, own, other, gain, bias, w_q, w_k, w_v, flipped, low_own, low_other, raw_own, raw_other):
    rows = low_own.shape[0]
    for h in range(heads):
        for part, weights in enumerate((w_q, w_k, w_v)):
            row = (h * 3 + part) * HEAD_DIM
            flipped[row : row + HEAD_DIM, :] = jnp.transpose(weights[:, h * HEAD_DIM : (h + 1) * HEAD_DIM])
    low_own[...], raw_own[...] = project_rows(own[:rows, :], gain[...], bias[...], flipped[...])
    low_other[...], raw_other[...] = project_rows(other[:rows, :], gain[...], bias[...], flipped[...])


def far_kernel(ns, place, *refs):
    near, toks = (refs[:4], refs[4 : 4 + ns])
    gain, bias, flipped, taps, raw, conv, normed_out, starts_out = refs[4 + ns :]
    rows = near[0].shape[0]

    def offset(k):
        return pl.multiple_of((place[0] ^ k) * rows, rows)

    for k in range(ns):
        codes = toks[k][rows : rows + ID_ROWS, :rows].astype(F32)
        starts_out[:, pl.ds(offset(k), rows)] = (codes[0:1, :] * 256.0 + codes[1:2, :]).astype(jnp.int32)
        if k < 2:
            normed_out[pl.ds(offset(k), rows), :] = near[k][...]
            raw[:, pl.ds(offset(k), rows)] = near[2 + k][...]
        else:
            low, projected = project_rows(toks[k][:rows, :], gain[...], bias[...], flipped[...])
            normed_out[pl.ds(offset(k), rows), :] = low
            raw[:, pl.ds(offset(k), rows)] = projected
    starts = starts_out[...]
    positions = lax.broadcasted_iota(jnp.int32, starts.shape, 1)
    step = HEAD_DIM
    for r in range(0, raw.shape[0], step):
        values = raw[r : r + step, :].astype(F32)
        result = taps[r : r + step, 0:1] * values
        for lag in (1, 2):
            moved = jnp.where(lag_mask(starts, positions, lag), pltpu.roll(values, lag, 1), 0.0)
            result = result + taps[r : r + step, lag : lag + 1] * moved
        conv[r : r + step, :] = result.astype(BF)


def masked_scores(scores, starts, key_begin, query_begin, length):
    keys, queries = scores.shape
    diagonal = key_begin + keys > query_begin
    inside = key_begin >= LONG and query_begin + queries <= length - LONG
    if inside and not diagonal:
        return scores
    key_pos = key_begin + lax.broadcasted_iota(jnp.int32, scores.shape, 0)
    allowed = None
    if not inside:
        allowed = key_pos >= starts
    if diagonal:
        query_pos = query_begin + lax.broadcasted_iota(jnp.int32, scores.shape, 1)
        causal = key_pos <= query_pos
        allowed = causal if allowed is None else allowed & causal
    return jnp.where(allowed, scores, NEG_FILL)


def attend_kernel(ns, block, place, starts_ref, qkv, pieces, out_full, lse_out):
    length = qkv.shape[1]
    rows = length // ns
    keys = jnp.transpose(qkv[HEAD_DIM : 2 * HEAD_DIM, :])
    factor = LOG2E * HEAD_DIM ** (-0.5)
    for q in range(0, length, block):
        queries = qkv[0:HEAD_DIM, q : q + block]
        starts = starts_ref[:, q : q + block]
        scores = [
            masked_scores(nn(keys[u : u + block], queries), starts, u, q, length) * factor
            for u in range(0, q + block, block)
        ]
        top = scores[0]
        for one in scores[1:]:
            top = jnp.maximum(top, one)
        top = jnp.max(top, 0, keepdims=True)
        total = jnp.zeros((8, block), F32)
        result = jnp.zeros((HEAD_DIM, block), F32)
        for index, one in enumerate(scores):
            prob = jnp.exp2(one - top)
            total = total + jnp.sum(prob.reshape(block // 8, 8, block), 0)
            values = qkv[2 * HEAD_DIM :, index * block : (index + 1) * block]
            result = result + nn(values, prob.astype(BF))
        total = jnp.sum(total, 0, keepdims=True)
        lse_out[0, :, q : q + block] = top + jnp.log2(total)
        out_full[:, q : q + block] = result / total
    for k in range(ns):
        pieces[k] = out_full[:, k * rows : (k + 1) * rows].astype(BF)


def attend_back_kernel(ns, block, place, starts_ref, conv, raw, taps, flipped, gain, bias, normed, out_full, lse, *refs):
    grads_in, grads_out, grad_w, norm_sums, grad_attn, grad_conv, grad_raw = refs
    length = conv.shape[1]
    rows = length // ns
    head_scale = HEAD_DIM ** (-0.5)
    factor = LOG2E * head_scale
    for k in range(ns):
        grad_attn[:, k * rows : (k + 1) * rows] = grads_in[k]
    delta = jnp.sum(grad_attn[...].astype(F32) * out_full[...], 0, keepdims=True)
    keys = jnp.transpose(conv[HEAD_DIM : 2 * HEAD_DIM, :])
    values = jnp.transpose(conv[2 * HEAD_DIM :, :])
    grad_conv[HEAD_DIM:, :] = jnp.zeros((2 * HEAD_DIM, length), F32)
    for q in range(0, length, block):
        queries = conv[0:HEAD_DIM, q : q + block]
        grad_block = grad_attn[:, q : q + block]
        starts = starts_ref[:, q : q + block]
        grad_query = jnp.zeros((HEAD_DIM, block), F32)
        for u in range(0, q + block, block):
            scores = masked_scores(nn(keys[u : u + block], queries), starts, u, q, length)
            prob = jnp.exp2(scores * factor - lse[0, :, q : q + block])
            grad_prob = nn(values[u : u + block], grad_block)
            grad_scores = (prob * (grad_prob - delta[:, q : q + block])).astype(BF)
            grad_query = grad_query + nn(conv[HEAD_DIM : 2 * HEAD_DIM, u : u + block], grad_scores)
            grad_conv[HEAD_DIM : 2 * HEAD_DIM, u : u + block] += nt(queries, grad_scores)
            grad_conv[2 * HEAD_DIM :, u : u + block] += nt(grad_block, prob.astype(BF))
        grad_conv[0:HEAD_DIM, q : q + block] = grad_query
    starts = starts_ref[...]
    positions = lax.broadcasted_iota(jnp.int32, starts.shape, 1)
    tap_columns = []
    for part in range(3):
        at = slice(part * HEAD_DIM, (part + 1) * HEAD_DIM)
        grad = grad_conv[at, :] * (head_scale if part < 2 else 1.0)
        inputs = raw[at, :].astype(F32)
        result = taps[at, 0:1] * grad
        sums = [jnp.sum(grad * inputs, 1, keepdims=True)]
        for lag in (1, 2):
            kept = jnp.where(lag_mask(starts, positions, lag), grad, 0.0)
            result = result + taps[at, lag : lag + 1] * pltpu.roll(kept, length - lag, 1)
            sums.append(jnp.sum(kept * pltpu.roll(inputs, lag, 1), 1, keepdims=True))
        grad_raw[at, :] = result.astype(BF)
        lane = lax.broadcasted_iota(jnp.int32, (HEAD_DIM, grad_w.shape[1] - normed.shape[1]), 1)
        tap_columns.append(
            jnp.where(lane == 0, sums[0], jnp.where(lane == 1, sums[1], jnp.where(lane == 2, sums[2], 0.0)))
        )
    width = normed.shape[1]
    grads = nn(grad_raw[...], normed[...])
    grad_w[:, :width] = grads.astype(BF)
    weights = flipped[...].astype(F32)
    column = jnp.sum(grad_raw[...].astype(F32), 1, keepdims=True)
    norm_sums[0, 0:1, :] = jnp.sum(weights * (grads - bias[...] * column), 0, keepdims=True) / gain[...]
    norm_sums[0, 1:2, :] = jnp.sum(weights * column, 0, keepdims=True)
    for part in range(3):
        grad_w[part * HEAD_DIM : (part + 1) * HEAD_DIM, width:] = tap_columns[part].astype(BF)
    for k in range(ns):
        grads_out[k] = grad_raw[:, k * rows : (k + 1) * rows]


def middle_kernel(place, attn, tokens, w_o, cotangent, gain, bias, w_up, w_down, *refs):
    mixed, grad_middle, grad_low, sent, kept, normed_low, sums, grad_attn = refs[:8]
    middle, normed_two, grad_normed, scale = refs[8:]
    step = pl.program_id(0)
    steps = pl.num_programs(0)

    @pl.when(step == 0)
    def _():
        value = tokens[...].astype(F32) + tn(attn[...], w_o[...])
        normed, inv_scale = norm_stats(value)
        middle[...] = value
        normed_two[...] = normed
        scale[...] = jnp.broadcast_to(inv_scale, scale.shape)
        normed_low[...] = (normed * gain[...] + bias[...]).astype(BF)
        grad_normed[...] = jnp.zeros_like(grad_normed)

    positive = jnp.maximum(nn(normed_low[...], w_up[...]), 0.0)
    hidden = (positive * positive).astype(BF)
    grad_pre = (nt(cotangent[...], w_down[...]) * (2.0 * positive)).astype(BF)

    @pl.when(step < steps // 2)
    def _():
        sent[0] = hidden
        sent[1] = grad_pre

    @pl.when(step >= steps // 2)
    def _():
        kept[0] = hidden
        kept[1] = grad_pre

    middle[...] += nn(hidden, w_down[...])
    grad_normed[...] += nt(grad_pre, w_up[...])

    @pl.when(step == steps - 1)
    def _():
        mixed[...] = middle[...].astype(BF)
        back, grad_gain, grad_bias = norm_back(grad_normed[...], normed_two[...], scale[:, 0:1], gain[...])
        total = cotangent[...].astype(F32) + back
        grad_middle[...] = total
        low = total.astype(BF)
        grad_low[...] = low
        row = lax.broadcasted_iota(jnp.int32, sums.shape, 0)
        sums[...] = jnp.where(row == 0, grad_gain, jnp.where(row == 1, grad_bias, 0.0))
        grad_attn[...] = nt(w_o[...], low).astype(BF)


def grad_units(pre_low, pre_high, normed):
    both = jnp.concatenate([jnp.transpose(pre_low[0]), jnp.transpose(pre_high[0])], 0)
    grads = nn(both, normed[...])
    rows = grads.shape[0] // 2
    return jnp.concatenate([grads[:rows], grads[rows:]], 1)


def flip_half(columns, phase, place, cut, whole_flip, half_flip):
    side = jnp.where(phase == 0, 1 - place[3], place[3])
    whole_flip[...] = jnp.transpose(columns[...])
    half = cut // 2
    for i in range(whole_flip.shape[0] // cut):
        begin = pl.multiple_of(i * cut + side * half, half)
        half_flip[i * half : (i + 1) * half, :] = whole_flip[pl.ds(begin, half), :]


def rest_kernel(place, grad_low, attn_sent, attn_kept, sums, sent, kept):
    columns = jnp.transpose(grad_low[...])
    width = columns.shape[0]
    filled = jnp.transpose(jnp.concatenate([sums[...], jnp.zeros((128 - sums.shape[0], width), F32)], 0)).astype(BF)
    for attn, rest in ((attn_sent, sent), (attn_kept, kept)):
        half = attn.shape[0]
        rest[:, :half] = nt(columns, attn[...]).astype(BF)
        rest[:, half:] = filled


def own_kernel(cut, place, cotangent, hidden, pre_low, pre_high, normed, grad_down, grad_up, whole_flip, half_flip):
    @pl.when(pl.program_id(1) == 0)
    def _():
        flip_half(cotangent, pl.program_id(0), place, cut, whole_flip, half_flip)

    grad_down[0] = nn(half_flip[...], hidden[0]).astype(BF)
    grad_up[0] = grad_units(pre_low, pre_high, normed).astype(BF)


def other_kernel(
    cut, phase, place, cotangent, hidden, pre_low, pre_high, normed, own_down, own_up, grad_down, grad_up, whole_flip, half_flip
):
    @pl.when(pl.program_id(0) == 0)
    def _():
        flip_half(cotangent, phase, place, cut, whole_flip, half_flip)

    grad_down[...] = (own_down[0].astype(F32) + nn(half_flip[...], hidden[0])).astype(BF)
    grad_up[...] = (own_up[0].astype(F32) + grad_units(pre_low, pre_high, normed)).astype(BF)


def final_kernel(heads, groups, place, *refs):
    pieces, weights, (tokens, gain, grad_middle, d_tokens, stacked) = (refs[: len(groups)], refs[len(groups) : -5], refs[-5:])
    for (first, size), piece in zip(groups, pieces):
        for k in range(piece.shape[0]):
            for h in range(size):
                begin = (k * heads + first + h) * HEAD_DIM
                for part in range(3):
                    row = (h * 3 + part) * HEAD_DIM
                    stacked[part, begin : begin + HEAD_DIM, :] = piece[k, row : row + HEAD_DIM, :]
    grad_normed = nt(jnp.transpose(stacked[0]), weights[0][...])
    for part in (1, 2):
        grad_normed = grad_normed + nt(jnp.transpose(stacked[part]), weights[part][...])
    normed, inv_scale = norm_stats(tokens[...].astype(F32))
    back, _, _ = norm_back(grad_normed, normed, inv_scale, gain[...])
    d_tokens[...] = (grad_middle[...] + back).astype(BF)


def whole(shape):
    return pl.BlockSpec(shape, lambda *_: (0,) * len(shape))


def shaped(shape, dtype):
    return jax.ShapeDtypeStruct(shape, dtype)


def call(kernel, grid, inputs, outputs, scratch, flops, moved, name, place, ties=(), token=False):
    count = len(inputs)
    end = count + len(ties) + len(outputs)

    def body(place, *refs):
        kernel(place, *refs[:count], *refs[count + len(ties) : end], *refs[end + token :])
        if token:
            refs[end][...] = jnp.zeros_like(refs[end])

    if token:
        outputs = [*outputs, out((8, 128), F32)]

    return pl.pallas_call(
        body,
        grid_spec=pltpu.PrefetchScalarGridSpec(
            num_scalar_prefetch=1,
            grid=grid,
            in_specs=[spec for _, spec in inputs] + [pl.BlockSpec(memory_space=pl.ANY)] * len(ties),
            out_specs=[spec for _, _, spec in outputs],
            scratch_shapes=scratch,
        ),
        out_shape=[jax.ShapeDtypeStruct(shape, dtype) for shape, dtype, _ in outputs],
        compiler_params=pltpu.CompilerParams(vmem_limit_bytes=VMEM_LIMIT),
        cost_estimate=pl.CostEstimate(flops=flops // COST, bytes_accessed=moved // COST, transcendentals=0),
        name=name,
    )(place, *[array for array, _ in inputs], *ties)


def full(array):
    return (array, whole(array.shape))


def out(shape, dtype):
    return (shape, dtype, whole(shape))


def swap(values, axis, count, mask):
    return lax.ppermute(values, axis, [(i, i ^ mask) for i in range(count)])


def add_all(terms):
    total = terms[0].astype(F32)
    for one in terms[1:]:
        total = total + jnp.asarray(one, F32)
    return total


def after(values, tie, place):
    anywhere = pl.BlockSpec(memory_space=pl.ANY)
    return pl.pallas_call(
        lambda place, values, tie, result: None,
        in_specs=[pl.BlockSpec(memory_space=pltpu.SMEM), anywhere, anywhere],
        out_specs=anywhere,
        out_shape=jax.ShapeDtypeStruct(values.shape, values.dtype),
        input_output_aliases={1: 0},
        name="after",
    )(place, values, tie)


def add_low(*terms):
    return add_all(terms).astype(BF)


def sides(values, index, dim):
    block = values.shape[dim] // 2
    return [lax.dynamic_slice_in_dim(values, i * block, block, dim) for i in (index, 1 - index)]


def scatter(values, axis, groups=None):
    return lax.all_to_all(values, axis, split_axis=0, concat_axis=0, tiled=True, axis_index_groups=groups)


def zero_of(values):
    return jnp.minimum(jnp.abs(values[(0,) * values.ndim].astype(F32)), 0.0)


def local(tokens, segment_ids, cotangent, w_q, w_k, w_v, conv_weight, w_o, gain_one, bias_one, gain_two, bias_two, w_up, w_down):
    ns, nb = (lax.axis_size("seq"), lax.axis_size("batch"))
    s_index, b_index = (lax.axis_index("seq"), lax.axis_index("batch"))
    cores, y_size = (2, 2)
    x_size, z_size = (ns // cores, nb // y_size)
    rows, width = tokens.shape
    units = w_up.shape[1]
    heads = width // HEAD_DIM // ns
    length = rows * ns
    part = 3 * HEAD_DIM
    mine = heads * HEAD_DIM
    core = s_index % cores
    place = jnp.stack([s_index, core, s_index // cores, b_index % y_size]).astype(jnp.int32)
    gain_one, bias_one, gain_two, bias_two = (v.reshape(1, width) for v in (gain_one, bias_one, gain_two, bias_two))
    groups = [(0, heads - 1), (heads - 1, 1)]

    def to_core(values):
        return swap(values, "seq", ns, 1)

    codes = jnp.stack([segment_ids // 256, segment_ids % 256]).astype(BF)
    codes = jnp.pad(codes, ((0, ID_ROWS - 2), (0, width - rows)))
    coded = jnp.concatenate([tokens, codes], 0)
    toks = [coded] + [None] * (ns - 1)
    for k in range(2, ns, 2):
        toks[k] = swap(coded, "seq", ns, k)
    toks[1] = to_core(coded)
    columns_own, cut = (cotangent, width // z_size)
    if cut // 2 % 16:
        columns_own = columns_own.reshape(rows, z_size, y_size, width // nb)
        columns_own, cut = (jnp.transpose(columns_own, (0, 2, 1, 3)).reshape(rows, width), width)
    columns_other = to_core(columns_own)

    own = [lax.dynamic_slice_in_dim(w, s_index * mine, mine, 1) for w in (w_q, w_k, w_v)]
    taps = jnp.transpose(
        lax.dynamic_slice_in_dim(conv_weight, s_index * mine, mine, 2).reshape(3, 3, heads, HEAD_DIM), (2, 0, 3, 1)
    ).reshape(heads * part, 3)

    near = call(
        functools.partial(near_kernel, heads),
        (1,),
        [full(v) for v in (coded, toks[1], gain_one, bias_one, *own)],
        [
            out((heads * part, width), BF),
            out((rows, width), BF),
            out((rows, width), BF),
            out((heads * part, rows), BF),
            out((heads * part, rows), BF),
        ],
        [],
        4 * rows * width * heads * part,
        8 * rows * width,
        "near",
        place,
    )
    flipped = near[0]
    for k in range(2, ns, 2):
        toks[k] = after(toks[k], near[4], place)
        toks[k + 1] = to_core(toks[k])
    raw, conv, normed_in, starts = call(
        functools.partial(far_kernel, ns),
        (1,),
        [full(v) for v in (*near[1:], *toks, gain_one, bias_one, flipped, taps)],
        [
            out((heads * part, length), BF),
            out((heads * part, length), BF),
            out((length, width), BF),
            out((1, length), jnp.int32),
        ],
        [],
        4 * rows * width * heads * part,
        8 * length * width,
        "far",
        place,
    )

    block = 256

    def by_head(array, first, columns):
        return (array, pl.BlockSpec((array.shape[0] // heads, columns), lambda i, place: (first + i, 0)))

    def per_head(size, height, columns, dtype):
        return ((size * height, columns), dtype, pl.BlockSpec((height, columns), lambda i, place: (i, 0)))

    for first, size in [(0, heads)]:
        results = call(
            functools.partial(attend_kernel, ns, block),
            (size,),
            [full(starts), by_head(conv, first, length)],
            [
                ((ns, size * HEAD_DIM, rows), BF, pl.BlockSpec((ns, HEAD_DIM, rows), lambda i, place: (0, i, 0))),
                per_head(size, HEAD_DIM, length, F32),
                ((size, 1, length), F32, pl.BlockSpec((1, 1, length), lambda i, place: (i, 0, 0))),
            ],
            [],
            2 * length * length * HEAD_DIM * 4 * size,
            part * length * 4,
            "attend",
            place,
            [columns_other],
        )
        attn = scatter(results[0], "seq").reshape(width, rows)
        out_full, lse = results[1:]

    chunk = 512
    half = units // 2
    steps = half // chunk

    def unit_block(i, place):
        return jnp.where(i < steps, 1 - place[1], place[1]) * steps + lax.rem(i, steps)

    pair = (2, rows, half)
    results = call(
        middle_kernel,
        (2 * steps,),
        [full(v) for v in (attn, tokens, w_o, cotangent, gain_two, bias_two)]
        + [
            (w_up, pl.BlockSpec((width, chunk), lambda i, place: (0, unit_block(i, place)))),
            (w_down, pl.BlockSpec((chunk, width), lambda i, place: (unit_block(i, place), 0))),
        ],
        [
            out((rows, width), BF),
            out((rows, width), F32),
            out((rows, width), BF),
            (pair, BF, pl.BlockSpec((2, rows, chunk), lambda i, place: (0, 0, jnp.minimum(i, steps - 1)))),
            (pair, BF, pl.BlockSpec((2, rows, chunk), lambda i, place: (0, 0, jnp.maximum(i - steps, 0)))),
            out((rows, width), BF),
            out((8, width), F32),
            out((width, rows), BF),
        ],
        [pltpu.VMEM((rows, width), F32)] * 3 + [pltpu.VMEM((rows, 128), F32)],
        8 * rows * width * units + 4 * rows * width * width,
        4 * width * units,
        "middle",
        place,
    )
    mixed, grad_middle, grad_low, sent, kept, normed_mid, sums_two, grad_attn = results
    grad_attn = scatter(grad_attn.reshape(ns, mine, rows), "seq")
    normed_other = to_core(normed_mid)
    got = to_core(sent)

    half_width = width // 2
    piece = 128
    steps = half // 4 // piece
    chunk = half // steps
    lanes = width + 128

    def unit_inputs(array, columns, turn):
        at = lambda i, place: turn(i, place)[2] * steps + turn(i, place)[1]
        return [
            full(columns),
            (array, pl.BlockSpec((1, rows, chunk), lambda *i: (0, 0, turn(i[:-1], i[-1])[1]))),
            (array, pl.BlockSpec((1, rows, piece), lambda *i: (1, 0, at(i[:-1], i[-1])))),
            (array, pl.BlockSpec((1, rows, piece), lambda *i: (1, 0, 2 * steps + at(i[:-1], i[-1])))),
        ]

    def turn_for(phase):
        def turn(i, place):
            now, step = (i[0], i[1]) if phase is None else (phase, i[0])
            flip = lambda index: jnp.where(now == 0, 1 - index, index)
            return (now, step, flip(place[2]), flip(place[3]))

        return turn

    summed = [((2, half_width, half), (1, half_width, chunk), 2), ((2, half // 4, 2 * width), (1, piece, 2 * width), 1)]

    def partial_spec(which, turn):
        _, shape, dim = summed[which]
        place_of = lambda t: (t[0], t[1], 0) if dim == 1 else (t[0], 0, t[1])
        return pl.BlockSpec(shape, lambda *i: place_of(turn(i[:-1], i[-1])))

    rest = half_width + 128
    rest_sent, rest_kept = call(
        rest_kernel,
        (1,),
        [
            full(grad_low),
            (attn, pl.BlockSpec((half_width, rows), lambda i, place: (1 - place[1], 0))),
            (attn, pl.BlockSpec((half_width, rows), lambda i, place: (place[1], 0))),
            full(sums_two),
        ],
        [out((width, rest), BF), out((width, rest), BF)],
        [],
        2 * rows * width * width,
        4 * width * width,
        "rest",
        place,
    )
    rest_got = to_core(rest_sent)
    flip = [pltpu.VMEM((width, rows), BF), pltpu.VMEM((half_width, rows), BF)]
    turn = turn_for(None)
    own_down, own_up = call(
        functools.partial(own_kernel, cut),
        (2, steps),
        unit_inputs(kept, columns_own, turn) + [full(normed_mid)],
        [(summed[w][0], BF, partial_spec(w, turn)) for w in range(2)],
        flip,
        2 * rows * width * units,
        3 * width * units,
        "own_rows",
        place,
        [rest_kept],
    )

    def other_rows(phase, ties=()):
        turn = turn_for(phase)
        return call(
            functools.partial(other_kernel, cut, phase),
            (steps,),
            unit_inputs(got, columns_other, turn)
            + [full(normed_other), (own_down, partial_spec(0, turn)), (own_up, partial_spec(1, turn))],
            [
                ((half_width, half), BF, pl.BlockSpec((half_width, chunk), lambda i, place: (0, i))),
                ((half // 4, 2 * width), BF, pl.BlockSpec((piece, 2 * width), lambda i, place: (i, 0))),
            ],
            flip,
            rows * width * units,
            2 * width * units,
            "other_rows",
            place,
            ties,
            True,
        )

    chips = nb * x_size
    x_index, y_index = (s_index // cores, b_index % y_size)
    z_groups = [[z * y_size + y for z in range(z_size)] for y in range(y_size)]

    def over_z(groups, hold=0.0):
        if z_size > 4:
            values = jnp.concatenate([add_low(*terms, hold) for terms in groups], -1)
            return (jnp.sum(scatter(values, "batch", z_groups).astype(F32), 0), [values])
        cut = lambda m: jnp.concatenate(
            [
                add_low(*[lax.dynamic_index_in_dim(v, (b_index // y_size) ^ m, 0, keepdims=False) for v in terms], hold)
                for terms in groups
            ],
            -1,
        )
        sent = [cut(m) for m in range(1, z_size)]
        return (add_all([cut(0)] + [swap(v, "batch", nb, (m + 1) * y_size) for m, v in enumerate(sent)]), sent)

    down_sent, up_sent, token = other_rows(0)
    rest_sum = add_low(rest_kept, rest_got, token[0, 0], zero_of(grad_attn)).reshape(z_size, width // z_size, rest)
    rest_z = jnp.sum(scatter(rest_sum, "batch", z_groups).astype(F32), 0)
    up_got = swap(up_sent, "seq", ns, cores)
    down_got = swap(down_sent, "batch", nb, 1)
    down_kept, up_kept, _ = other_rows(1)

    head_rows = HEAD_DIM // nb

    back_pieces, head_grads, sums_heads = ([], [], [])

    def back(g, ties):
        first, size = groups[g]
        results = call(
            functools.partial(attend_back_kernel, ns, block),
            (size,),
            [
                full(starts),
                by_head(conv, first, length),
                by_head(raw, first, length),
                by_head(taps, first, 3),
                by_head(flipped, first, width),
                full(gain_one),
                full(bias_one),
                full(normed_in),
                by_head(out_full, first, length),
                (lse, pl.BlockSpec((1, 1, length), lambda i, place: (first + i, 0, 0))),
            ]
            + [(grad_attn, pl.BlockSpec((ns, HEAD_DIM, rows), lambda i, place: (0, first + i, 0)))],
            [
                ((ns, size * part, rows), BF, pl.BlockSpec((ns, part, rows), lambda i, place: (0, i, 0))),
                per_head(size, part, lanes, BF),
                ((size, 2, width), F32, pl.BlockSpec((1, 2, width), lambda i, place: (i, 0, 0))),
            ],
            [pltpu.VMEM((HEAD_DIM, length), BF), pltpu.VMEM((part, length), F32), pltpu.VMEM((part, length), BF)],
            2 * length * length * HEAD_DIM * 10 * size,
            length * width * 2,
            "attend_back",
            place,
            ties,
            True,
        )
        back_pieces.append(scatter(results[0], "seq"))
        head_grads.append(results[1])
        sums_heads.append(results[2])
        return results[3]

    piece = half // 2 // chips
    token = back(0, [down_kept, up_kept, rest_sum])
    hold = token[0, 0]
    up_there, up_here = [
        [v.reshape(z_size, piece, 2 * width) for v in side]
        for side in zip(*[sides(v, 1 - y_index, 0) for v in (up_kept, up_got)])
    ]
    pair = head_grads[0].reshape(-1, y_size, z_size, head_rows, lanes)
    pair = jnp.transpose(pair, (1, 2, 0, 3, 4)).reshape(y_size, z_size, -1, lanes)
    pair_there, pair_here = [v[0] for v in sides(pair, 1 - y_index, 0)]
    times = z_size // x_size
    fold = lambda v: jnp.stack(jnp.split(v.reshape(x_size, -1, rest), times, -1), 1).reshape(z_size, -1, rest // times)
    rest_there, rest_here = sides(rest_z.astype(BF), 1 - y_index, 0)
    y_sent = jnp.concatenate([add_low(*up_there, hold), pair_there, fold(rest_there)], -1)
    y_kept = jnp.concatenate([add_low(*up_here, hold), pair_here, fold(rest_here)], -1)
    y_got = swap(y_sent, "batch", nb, 1)
    hold = hold + zero_of(y_sent)
    down_z, down_sent = over_z([[v.reshape(z_size, -1, half) for v in (down_kept, down_got)]], hold)
    token = back(1, [y_sent, *down_sent])
    hold = token[0, 0]

    wide = 2 * width + lanes
    up_z, up_sent = over_z([[v[..., :wide] for v in (y_kept, y_got)]], hold + zero_of(back_pieces[0]))

    total = jnp.sum(jnp.concatenate(sums_heads, 0), 0)
    total = jnp.transpose(total.reshape(2, nb, ns, 3 * head_rows), (1, 3, 0, 2)).reshape(nb, 3 * head_rows, 2 * ns)
    total = jnp.pad(total, ((0, 0), (0, 0), (width + 3, lanes - width - 3 - 2 * ns)))
    single = jnp.transpose(head_grads[1].reshape(3, y_size, z_size, head_rows, lanes), (2, 1, 0, 3, 4))
    single = single.reshape(nb, -1, lanes)
    single = jnp.sum(scatter(add_low(single, total, zero_of(back_pieces[1])), "batch").astype(F32), 0).reshape(3, head_rows, lanes)
    unfold = lambda v: jnp.concatenate(
        [v.reshape(x_size, times, -1, rest // times)[:, i] for i in range(times)], -1
    ).reshape(-1, rest)
    rest_y = unfold(add_low(y_kept[..., wide:], y_got[..., wide:]))
    x_there, x_here = sides(jnp.concatenate([add_low(down_z, hold), rest_y], -1), 1 - x_index, 0)
    x_got = swap(x_there, "seq", ns, cores)

    (d_tokens,) = call(
        functools.partial(final_kernel, heads, groups),
        (1,),
        [full(v) for v in (*back_pieces, w_q, w_k, w_v, tokens, gain_one, grad_middle)],
        [out((rows, width), BF)],
        [pltpu.VMEM((3, width, rows), BF)],
        6 * rows * width * width,
        8 * width * width,
        "final",
        place,
        up_sent,
    )

    devices = [(d // ns, d % ns) for d in range(nb * ns)]
    everywhere = ("batch", "seq")

    pair = up_z[:, 2 * width : wide].astype(BF)
    granules = [*pair.reshape(-1, 3, head_rows, lanes), single.astype(BF)]
    norm_sums = single[:, :, width + 3 : width + 3 + 2 * ns].reshape(3 * head_rows, 2, ns)
    sums_one = jnp.sum(scatter(jnp.transpose(norm_sums, (2, 1, 0)), "seq"), 0)

    def position(b):
        return (b % y_size) * z_size + b // y_size

    pieces = []
    for slot in range(heads):
        perm = []
        for d, (b, s) in enumerate(devices):
            for h in range(heads):
                granule = (s * heads + h) * nb + position(b)
                if granule % heads == slot:
                    perm.append((d, granule // heads))
        ours = [(h * nb + position(b_index)) % heads == slot for h in range(heads)]
        sent = granules[-1]
        for h in range(heads - 1):
            sent = jnp.where(ours[h], granules[h], sent)
        pieces.append(lax.ppermute(sent, everywhere, perm))
    grad_qkv = jnp.concatenate(pieces, 1).astype(F32)

    size = piece
    up_value = up_z.astype(BF)
    chip = lambda b, s: ((s // cores) * y_size + b % y_size) * z_size + b // y_size
    got_up = []
    for color in range(2):
        perm = []
        for d, (b, s) in enumerate(devices):
            p = (color + chip(b, s)) % 2
            begin = (s % cores) * half + p * (half // 2) + chip(b, s) * size
            perm.append((d, begin // (2 * size)))
        first = (color + chip(b_index, s_index)) % 2 == 0
        got_up.append(lax.ppermute(jnp.where(first, up_value[:, :width], up_value[:, width : 2 * width]), everywhere, perm))
    first = (b_index * ns + s_index) * 2 * size % half < half // 2
    got_up = [jnp.where(first, got_up[0], got_up[1]), jnp.where(first, got_up[1], got_up[0])]
    got_up = jnp.concatenate(got_up, 0).astype(F32)

    value = add_low(x_here, x_got)
    size = value.shape[0] // cores
    here = lax.dynamic_slice_in_dim(value, core * size, size, 0)
    there = to_core(lax.dynamic_slice_in_dim(value, (1 - core) * size, size, 0))
    by_core = [jnp.where(core == 0, here, there).astype(F32), jnp.where(core == 0, there, here).astype(F32)]
    got_down = jnp.concatenate([v[:, :half] for v in by_core], 1)
    got_rest = jnp.concatenate([v[:, half : half + half_width] for v in by_core], 1)
    sums_two = here[:, half + half_width : half + half_width + 2].astype(F32)

    flat = jnp.swapaxes(grad_qkv[:, :, :width], 1, 2)
    return (
        mixed,
        d_tokens,
        flat[0],
        flat[1],
        flat[2],
        jnp.swapaxes(grad_qkv[:, :, width : width + 3], 1, 2),
        got_rest.T,
        sums_one[0],
        sums_one[1],
        sums_two[:, 0],
        sums_two[:, 1],
        got_up.T,
        got_down.T,
    )


def solution(mesh):
    split = ("batch", "seq")
    in_specs = (P(split, None), P(split), P(split, None)) + (P(),) * 11
    out_specs = (
        P(split, None),
        P(split, None),
        P(None, split),
        P(None, split),
        P(None, split),
        P(None, None, split),
        P(None, split),
        P(split),
        P(split),
        P(split),
        P(split),
        P(None, split),
        P(None, split),
    )
    return jax.shard_map(local, mesh=mesh, in_specs=in_specs, out_specs=out_specs, check_vma=False)
```

```python
import functools
import math

import jax
import jax.numpy as jnp
from jax import lax
from jax.experimental import pallas as pl
from jax.experimental.pallas import tpu as pltpu
from jax.sharding import PartitionSpec as P

HEAD_DIM = 64
EPS = 1e-05
NEG_FILL = -1e30
LONG = 512
ID_ROWS = 16
COST = 1
LOG2E = math.log2(math.e)
BF = jnp.bfloat16
F32 = jnp.float32
VMEM_LIMIT = 60 * 1024 * 1024


def nn(first, second):
    return lax.dot_general(first, second, (((1,), (0,)), ((), ())), preferred_element_type=F32)


def nt(first, second):
    return lax.dot_general(first, second, (((1,), (1,)), ((), ())), preferred_element_type=F32)


def tn(first, second):
    return lax.dot_general(first, second, (((0,), (0,)), ((), ())), preferred_element_type=F32)


def norm_stats(values):
    centred = values - jnp.mean(values, axis=-1, keepdims=True)
    variance = jnp.mean(centred * centred, axis=-1, keepdims=True)
    inv_scale = lax.rsqrt(variance + EPS)
    return (centred * inv_scale, inv_scale)


def norm_back(grad_out, normed, inv_scale, gain):
    grad_norm = grad_out * gain
    projected = (
        grad_norm
        - jnp.mean(grad_norm, -1, keepdims=True)
        - normed * jnp.mean(grad_norm * normed, -1, keepdims=True)
    )
    return (projected * inv_scale, jnp.sum(grad_out * normed, 0, keepdims=True), jnp.sum(grad_out, 0, keepdims=True))


def lag_mask(starts, positions, lag):
    return positions - lag >= starts


def project_rows(tok, gain, bias, flipped):
    normed, _ = norm_stats(tok.astype(F32))
    low = (normed * gain + bias).astype(BF)
    return (low, nn(flipped, jnp.transpose(low)).astype(BF))


def near_kernel(heads, place, own, other, gain, bias, w_q, w_k, w_v, flipped, low_own, low_other, raw_own, raw_other):
    rows = low_own.shape[0]
    for h in range(heads):
        for part, weights in enumerate((w_q, w_k, w_v)):
            row = (h * 3 + part) * HEAD_DIM
            flipped[row : row + HEAD_DIM, :] = jnp.transpose(weights[:, h * HEAD_DIM : (h + 1) * HEAD_DIM])
    low_own[...], raw_own[...] = project_rows(own[:rows, :], gain[...], bias[...], flipped[...])
    low_other[...], raw_other[...] = project_rows(other[:rows, :], gain[...], bias[...], flipped[...])


def far_kernel(ns, place, *refs):
    near, toks = (refs[:4], refs[4 : 4 + ns])
    gain, bias, flipped, taps, raw, conv, normed_out, starts_out = refs[4 + ns :]
    rows = near[0].shape[0]

    def offset(k):
        return pl.multiple_of((place[0] ^ k) * rows, rows)

    for k in range(ns):
        codes = toks[k][rows : rows + ID_ROWS, :rows].astype(F32)
        starts_out[:, pl.ds(offset(k), rows)] = (codes[0:1, :] * 256.0 + codes[1:2, :]).astype(jnp.int32)
        if k < 2:
            normed_out[pl.ds(offset(k), rows), :] = near[k][...]
            raw[:, pl.ds(offset(k), rows)] = near[2 + k][...]
        else:
            low, projected = project_rows(toks[k][:rows, :], gain[...], bias[...], flipped[...])
            normed_out[pl.ds(offset(k), rows), :] = low
            raw[:, pl.ds(offset(k), rows)] = projected
    starts = starts_out[...]
    positions = lax.broadcasted_iota(jnp.int32, starts.shape, 1)
    step = HEAD_DIM
    for r in range(0, raw.shape[0], step):
        values = raw[r : r + step, :].astype(F32)
        result = taps[r : r + step, 0:1] * values
        for lag in (1, 2):
            moved = jnp.where(lag_mask(starts, positions, lag), pltpu.roll(values, lag, 1), 0.0)
            result = result + taps[r : r + step, lag : lag + 1] * moved
        conv[r : r + step, :] = result.astype(BF)


def masked_scores(scores, starts, key_begin, query_begin, length):
    keys, queries = scores.shape
    diagonal = key_begin + keys > query_begin
    inside = key_begin >= LONG and query_begin + queries <= length - LONG
    if inside and not diagonal:
        return scores
    key_pos = key_begin + lax.broadcasted_iota(jnp.int32, scores.shape, 0)
    allowed = None
    if not inside:
        allowed = key_pos >= starts
    if diagonal:
        query_pos = query_begin + lax.broadcasted_iota(jnp.int32, scores.shape, 1)
        causal = key_pos <= query_pos
        allowed = causal if allowed is None else allowed & causal
    return jnp.where(allowed, scores, NEG_FILL)


def attend_kernel(ns, block, step, place, starts_ref, qkv, pieces, out_full, lse_out):
    length = qkv.shape[1]
    rows = length // ns
    keys = jnp.transpose(qkv[HEAD_DIM : 2 * HEAD_DIM, :])
    factor = LOG2E * HEAD_DIM ** (-0.5)
    for q in range(0, length, block):
        queries = qkv[0:HEAD_DIM, q : q + block]
        starts = starts_ref[:, q : q + block]
        scores = [
            masked_scores(nn(keys[u : u + step], queries), starts, u, q, length) * factor
            for u in range(0, q + block, step)
        ]
        top = scores[0]
        for one in scores[1:]:
            top = jnp.maximum(top, one)
        top = jnp.max(top, 0, keepdims=True)
        total = jnp.zeros((8, block), F32)
        result = jnp.zeros((HEAD_DIM, block), F32)
        for index, one in enumerate(scores):
            prob = jnp.exp2(one - top)
            total = total + jnp.sum(prob.reshape(step // 8, 8, block), 0)
            values = qkv[2 * HEAD_DIM :, index * step : (index + 1) * step]
            result = result + nn(values, prob.astype(BF))
        total = jnp.sum(total, 0, keepdims=True)
        lse_out[0, :, q : q + block] = top + jnp.log2(total)
        out_full[:, q : q + block] = result / total
    for k in range(ns):
        pieces[k] = out_full[:, k * rows : (k + 1) * rows].astype(BF)


def attend_back_kernel(ns, block, step, place, starts_ref, conv, raw, taps, flipped, gain, bias, normed, out_full, lse, *refs):
    grads_in, grads_out, grad_w, norm_sums, grad_attn, grad_conv, grad_raw = refs
    length = conv.shape[1]
    rows = length // ns
    head_scale = HEAD_DIM ** (-0.5)
    factor = LOG2E * head_scale
    for k in range(ns):
        grad_attn[:, k * rows : (k + 1) * rows] = grads_in[k]
    delta = jnp.sum(grad_attn[...].astype(F32) * out_full[...], 0, keepdims=True)
    keys = jnp.transpose(conv[HEAD_DIM : 2 * HEAD_DIM, :])
    values = jnp.transpose(conv[2 * HEAD_DIM :, :])
    grad_conv[HEAD_DIM:, :] = jnp.zeros((2 * HEAD_DIM, length), F32)
    for q in range(0, length, block):
        queries = conv[0:HEAD_DIM, q : q + block]
        grad_block = grad_attn[:, q : q + block]
        starts = starts_ref[:, q : q + block]
        grad_query = jnp.zeros((HEAD_DIM, block), F32)
        for u in range(0, q + block, step):
            scores = masked_scores(nn(keys[u : u + step], queries), starts, u, q, length)
            prob = jnp.exp2(scores * factor - lse[0, :, q : q + block])
            grad_prob = nn(values[u : u + step], grad_block)
            grad_scores = (prob * (grad_prob - delta[:, q : q + block])).astype(BF)
            grad_query = grad_query + nn(conv[HEAD_DIM : 2 * HEAD_DIM, u : u + step], grad_scores)
            grad_conv[HEAD_DIM : 2 * HEAD_DIM, u : u + step] += nt(queries, grad_scores)
            grad_conv[2 * HEAD_DIM :, u : u + step] += nt(grad_block, prob.astype(BF))
        grad_conv[0:HEAD_DIM, q : q + block] = grad_query
    starts = starts_ref[...]
    positions = lax.broadcasted_iota(jnp.int32, starts.shape, 1)
    tap_columns = []
    for part in range(3):
        at = slice(part * HEAD_DIM, (part + 1) * HEAD_DIM)
        grad = grad_conv[at, :] * (head_scale if part < 2 else 1.0)
        inputs = raw[at, :].astype(F32)
        result = taps[at, 0:1] * grad
        sums = [jnp.sum(grad * inputs, 1, keepdims=True)]
        for lag in (1, 2):
            kept = jnp.where(lag_mask(starts, positions, lag), grad, 0.0)
            result = result + taps[at, lag : lag + 1] * pltpu.roll(kept, length - lag, 1)
            sums.append(jnp.sum(kept * pltpu.roll(inputs, lag, 1), 1, keepdims=True))
        grad_raw[at, :] = result.astype(BF)
        lane = lax.broadcasted_iota(jnp.int32, (HEAD_DIM, grad_w.shape[1] - normed.shape[1]), 1)
        tap_columns.append(
            jnp.where(lane == 0, sums[0], jnp.where(lane == 1, sums[1], jnp.where(lane == 2, sums[2], 0.0)))
        )
    width = normed.shape[1]
    grads = nn(grad_raw[...], normed[...])
    grad_w[:, :width] = grads.astype(BF)
    weights = flipped[...].astype(F32)
    column = jnp.sum(grad_raw[...].astype(F32), 1, keepdims=True)
    norm_sums[0, 0:1, :] = jnp.sum(weights * (grads - bias[...] * column), 0, keepdims=True) / gain[...]
    norm_sums[0, 1:2, :] = jnp.sum(weights * column, 0, keepdims=True)
    for part in range(3):
        grad_w[part * HEAD_DIM : (part + 1) * HEAD_DIM, width:] = tap_columns[part].astype(BF)
    for k in range(ns):
        grads_out[k] = grad_raw[:, k * rows : (k + 1) * rows]


def middle_kernel(place, attn, tokens, w_o, cotangent, gain, bias, w_up, w_down, *refs):
    mixed, grad_middle, grad_low, sent, kept, normed_low, sums, grad_attn = refs[:8]
    middle, normed_two, grad_normed, scale = refs[8:]
    step = pl.program_id(0)
    steps = pl.num_programs(0)

    @pl.when(step == 0)
    def _():
        value = tokens[...].astype(F32) + tn(attn[...], w_o[...])
        normed, inv_scale = norm_stats(value)
        middle[...] = value
        normed_two[...] = normed
        scale[...] = jnp.broadcast_to(inv_scale, scale.shape)
        normed_low[...] = (normed * gain[...] + bias[...]).astype(BF)
        grad_normed[...] = jnp.zeros_like(grad_normed)

    positive = jnp.maximum(nn(normed_low[...], w_up[...]), 0.0)
    hidden = (positive * positive).astype(BF)
    grad_pre = (nt(cotangent[...], w_down[...]) * (2.0 * positive)).astype(BF)

    @pl.when(step < steps // 2)
    def _():
        sent[0] = hidden
        sent[1] = grad_pre

    @pl.when(step >= steps // 2)
    def _():
        kept[0] = hidden
        kept[1] = grad_pre

    middle[...] += nn(hidden, w_down[...])
    grad_normed[...] += nt(grad_pre, w_up[...])

    @pl.when(step == steps - 1)
    def _():
        mixed[...] = middle[...].astype(BF)
        back, grad_gain, grad_bias = norm_back(grad_normed[...], normed_two[...], scale[:, 0:1], gain[...])
        total = cotangent[...].astype(F32) + back
        grad_middle[...] = total
        low = total.astype(BF)
        grad_low[...] = low
        row = lax.broadcasted_iota(jnp.int32, sums.shape, 0)
        sums[...] = jnp.where(row == 0, grad_gain, jnp.where(row == 1, grad_bias, 0.0))
        grad_attn[...] = nt(w_o[...], low).astype(BF)


def grad_units(pre_low, pre_high, normed):
    both = jnp.concatenate([jnp.transpose(pre_low[0]), jnp.transpose(pre_high[0])], 0)
    grads = nn(both, normed[...])
    rows = grads.shape[0] // 2
    return jnp.concatenate([grads[:rows], grads[rows:]], 1)


def flip_half(columns, phase, place, cut, whole_flip, half_flip):
    side = jnp.where(phase == 0, 1 - place[3], place[3])
    whole_flip[...] = jnp.transpose(columns[...])
    half = cut // 2
    for i in range(whole_flip.shape[0] // cut):
        begin = pl.multiple_of(i * cut + side * half, half)
        half_flip[i * half : (i + 1) * half, :] = whole_flip[pl.ds(begin, half), :]


def rest_kernel(place, grad_low, attn_sent, attn_kept, sums, sent, kept):
    columns = jnp.transpose(grad_low[...])
    width = columns.shape[0]
    filled = jnp.transpose(jnp.concatenate([sums[...], jnp.zeros((128 - sums.shape[0], width), F32)], 0)).astype(BF)
    for attn, rest in ((attn_sent, sent), (attn_kept, kept)):
        half = attn.shape[0]
        rest[:, :half] = nt(columns, attn[...]).astype(BF)
        rest[:, half:] = filled


def weight_kernel(cut, phase, place, *refs):
    g_own, g_got, hidden_own, hidden_got, low_own, low_got, high_own, high_got, n_own, n_got = refs[:10]
    grad_down, grad_up = refs[10 + 2 * phase : 12 + 2 * phase]
    whole_flip, flip_own, flip_got = refs[-3:]

    @pl.when(pl.program_id(0) == 0)
    def _():
        flip_half(g_own, phase, place, cut, whole_flip, flip_own)
        flip_half(g_got, phase, place, cut, whole_flip, flip_got)
        if phase == 1:
            refs[14][...] = (refs[10][...].astype(F32) + refs[11][...].astype(F32)).astype(BF)

    grad_down[...] = (nn(flip_own[...], hidden_own[0]) + nn(flip_got[...], hidden_got[0])).astype(BF)
    pre_own = jnp.concatenate([jnp.transpose(low_own[0]), jnp.transpose(high_own[0])], 0)
    pre_got = jnp.concatenate([jnp.transpose(low_got[0]), jnp.transpose(high_got[0])], 0)
    grads = (nn(pre_own, n_own[...]) + nn(pre_got, n_got[...])).astype(BF)
    rows, width = (grads.shape[0] // 2, grads.shape[1])
    grad_up[:, :width] = grads[:rows]
    grad_up[:, width:] = grads[rows:]


def sum_refs(refs, index):
    total = refs[0][index].astype(F32)
    for ref in refs[1:]:
        total = total + ref[index].astype(F32)
    return total


def turn_y_kernel(heads, head_rows, place, up_kept, up_got, pair, rest_z, down_kept, down_got, y_sent, y_kept, *downs):
    y, z = (place[3], place[4])
    z_size, piece, _ = y_sent.shape
    wide, lanes = (up_kept.shape[1], pair.shape[1])
    rest = rest_z.shape[2]
    x_size = rest_z.shape[1] // (2 * piece)
    times = z_size // x_size
    cut = rest // times
    parts = heads * 3
    for side, result in ((1 - y, y_sent), (y, y_kept)):
        block = z_size * piece
        at = pl.ds(pl.multiple_of(side * block, block), block)
        result[:, :, :wide] = sum_refs((up_kept, up_got), (at, slice(None))).astype(BF).reshape(z_size, piece, wide)
        run = z_size * head_rows
        taken = [
            pair[pl.ds(pl.multiple_of(p * HEAD_DIM + side * run, run), run), :].astype(F32) for p in range(parts)
        ]
        for i in range(z_size):
            rows = jnp.concatenate([v[i * head_rows : (i + 1) * head_rows] for v in taken], 0)
            result[i, :, wide : wide + lanes] = rows.astype(BF)
        for x in range(x_size):
            at = pl.ds(pl.multiple_of((side * x_size + x) * piece, piece), piece)
            total = rest_z[0, at, :].astype(F32)
            for i in range(1, rest_z.shape[0]):
                total = total + rest_z[i, at, :].astype(F32)
            for i in range(times):
                result[x * times + i, :, wide + lanes :] = total[:, i * cut : (i + 1) * cut].astype(BF)
    block = downs[0].shape[0]
    for m, result in enumerate(downs):
        at = pl.ds(pl.multiple_of((z ^ m) * block, block), block)
        result[...] = sum_refs((down_kept, down_got), (at, slice(None))).astype(BF)


def turn_z_kernel(rest, place, *refs):
    y_kept, y_got, last_kept, last_got, own, one, two, three, sent, kept = refs[:10]
    ups = refs[10:]
    x, z = (place[2], place[4])
    last_lanes = last_kept.shape[2]
    wide = ups[0].shape[1] - last_lanes // 2
    z_size, piece, lanes = y_kept.shape
    last_rows = last_kept.shape[1]
    for m, result in enumerate(ups):
        result[:, :wide] = sum_refs((y_kept, y_got), (z ^ m, slice(None), slice(0, wide))).astype(BF)
        last = sum_refs((last_kept, last_got), z ^ m)
        last = jnp.concatenate([last[:, : last_lanes // 2], last[:, last_lanes // 2 :]], 0)
        result[:, wide:] = last.astype(BF)
    cut = lanes - wide
    times = rest // cut
    half = own.shape[1]
    for side, result in ((1 - x, sent), (x, kept)):
        at = pl.ds(pl.multiple_of(side * piece, piece), piece)
        result[:, :half] = sum_refs((own, one, two, three), (at, slice(None))).astype(BF)
        for i in range(times):
            both = sum_refs((y_kept, y_got), (side * times + i, slice(None), slice(wide, lanes)))
            result[:, half + i * cut : half + (i + 1) * cut] = both.astype(BF)


def final_kernel(heads, groups, place, *refs):
    pieces, weights, (tokens, gain, grad_middle, d_tokens, stacked) = (refs[: len(groups)], refs[len(groups) : -5], refs[-5:])
    for (first, size), piece in zip(groups, pieces):
        for k in range(piece.shape[0]):
            for h in range(size):
                begin = (k * heads + first + h) * HEAD_DIM
                for part in range(3):
                    row = (h * 3 + part) * HEAD_DIM
                    stacked[part, begin : begin + HEAD_DIM, :] = piece[k, row : row + HEAD_DIM, :]
    grad_normed = nt(jnp.transpose(stacked[0]), weights[0][...])
    for part in (1, 2):
        grad_normed = grad_normed + nt(jnp.transpose(stacked[part]), weights[part][...])
    normed, inv_scale = norm_stats(tokens[...].astype(F32))
    back, _, _ = norm_back(grad_normed, normed, inv_scale, gain[...])
    d_tokens[...] = (grad_middle[...] + back).astype(BF)


def whole(shape):
    return pl.BlockSpec(shape, lambda *_: (0,) * len(shape))


def shaped(shape, dtype):
    return jax.ShapeDtypeStruct(shape, dtype)


def call(kernel, grid, inputs, outputs, scratch, flops, moved, name, place, ties=(), token=False, through=()):
    count = len(inputs)
    held = len(ties) + len(through)
    end = count + held + len(outputs)

    def body(place, *refs):
        kernel(place, *refs[:count], *refs[count + held : end], *refs[end + token + len(through) :])
        if token:
            refs[end][...] = jnp.zeros_like(refs[end])

    aliases = {}
    if token:
        outputs = [*outputs, out((8, 128), F32)]
    for array in through:
        aliases[1 + count + len(ties) + len(aliases)] = len(outputs)
        outputs = [*outputs, (array.shape, array.dtype, pl.BlockSpec(memory_space=pl.ANY))]

    return pl.pallas_call(
        body,
        grid_spec=pltpu.PrefetchScalarGridSpec(
            num_scalar_prefetch=1,
            grid=grid,
            in_specs=[spec for _, spec in inputs] + [pl.BlockSpec(memory_space=pl.ANY)] * held,
            out_specs=[spec for _, _, spec in outputs],
            scratch_shapes=scratch,
        ),
        out_shape=[jax.ShapeDtypeStruct(shape, dtype) for shape, dtype, _ in outputs],
        compiler_params=pltpu.CompilerParams(vmem_limit_bytes=VMEM_LIMIT),
        cost_estimate=pl.CostEstimate(flops=flops // COST, bytes_accessed=moved // COST, transcendentals=0),
        name=name,
        input_output_aliases=aliases,
    )(place, *[array for array, _ in inputs], *ties, *through)


def full(array):
    return (array, whole(array.shape))


def out(shape, dtype):
    return (shape, dtype, whole(shape))


def swap(values, axis, count, mask):
    return lax.ppermute(values, axis, [(i, i ^ mask) for i in range(count)])


def add_all(terms):
    total = terms[0].astype(F32)
    for one in terms[1:]:
        total = total + jnp.asarray(one, F32)
    return total


def after(values, tie, place):
    anywhere = pl.BlockSpec(memory_space=pl.ANY)
    return pl.pallas_call(
        lambda place, values, tie, result: None,
        in_specs=[pl.BlockSpec(memory_space=pltpu.SMEM), anywhere, anywhere],
        out_specs=anywhere,
        out_shape=jax.ShapeDtypeStruct(values.shape, values.dtype),
        input_output_aliases={1: 0},
        name="after",
    )(place, values, tie)


def add_low(*terms):
    return add_all(terms).astype(BF)


def sides(values, index, dim):
    block = values.shape[dim] // 2
    return [lax.dynamic_slice_in_dim(values, i * block, block, dim) for i in (index, 1 - index)]


def scatter(values, axis, groups=None):
    return lax.all_to_all(values, axis, split_axis=0, concat_axis=0, tiled=True, axis_index_groups=groups)


def zero_of(values):
    return jnp.minimum(jnp.abs(values[(0,) * values.ndim].astype(F32)), 0.0)


def local(tokens, segment_ids, cotangent, w_q, w_k, w_v, conv_weight, w_o, gain_one, bias_one, gain_two, bias_two, w_up, w_down):
    ns, nb = (lax.axis_size("seq"), lax.axis_size("batch"))
    s_index, b_index = (lax.axis_index("seq"), lax.axis_index("batch"))
    cores, y_size = (2, 2)
    x_size, z_size = (ns // cores, nb // y_size)
    rows, width = tokens.shape
    units = w_up.shape[1]
    heads = width // HEAD_DIM // ns
    length = rows * ns
    part = 3 * HEAD_DIM
    mine = heads * HEAD_DIM
    core = s_index % cores
    place = jnp.stack([s_index, core, s_index // cores, b_index % y_size, b_index // y_size]).astype(jnp.int32)
    gain_one, bias_one, gain_two, bias_two = (v.reshape(1, width) for v in (gain_one, bias_one, gain_two, bias_two))
    groups = [(0, heads - 1), (heads - 1, 1)]

    def to_core(values):
        return swap(values, "seq", ns, 1)

    codes = jnp.stack([segment_ids // 256, segment_ids % 256]).astype(BF)
    codes = jnp.pad(codes, ((0, ID_ROWS - 2), (0, width - rows)))
    coded = jnp.concatenate([tokens, codes], 0)
    toks = [coded] + [None] * (ns - 1)
    for k in range(2, ns, 2):
        toks[k] = swap(coded, "seq", ns, k)
    toks[1] = to_core(coded)
    columns_own, cut = (cotangent, width // z_size)
    if cut // 2 % 16:
        columns_own = columns_own.reshape(rows, z_size, y_size, width // nb)
        columns_own, cut = (jnp.transpose(columns_own, (0, 2, 1, 3)).reshape(rows, width), width)
    columns_other = to_core(columns_own)

    own = [lax.dynamic_slice_in_dim(w, s_index * mine, mine, 1) for w in (w_q, w_k, w_v)]
    taps = jnp.transpose(
        lax.dynamic_slice_in_dim(conv_weight, s_index * mine, mine, 2).reshape(3, 3, heads, HEAD_DIM), (2, 0, 3, 1)
    ).reshape(heads * part, 3)

    near = call(
        functools.partial(near_kernel, heads),
        (1,),
        [full(v) for v in (coded, toks[1], gain_one, bias_one, *own)],
        [
            out((heads * part, width), BF),
            out((rows, width), BF),
            out((rows, width), BF),
            out((heads * part, rows), BF),
            out((heads * part, rows), BF),
        ],
        [],
        4 * rows * width * heads * part,
        8 * rows * width,
        "near",
        place,
    )
    flipped = near[0]
    for k in range(2, ns, 2):
        toks[k] = after(toks[k], near[4], place)
        toks[k + 1] = to_core(toks[k])
    raw, conv, normed_in, starts = call(
        functools.partial(far_kernel, ns),
        (1,),
        [full(v) for v in (*near[1:], *toks, gain_one, bias_one, flipped, taps)],
        [
            out((heads * part, length), BF),
            out((heads * part, length), BF),
            out((length, width), BF),
            out((1, length), jnp.int32),
        ],
        [],
        4 * rows * width * heads * part,
        8 * length * width,
        "far",
        place,
    )

    fore, hind = ((512, 512), (512, 512))

    def by_head(array, first, columns):
        return (array, pl.BlockSpec((array.shape[0] // heads, columns), lambda i, place: (first + i, 0)))

    def per_head(size, height, columns, dtype):
        return ((size * height, columns), dtype, pl.BlockSpec((height, columns), lambda i, place: (i, 0)))

    for first, size in [(0, heads)]:
        results = call(
            functools.partial(attend_kernel, ns, *fore),
            (size,),
            [full(starts), by_head(conv, first, length)],
            [
                ((ns, size * HEAD_DIM, rows), BF, pl.BlockSpec((ns, HEAD_DIM, rows), lambda i, place: (0, i, 0))),
                per_head(size, HEAD_DIM, length, F32),
                ((size, 1, length), F32, pl.BlockSpec((1, 1, length), lambda i, place: (i, 0, 0))),
            ],
            [],
            2 * length * length * HEAD_DIM * 4 * size,
            part * length * 4,
            "attend",
            place,
            [columns_other],
        )
        attn = scatter(results[0], "seq").reshape(width, rows)
        out_full, lse = results[1:]

    chunk = 512
    half = units // 2
    steps = half // chunk

    def unit_block(i, place):
        return jnp.where(i < steps, 1 - place[1], place[1]) * steps + lax.rem(i, steps)

    pair = (2, rows, half)
    results = call(
        middle_kernel,
        (2 * steps,),
        [full(v) for v in (attn, tokens, w_o, cotangent, gain_two, bias_two)]
        + [
            (w_up, pl.BlockSpec((width, chunk), lambda i, place: (0, unit_block(i, place)))),
            (w_down, pl.BlockSpec((chunk, width), lambda i, place: (unit_block(i, place), 0))),
        ],
        [
            out((rows, width), BF),
            out((rows, width), F32),
            out((rows, width), BF),
            (pair, BF, pl.BlockSpec((2, rows, chunk), lambda i, place: (0, 0, jnp.minimum(i, steps - 1)))),
            (pair, BF, pl.BlockSpec((2, rows, chunk), lambda i, place: (0, 0, jnp.maximum(i - steps, 0)))),
            out((rows, width), BF),
            out((8, width), F32),
            out((width, rows), BF),
        ],
        [pltpu.VMEM((rows, width), F32)] * 3 + [pltpu.VMEM((rows, 128), F32)],
        8 * rows * width * units + 4 * rows * width * width,
        4 * width * units,
        "middle",
        place,
    )
    mixed, grad_middle, grad_low, sent, kept, normed_mid, sums_two, grad_attn = results
    grad_attn = scatter(grad_attn.reshape(ns, mine, rows), "seq")
    normed_other = to_core(normed_mid)
    got = to_core(sent)

    half_width = width // 2
    piece = 128
    steps = half // 4 // piece
    chunk = half // steps
    lanes = width + 256

    rest = half_width + 128
    rest_sent, rest_kept = call(
        rest_kernel,
        (1,),
        [
            full(grad_low),
            (attn, pl.BlockSpec((half_width, rows), lambda i, place: (1 - place[1], 0))),
            (attn, pl.BlockSpec((half_width, rows), lambda i, place: (place[1], 0))),
            full(sums_two),
        ],
        [out((width, rest), BF), out((width, rest), BF)],
        [],
        2 * rows * width * width,
        4 * width * width,
        "rest",
        place,
    )
    rest_got = to_core(rest_sent)
    def weights(phase, rest_parts=(), ties=()):
        def x_half(place):
            return (1 - place[2] if phase == 0 else place[2]) * steps

        return call(
            functools.partial(weight_kernel, cut, phase),
            (steps,),
            [full(columns_own), full(columns_other)]
            + [(v, pl.BlockSpec((1, rows, chunk), lambda i, place: (0, 0, i))) for v in (kept, got)]
            + [(v, pl.BlockSpec((1, rows, piece), lambda i, place: (1, 0, x_half(place) + i))) for v in (kept, got)]
            + [
                (v, pl.BlockSpec((1, rows, piece), lambda i, place: (1, 0, 2 * steps + x_half(place) + i)))
                for v in (kept, got)
            ]
            + [full(v) for v in (normed_mid, normed_other, *rest_parts)],
            [
                ((half_width, half), BF, pl.BlockSpec((half_width, chunk), lambda i, place: (0, i))),
                ((half // 4, 2 * width), BF, pl.BlockSpec((piece, 2 * width), lambda i, place: (i, 0))),
            ]
            + [out(v.shape, BF) for v in rest_parts[:1]],
            [pltpu.VMEM((width, rows), BF)] + [pltpu.VMEM((half_width, rows), BF)] * 2,
            2 * rows * width * units,
            3 * width * units,
            "weights",
            place,
            ties,
        )

    chips = nb * x_size
    x_index, y_index = (s_index // cores, b_index % y_size)
    z_groups = [[z * y_size + y for z in range(z_size)] for y in range(y_size)]

    down_sent, up_sent = weights(0)
    up_got = swap(up_sent, "seq", ns, cores)
    down_got = swap(down_sent, "batch", nb, 1)
    down_kept, up_kept, rest_sum = weights(1, (rest_kept, rest_got), [grad_attn, up_sent])
    rest_z = scatter(rest_sum.reshape(z_size, width // z_size, rest), "batch", z_groups)

    head_rows = HEAD_DIM // nb

    back_pieces, head_grads, sums_heads = ([], [], [])

    def back(g, ties):
        first, size = groups[g]
        results = call(
            functools.partial(attend_back_kernel, ns, *hind),
            (size,),
            [
                full(starts),
                by_head(conv, first, length),
                by_head(raw, first, length),
                by_head(taps, first, 3),
                by_head(flipped, first, width),
                full(gain_one),
                full(bias_one),
                full(normed_in),
                by_head(out_full, first, length),
                (lse, pl.BlockSpec((1, 1, length), lambda i, place: (first + i, 0, 0))),
            ]
            + [(grad_attn, pl.BlockSpec((ns, HEAD_DIM, rows), lambda i, place: (0, first + i, 0)))],
            [
                ((ns, size * part, rows), BF, pl.BlockSpec((ns, part, rows), lambda i, place: (0, i, 0))),
                per_head(size, part, lanes, BF),
                ((size, 2, width), F32, pl.BlockSpec((1, 2, width), lambda i, place: (i, 0, 0))),
            ],
            [pltpu.VMEM((HEAD_DIM, length), BF), pltpu.VMEM((part, length), F32), pltpu.VMEM((part, length), BF)],
            2 * length * length * HEAD_DIM * 10 * size,
            length * width * 2,
            "attend_back",
            place,
            ties,
            True,
        )
        back_pieces.append(results[0])
        head_grads.append(results[1])
        sums_heads.append(results[2])
        return results[3]

    piece = half // 2 // chips
    token = back(0, [down_kept, up_kept, rest_sum])
    wide = 2 * width + lanes
    times = z_size // x_size

    def fold(values):
        return jnp.stack(jnp.split(values.reshape(x_size, -1, rest), times, -1), 1).reshape(z_size, -1, rest // times)

    def unfold(values):
        values = values.reshape(x_size, times, -1, rest // times)
        return jnp.concatenate([values[:, i] for i in range(times)], -1).reshape(-1, rest)

    aligned = head_rows % 8 == 0 and piece % 16 == 0 and z_size <= 4
    if aligned:
        turned = call(
            functools.partial(turn_y_kernel, heads - 1, head_rows),
            (1,),
            [full(v) for v in (up_kept, up_got, head_grads[0], rest_z, down_kept, down_got)],
            [out((z_size, piece, wide + rest // times), BF)] * 2 + [out((x_size * piece, half), BF)] * z_size,
            [],
            width * units,
            4 * width * units,
            "turn_y",
            place,
        )
        y_sent, y_kept, down_own, down_sent = (turned[0], turned[1], turned[2], turned[3:])
    else:
        up_there, up_here = [
            [v.reshape(z_size, piece, 2 * width) for v in side]
            for side in zip(*[sides(v, 1 - y_index, 0) for v in (up_kept, up_got)])
        ]
        pair = head_grads[0].reshape(-1, y_size, z_size, head_rows, lanes)
        pair = jnp.transpose(pair, (1, 2, 0, 3, 4)).reshape(y_size, z_size, -1, lanes)
        pair_there, pair_here = [v[0] for v in sides(pair, 1 - y_index, 0)]
        rest_there, rest_here = sides(jnp.sum(rest_z.astype(F32), 0).astype(BF), 1 - y_index, 0)
        y_sent = jnp.concatenate([add_low(*up_there), pair_there, fold(rest_there)], -1)
        y_kept = jnp.concatenate([add_low(*up_here), pair_here, fold(rest_here)], -1)
        down_sum = add_low(down_kept, down_got).reshape(z_size, -1, half)
        down_sent = [down_sum]
    y_got = swap(y_sent, "batch", nb, 1)
    if aligned:
        down_got = [swap(v, "batch", nb, (m + 1) * y_size) for m, v in enumerate(down_sent)]
    else:
        down_z = jnp.sum(scatter(down_sum, "batch", z_groups).astype(F32), 0).astype(BF)
    back_pieces[0] = scatter(back_pieces[0], "seq")
    back(1, [y_sent, *down_sent])

    total = jnp.sum(jnp.concatenate(sums_heads, 0), 0).reshape(2, z_size, y_size, ns, 3 * head_rows)
    total = jnp.transpose(total, (2, 1, 4, 0, 3)).reshape(y_size, z_size, 3 * head_rows, 2 * ns)
    total = jnp.pad(total, ((0, 0), (0, 0), (0, 0), (width + 3, lanes - width - 3 - 2 * ns)))
    last = jnp.transpose(head_grads[1].reshape(3, y_size, z_size, head_rows, lanes), (1, 2, 0, 3, 4))
    last = last.reshape(y_size, z_size, -1, lanes)
    last_there, last_kept = [
        add_low(*pair)[0] for pair in zip(*[sides(v, 1 - y_index, 0) for v in (last, total)])
    ]
    last_got = swap(last_there, "batch", nb, 1)
    if aligned:
        turned = call(
            functools.partial(turn_z_kernel, rest),
            (1,),
            [full(v) for v in (y_kept, y_got, last_kept, last_got, down_own, *down_got)],
            [out((piece, half + rest), BF)] * 2 + [out((piece, wide + lanes // 2), BF)] * z_size,
            [],
            width * units,
            2 * width * units,
            "turn_z",
            place,
            [back_pieces[0]],
            False,
            [back_pieces[1]],
        )
        x_there, x_here, up_own = turned[:3]
        up_sent, back_pieces[1] = (turned[3:-1], turned[-1])
        up_terms = [up_own] + [swap(v, "batch", nb, (m + 1) * y_size) for m, v in enumerate(up_sent)]
    else:
        last_sum = add_low(last_kept, last_got)
        last_sum = jnp.concatenate([last_sum[..., : lanes // 2], last_sum[..., lanes // 2 :]], -2)
        up_sum = jnp.concatenate([add_low(y_kept[..., :wide], y_got[..., :wide]), last_sum], -1)
        up_sent = [up_sum]
        up_terms = [jnp.sum(scatter(up_sum, "batch", z_groups).astype(F32), 0)]
        rest_y = unfold(add_low(y_kept[..., wide:], y_got[..., wide:]))
        x_there, x_here = sides(jnp.concatenate([down_z, rest_y], -1), 1 - x_index, 0)
    x_got = swap(x_there, "seq", ns, cores)
    back_pieces[1] = scatter(back_pieces[1], "seq")

    d_tokens, token = call(
        functools.partial(final_kernel, heads, groups),
        (1,),
        [full(v) for v in (*back_pieces, w_q, w_k, w_v, tokens, gain_one, grad_middle)],
        [out((rows, width), BF)],
        [pltpu.VMEM((3, width, rows), BF)],
        6 * rows * width * width,
        8 * width * width,
        "final",
        place,
        up_sent,
        True,
    )
    up_z = add_all([*up_terms, token[0, 0]])
    single = jnp.concatenate(jnp.split(up_z[:, wide:], 2, 0), -1).reshape(3, head_rows, lanes)

    devices = [(d // ns, d % ns) for d in range(nb * ns)]
    everywhere = ("batch", "seq")

    pair = up_z[:, 2 * width : wide].astype(BF)
    granules = [*pair.reshape(-1, 3, head_rows, lanes), single.astype(BF)]
    norm_sums = single[:, :, width + 3 : width + 3 + 2 * ns].reshape(3 * head_rows, 2, ns)
    norm_sums = jnp.transpose(norm_sums, (2, 1, 0))
    take = lambda k: lax.dynamic_index_in_dim(norm_sums, s_index ^ k, 0, keepdims=False)
    sums_one = add_all([take(0)] + [swap(take(k), "seq", ns, k) for k in range(1, ns)])

    def position(b):
        return (b % y_size) * z_size + b // y_size

    pieces = []
    for slot in range(heads):
        perm = []
        for d, (b, s) in enumerate(devices):
            for h in range(heads):
                granule = (s * heads + h) * nb + position(b)
                if granule % heads == slot:
                    perm.append((d, granule // heads))
        ours = [(h * nb + position(b_index)) % heads == slot for h in range(heads)]
        sent = granules[-1]
        for h in range(heads - 1):
            sent = jnp.where(ours[h], granules[h], sent)
        pieces.append(lax.ppermute(sent, everywhere, perm))
    grad_qkv = jnp.concatenate(pieces, 1).astype(F32)

    size = piece
    up_value = up_z.astype(BF)
    chip = lambda b, s: ((s // cores) * y_size + b % y_size) * z_size + b // y_size
    got_up = []
    for color in range(2):
        perm = []
        for d, (b, s) in enumerate(devices):
            p = (color + chip(b, s)) % 2
            begin = (s % cores) * half + p * (half // 2) + chip(b, s) * size
            perm.append((d, begin // (2 * size)))
        first = (color + chip(b_index, s_index)) % 2 == 0
        got_up.append(lax.ppermute(jnp.where(first, up_value[:, :width], up_value[:, width : 2 * width]), everywhere, perm))
    first = (b_index * ns + s_index) * 2 * size % half < half // 2
    got_up = [jnp.where(first, got_up[0], got_up[1]), jnp.where(first, got_up[1], got_up[0])]
    got_up = jnp.concatenate(got_up, 0).astype(F32)

    value = add_low(x_here, x_got)
    size = value.shape[0] // cores
    here = lax.dynamic_slice_in_dim(value, core * size, size, 0)
    there = to_core(lax.dynamic_slice_in_dim(value, (1 - core) * size, size, 0))
    by_core = [jnp.where(core == 0, here, there).astype(F32), jnp.where(core == 0, there, here).astype(F32)]
    got_down = jnp.concatenate([v[:, :half] for v in by_core], 1)
    got_rest = jnp.concatenate([v[:, half : half + half_width] for v in by_core], 1)
    sums_two = here[:, half + half_width : half + half_width + 2].astype(F32)

    flat = jnp.swapaxes(grad_qkv[:, :, :width], 1, 2)
    return (
        mixed,
        d_tokens,
        flat[0],
        flat[1],
        flat[2],
        jnp.swapaxes(grad_qkv[:, :, width : width + 3], 1, 2),
        got_rest.T,
        sums_one[0],
        sums_one[1],
        sums_two[:, 0],
        sums_two[:, 1],
        got_up.T,
        got_down.T,
    )


def solution(mesh):
    split = ("batch", "seq")
    in_specs = (P(split, None), P(split), P(split, None)) + (P(),) * 11
    out_specs = (
        P(split, None),
        P(split, None),
        P(None, split),
        P(None, split),
        P(None, split),
        P(None, None, split),
        P(None, split),
        P(split),
        P(split),
        P(split),
        P(split),
        P(None, split),
        P(None, split),
    )
    return jax.shard_map(local, mesh=mesh, in_specs=in_specs, out_specs=out_specs, check_vma=False)
```

```python
import functools
import math

import jax
import jax.numpy as jnp
from jax import lax
from jax.experimental import pallas as pl
from jax.experimental.pallas import tpu as pltpu
from jax.sharding import PartitionSpec as P

HEAD_DIM = 64
EPS = 1e-05
NEG_FILL = -1e30
LONG = 512
ID_ROWS = 16
COST = 1
LOG2E = math.log2(math.e)
BF = jnp.bfloat16
F32 = jnp.float32
VMEM_LIMIT = 60 * 1024 * 1024


def nn(first, second):
    return lax.dot_general(first, second, (((1,), (0,)), ((), ())), preferred_element_type=F32)


def nt(first, second):
    return lax.dot_general(first, second, (((1,), (1,)), ((), ())), preferred_element_type=F32)


def tn(first, second):
    return lax.dot_general(first, second, (((0,), (0,)), ((), ())), preferred_element_type=F32)


def norm_stats(values):
    centred = values - jnp.mean(values, axis=-1, keepdims=True)
    variance = jnp.mean(centred * centred, axis=-1, keepdims=True)
    inv_scale = lax.rsqrt(variance + EPS)
    return (centred * inv_scale, inv_scale)


def norm_back(grad_out, normed, inv_scale, gain):
    grad_norm = grad_out * gain
    projected = (
        grad_norm
        - jnp.mean(grad_norm, -1, keepdims=True)
        - normed * jnp.mean(grad_norm * normed, -1, keepdims=True)
    )
    return (projected * inv_scale, jnp.sum(grad_out * normed, 0, keepdims=True), jnp.sum(grad_out, 0, keepdims=True))


def lag_mask(starts, positions, lag):
    return positions - lag >= starts


def project_rows(tok, gain, bias, flipped):
    normed, _ = norm_stats(tok.astype(F32))
    low = (normed * gain + bias).astype(BF)
    return (low, nn(flipped, jnp.transpose(low)).astype(BF))


def near_kernel(heads, cut, place, own, other, gain, bias, w_q, w_k, w_v, cotangent, flipped, columns, normed, raw):
    rows = normed.shape[0]

    @pl.when(pl.program_id(0) == 0)
    def _():
        for h in range(heads):
            for part, weights in enumerate((w_q, w_k, w_v)):
                row = (h * 3 + part) * HEAD_DIM
                flipped[row : row + HEAD_DIM, :] = jnp.transpose(weights[:, h * HEAD_DIM : (h + 1) * HEAD_DIM])
        normed[...], raw[...] = project_rows(own[...], gain[...], bias[...], flipped[...])

    @pl.when(pl.program_id(0) == 1)
    def _():
        normed[...], raw[...] = project_rows(other[...], gain[...], bias[...], flipped[...])
        flip = jnp.transpose(cotangent[...])
        half = cut // 2
        for i in range(flip.shape[0] // cut):
            for side in range(2):
                to = side * (flip.shape[0] // 2) + i * half
                columns[to : to + half, :] = flip[i * cut + side * half : i * cut + (side + 1) * half]


def far_kernel(ns, place, *refs):
    codes, toks = (refs[:ns], refs[ns : 2 * ns - 2])
    gain, bias, flipped, normed, raw, starts = refs[2 * ns - 2 :]
    rows = normed.shape[0]

    @pl.when(pl.program_id(0) == 0)
    def _():
        for k in range(ns):
            begin = pl.multiple_of((place[0] ^ k) * rows, rows)
            code = codes[k][:, :rows].astype(F32)
            starts[:, pl.ds(begin, rows)] = (code[0:1, :] * 256.0 + code[1:2, :]).astype(jnp.int32)

    for k, tok in enumerate(toks):
        @pl.when(pl.program_id(0) == k)
        def _():
            normed[...], raw[...] = project_rows(tok[...], gain[...], bias[...], flipped[...])


def conv_rows(raw, taps, starts, conv):
    positions = lax.broadcasted_iota(jnp.int32, starts.shape, 1)
    step = HEAD_DIM
    for r in range(0, raw.shape[0], step):
        values = raw[r : r + step, :].astype(F32)
        result = taps[r : r + step, 0:1] * values
        for lag in (1, 2):
            moved = jnp.where(lag_mask(starts, positions, lag), pltpu.roll(values, lag, 1), 0.0)
            result = result + taps[r : r + step, lag : lag + 1] * moved
        conv[r : r + step, :] = result.astype(BF)


def masked_scores(scores, starts, key_begin, query_begin, length):
    keys, queries = scores.shape
    diagonal = key_begin + keys > query_begin
    inside = key_begin >= LONG and query_begin + queries <= length - LONG
    if inside and not diagonal:
        return scores
    key_pos = key_begin + lax.broadcasted_iota(jnp.int32, scores.shape, 0)
    allowed = None
    if not inside:
        allowed = key_pos >= starts
    if diagonal:
        query_pos = query_begin + lax.broadcasted_iota(jnp.int32, scores.shape, 1)
        causal = key_pos <= query_pos
        allowed = causal if allowed is None else allowed & causal
    return jnp.where(allowed, scores, NEG_FILL)


def attend_kernel(ns, block, step, place, starts_ref, raw, taps, *refs):
    pieces, (out_full, lse_out, qkv) = (refs[:ns], refs[ns:])
    conv_rows(raw, taps, starts_ref[...], qkv)
    length = qkv.shape[1]
    rows = length // ns
    keys = jnp.transpose(qkv[HEAD_DIM : 2 * HEAD_DIM, :])
    factor = LOG2E * HEAD_DIM ** (-0.5)
    for q in range(0, length, block):
        queries = qkv[0:HEAD_DIM, q : q + block]
        starts = starts_ref[:, q : q + block]
        scores = [
            masked_scores(nn(keys[u : u + step], queries), starts, u, q, length) * factor
            for u in range(0, q + block, step)
        ]
        top = scores[0]
        for one in scores[1:]:
            top = jnp.maximum(top, one)
        top = jnp.max(top, 0, keepdims=True)
        total = jnp.zeros((8, block), F32)
        result = jnp.zeros((HEAD_DIM, block), F32)
        for index, one in enumerate(scores):
            prob = jnp.exp2(one - top)
            total = total + jnp.sum(prob.reshape(step // 8, 8, block), 0)
            values = qkv[2 * HEAD_DIM :, index * step : (index + 1) * step]
            result = result + nn(values, prob.astype(BF))
        total = jnp.sum(total, 0, keepdims=True)
        lse_out[0, :, q : q + block] = top + jnp.log2(total)
        out_full[:, q : q + block] = result / total
    for k in range(ns):
        begin = pl.multiple_of((place[0] ^ k) * rows, rows)
        pieces[k][...] = out_full[:, pl.ds(begin, rows)].astype(BF)


def attend_back_kernel(ns, block, step, place, starts_ref, conv, raw, taps, flipped, gain, bias, normed, out_full, lse, *refs):
    grads_in, grads_out, grad_w, norm_sums, grad_attn, grad_conv, grad_raw = refs
    length = conv.shape[1]
    rows = length // ns
    head_scale = HEAD_DIM ** (-0.5)
    factor = LOG2E * head_scale
    for k in range(ns):
        grad_attn[:, k * rows : (k + 1) * rows] = grads_in[k]
    delta = jnp.sum(grad_attn[...].astype(F32) * out_full[...], 0, keepdims=True)
    keys = jnp.transpose(conv[HEAD_DIM : 2 * HEAD_DIM, :])
    values = jnp.transpose(conv[2 * HEAD_DIM :, :])
    grad_conv[HEAD_DIM:, :] = jnp.zeros((2 * HEAD_DIM, length), F32)
    for q in range(0, length, block):
        queries = conv[0:HEAD_DIM, q : q + block]
        grad_block = grad_attn[:, q : q + block]
        starts = starts_ref[:, q : q + block]
        grad_query = jnp.zeros((HEAD_DIM, block), F32)
        for u in range(0, q + block, step):
            scores = masked_scores(nn(keys[u : u + step], queries), starts, u, q, length)
            prob = jnp.exp2(scores * factor - lse[0, :, q : q + block])
            grad_prob = nn(values[u : u + step], grad_block)
            grad_scores = (prob * (grad_prob - delta[:, q : q + block])).astype(BF)
            grad_query = grad_query + nn(conv[HEAD_DIM : 2 * HEAD_DIM, u : u + step], grad_scores)
            grad_conv[HEAD_DIM : 2 * HEAD_DIM, u : u + step] += nt(queries, grad_scores)
            grad_conv[2 * HEAD_DIM :, u : u + step] += nt(grad_block, prob.astype(BF))
        grad_conv[0:HEAD_DIM, q : q + block] = grad_query
    starts = starts_ref[...]
    positions = lax.broadcasted_iota(jnp.int32, starts.shape, 1)
    tap_columns = []
    for part in range(3):
        at = slice(part * HEAD_DIM, (part + 1) * HEAD_DIM)
        grad = grad_conv[at, :] * (head_scale if part < 2 else 1.0)
        inputs = raw[at, :].astype(F32)
        result = taps[at, 0:1] * grad
        sums = [jnp.sum(grad * inputs, 1, keepdims=True)]
        for lag in (1, 2):
            kept = jnp.where(lag_mask(starts, positions, lag), grad, 0.0)
            result = result + taps[at, lag : lag + 1] * pltpu.roll(kept, length - lag, 1)
            sums.append(jnp.sum(kept * pltpu.roll(inputs, lag, 1), 1, keepdims=True))
        grad_raw[at, :] = result.astype(BF)
        lane = lax.broadcasted_iota(jnp.int32, (HEAD_DIM, grad_w.shape[1] - normed.shape[1]), 1)
        tap_columns.append(
            jnp.where(lane == 0, sums[0], jnp.where(lane == 1, sums[1], jnp.where(lane == 2, sums[2], 0.0)))
        )
    width = normed.shape[1]
    grads = nn(grad_raw[...], normed[...])
    grad_w[:, :width] = grads.astype(BF)
    weights = flipped[...].astype(F32)
    column = jnp.sum(grad_raw[...].astype(F32), 1, keepdims=True)
    norm_sums[0, 0:1, :] = jnp.sum(weights * (grads - bias[...] * column), 0, keepdims=True) / gain[...]
    norm_sums[0, 1:2, :] = jnp.sum(weights * column, 0, keepdims=True)
    for part in range(3):
        grad_w[part * HEAD_DIM : (part + 1) * HEAD_DIM, width:] = tap_columns[part].astype(BF)
    for k in range(ns):
        grads_out[k] = grad_raw[:, k * rows : (k + 1) * rows]


def middle_kernel(ns, place, *refs):
    pieces = refs[:ns]
    tokens, w_o, cotangent, gain, bias, w_up, w_down = refs[ns : ns + 7]
    mixed, grad_middle, grad_low, sent, kept, normed_low, sums, grad_attn, attn = refs[ns + 7 : ns + 16]
    middle, normed_two, grad_normed, scale = refs[ns + 16 :]
    step = pl.program_id(0)
    steps = pl.num_programs(0)

    @pl.when(step == 0)
    def _():
        for k in range(ns):
            part = pieces[k].shape[0]
            attn[pl.ds(pl.multiple_of((place[0] ^ k) * part, part), part), :] = pieces[k][...]
        value = tokens[...].astype(F32) + tn(attn[...], w_o[...])
        normed, inv_scale = norm_stats(value)
        middle[...] = value
        normed_two[...] = normed
        scale[...] = jnp.broadcast_to(inv_scale, scale.shape)
        normed_low[...] = (normed * gain[...] + bias[...]).astype(BF)
        grad_normed[...] = jnp.zeros_like(grad_normed)

    positive = jnp.maximum(nn(normed_low[...], w_up[...]), 0.0)
    hidden = (positive * positive).astype(BF)
    grad_pre = (nt(cotangent[...], w_down[...]) * (2.0 * positive)).astype(BF)

    @pl.when(step < steps // 2)
    def _():
        sent[0] = hidden
        sent[1] = grad_pre

    @pl.when(step >= steps // 2)
    def _():
        kept[0] = hidden
        kept[1] = grad_pre

    middle[...] += nn(hidden, w_down[...])
    grad_normed[...] += nt(grad_pre, w_up[...])

    @pl.when(step == steps - 1)
    def _():
        mixed[...] = middle[...].astype(BF)
        back, grad_gain, grad_bias = norm_back(grad_normed[...], normed_two[...], scale[:, 0:1], gain[...])
        total = cotangent[...].astype(F32) + back
        grad_middle[...] = total
        low = total.astype(BF)
        grad_low[...] = low
        row = lax.broadcasted_iota(jnp.int32, sums.shape, 0)
        sums[...] = jnp.where(row == 0, grad_gain, jnp.where(row == 1, grad_bias, 0.0))
        grad_attn[...] = nt(w_o[...], low).astype(BF)


def grad_units(pre_low, pre_high, normed):
    both = jnp.concatenate([jnp.transpose(pre_low[0]), jnp.transpose(pre_high[0])], 0)
    grads = nn(both, normed[...])
    rows = grads.shape[0] // 2
    return jnp.concatenate([grads[:rows], grads[rows:]], 1)


def rest_kernel(place, grad_low, attn_sent, attn_kept, sums, sent, kept):
    columns = jnp.transpose(grad_low[...])
    width = columns.shape[0]
    filled = jnp.transpose(jnp.concatenate([sums[...], jnp.zeros((128 - sums.shape[0], width), F32)], 0)).astype(BF)
    for attn, rest in ((attn_sent, sent), (attn_kept, kept)):
        half = attn.shape[0]
        rest[:, :half] = nt(columns, attn[...]).astype(BF)
        rest[:, half:] = filled


def weight_kernel(phase, place, *refs):
    g_own, g_got, hidden_own, hidden_got, low_own, low_got, high_own, high_got, n_own, n_got = refs[:10]
    grad_down, grad_up = refs[10 + 2 * phase : 12 + 2 * phase]

    if phase == 1:
        @pl.when(pl.program_id(0) == 0)
        def _():
            refs[14][...] = (refs[10][...].astype(F32) + refs[11][...].astype(F32)).astype(BF)

    grad_down[...] = (nn(g_own[...], hidden_own[0]) + nn(g_got[...], hidden_got[0])).astype(BF)
    pre_own = jnp.concatenate([jnp.transpose(low_own[0]), jnp.transpose(high_own[0])], 0)
    pre_got = jnp.concatenate([jnp.transpose(low_got[0]), jnp.transpose(high_got[0])], 0)
    grads = (nn(pre_own, n_own[...]) + nn(pre_got, n_got[...])).astype(BF)
    rows, width = (grads.shape[0] // 2, grads.shape[1])
    grad_up[:, :width] = grads[:rows]
    grad_up[:, width:] = grads[rows:]


def sum_refs(refs, index):
    total = refs[0][index].astype(F32)
    for ref in refs[1:]:
        total = total + ref[index].astype(F32)
    return total


def turn_y_kernel(heads, head_rows, place, up_kept, up_got, pair, rest_z, down_kept, down_got, y_sent, y_kept, *downs):
    y, z = (place[3], place[4])
    z_size, piece, _ = y_sent.shape
    wide, lanes = (up_kept.shape[1], pair.shape[1])
    rest = rest_z.shape[2]
    x_size = rest_z.shape[1] // (2 * piece)
    times = z_size // x_size
    cut = rest // times
    parts = heads * 3
    for side, result in ((1 - y, y_sent), (y, y_kept)):
        block = z_size * piece
        at = pl.ds(pl.multiple_of(side * block, block), block)
        result[:, :, :wide] = sum_refs((up_kept, up_got), (at, slice(None))).astype(BF).reshape(z_size, piece, wide)
        run = z_size * head_rows
        taken = [
            pair[pl.ds(pl.multiple_of(p * HEAD_DIM + side * run, run), run), :].astype(F32) for p in range(parts)
        ]
        for i in range(z_size):
            rows = jnp.concatenate([v[i * head_rows : (i + 1) * head_rows] for v in taken], 0)
            result[i, :, wide : wide + lanes] = rows.astype(BF)
        for x in range(x_size):
            at = pl.ds(pl.multiple_of((side * x_size + x) * piece, piece), piece)
            total = rest_z[0, at, :].astype(F32)
            for i in range(1, rest_z.shape[0]):
                total = total + rest_z[i, at, :].astype(F32)
            for i in range(times):
                result[x * times + i, :, wide + lanes :] = total[:, i * cut : (i + 1) * cut].astype(BF)
    block = downs[0].shape[0]
    for m, result in enumerate(downs):
        at = pl.ds(pl.multiple_of((z ^ m) * block, block), block)
        result[...] = sum_refs((down_kept, down_got), (at, slice(None))).astype(BF)


def turn_z_kernel(rest, place, *refs):
    y_kept, y_got, last_kept, last_got, own, one, two, three, sent, kept = refs[:10]
    ups = refs[10:]
    x, z = (place[2], place[4])
    last_lanes = last_kept.shape[2]
    wide = ups[0].shape[1] - last_lanes // 2
    z_size, piece, lanes = y_kept.shape
    last_rows = last_kept.shape[1]
    for m, result in enumerate(ups):
        result[:, :wide] = sum_refs((y_kept, y_got), (z ^ m, slice(None), slice(0, wide))).astype(BF)
        last = sum_refs((last_kept, last_got), z ^ m)
        last = jnp.concatenate([last[:, : last_lanes // 2], last[:, last_lanes // 2 :]], 0)
        result[:, wide:] = last.astype(BF)
    cut = lanes - wide
    times = rest // cut
    half = own.shape[1]
    for side, result in ((1 - x, sent), (x, kept)):
        at = pl.ds(pl.multiple_of(side * piece, piece), piece)
        result[:, :half] = sum_refs((own, one, two, three), (at, slice(None))).astype(BF)
        for i in range(times):
            both = sum_refs((y_kept, y_got), (side * times + i, slice(None), slice(wide, lanes)))
            result[:, half + i * cut : half + (i + 1) * cut] = both.astype(BF)


def final_kernel(heads, groups, place, *refs):
    pieces, weights, (tokens, gain, grad_middle, d_tokens, stacked) = (refs[: len(groups)], refs[len(groups) : -5], refs[-5:])
    for (first, size), piece in zip(groups, pieces):
        for k in range(piece.shape[0]):
            for h in range(size):
                begin = (k * heads + first + h) * HEAD_DIM
                for part in range(3):
                    row = (h * 3 + part) * HEAD_DIM
                    stacked[part, begin : begin + HEAD_DIM, :] = piece[k, row : row + HEAD_DIM, :]
    grad_normed = nt(jnp.transpose(stacked[0]), weights[0][...])
    for part in (1, 2):
        grad_normed = grad_normed + nt(jnp.transpose(stacked[part]), weights[part][...])
    normed, inv_scale = norm_stats(tokens[...].astype(F32))
    back, _, _ = norm_back(grad_normed, normed, inv_scale, gain[...])
    d_tokens[...] = (grad_middle[...] + back).astype(BF)


def whole(shape):
    return pl.BlockSpec(shape, lambda *_: (0,) * len(shape))


def shaped(shape, dtype):
    return jax.ShapeDtypeStruct(shape, dtype)


def call(kernel, grid, inputs, outputs, scratch, flops, moved, name, place, ties=(), token=False, through=(), onto=()):
    count = len(inputs)
    held = len(ties) + len(through) + len(onto)
    end = count + held + len(outputs)

    def body(place, *refs):
        kernel(place, *refs[:count], *refs[count + held : end], *refs[end + token + len(through) :])
        if token:
            refs[end][...] = jnp.zeros_like(refs[end])

    aliases = {}
    for i, (_, result) in enumerate(onto):
        aliases[1 + count + len(ties) + len(through) + i] = result
    if token:
        outputs = [*outputs, out((8, 128), F32)]
    for array in through:
        aliases[1 + count + len(ties) + len(aliases) - len(onto)] = len(outputs)
        outputs = [*outputs, (array.shape, array.dtype, pl.BlockSpec(memory_space=pl.ANY))]

    return pl.pallas_call(
        body,
        grid_spec=pltpu.PrefetchScalarGridSpec(
            num_scalar_prefetch=1,
            grid=grid,
            in_specs=[spec for _, spec in inputs] + [pl.BlockSpec(memory_space=pl.ANY)] * held,
            out_specs=[spec for _, _, spec in outputs],
            scratch_shapes=scratch,
        ),
        out_shape=[jax.ShapeDtypeStruct(shape, dtype) for shape, dtype, _ in outputs],
        compiler_params=pltpu.CompilerParams(vmem_limit_bytes=VMEM_LIMIT),
        cost_estimate=pl.CostEstimate(flops=flops // COST, bytes_accessed=moved // COST, transcendentals=0),
        name=name,
        input_output_aliases=aliases,
    )(place, *[array for array, _ in inputs], *ties, *through, *[array for array, _ in onto])


def full(array):
    return (array, whole(array.shape))


def out(shape, dtype):
    return (shape, dtype, whole(shape))


def swap(values, axis, count, mask):
    return lax.ppermute(values, axis, [(i, i ^ mask) for i in range(count)])


def add_all(terms):
    total = terms[0].astype(F32)
    for one in terms[1:]:
        total = total + jnp.asarray(one, F32)
    return total


def after(values, ties, place):
    anywhere = pl.BlockSpec(memory_space=pl.ANY)
    return pl.pallas_call(
        lambda *refs: None,
        in_specs=[pl.BlockSpec(memory_space=pltpu.SMEM)] + [anywhere] * (1 + len(ties)),
        out_specs=anywhere,
        out_shape=jax.ShapeDtypeStruct(values.shape, values.dtype),
        input_output_aliases={1: 0},
        name="after",
    )(place, values, *ties)


def add_low(*terms):
    return add_all(terms).astype(BF)


def sides(values, index, dim):
    block = values.shape[dim] // 2
    return [lax.dynamic_slice_in_dim(values, i * block, block, dim) for i in (index, 1 - index)]


def scatter(values, axis, groups=None):
    return lax.all_to_all(values, axis, split_axis=0, concat_axis=0, tiled=True, axis_index_groups=groups)


def zero_of(values):
    return jnp.minimum(jnp.abs(values[(0,) * values.ndim].astype(F32)), 0.0)


def local(tokens, segment_ids, cotangent, w_q, w_k, w_v, conv_weight, w_o, gain_one, bias_one, gain_two, bias_two, w_up, w_down):
    ns, nb = (lax.axis_size("seq"), lax.axis_size("batch"))
    s_index, b_index = (lax.axis_index("seq"), lax.axis_index("batch"))
    cores, y_size = (2, 2)
    x_size, z_size = (ns // cores, nb // y_size)
    rows, width = tokens.shape
    units = w_up.shape[1]
    heads = width // HEAD_DIM // ns
    length = rows * ns
    part = 3 * HEAD_DIM
    mine = heads * HEAD_DIM
    core = s_index % cores
    place = jnp.stack([s_index, core, s_index // cores, b_index % y_size, b_index // y_size]).astype(jnp.int32)
    gain_one, bias_one, gain_two, bias_two = (v.reshape(1, width) for v in (gain_one, bias_one, gain_two, bias_two))
    groups = [(0, heads - 1), (heads - 1, 1)]

    def to_core(values):
        return swap(values, "seq", ns, 1)

    toks = [tokens] + [None] * (ns - 1)
    for k in range(2, ns, 2):
        toks[k] = swap(tokens, "seq", ns, k)
    toks[1] = to_core(tokens)
    codes = jnp.stack([segment_ids // 256, segment_ids % 256]).astype(BF)
    codes = [jnp.pad(codes, ((0, ID_ROWS - 2), (0, width - rows)))] + [None] * (ns - 1)
    for k in range(2, ns, 2):
        codes[k] = swap(codes[0], "seq", ns, k)
    for k in range(1, ns, 2):
        codes[k] = to_core(codes[k - 1])
    columns, cut = (cotangent, width // z_size)
    if cut // 2 % 16:
        columns = columns.reshape(rows, z_size, y_size, width // nb)
        columns, cut = (jnp.transpose(columns, (0, 2, 1, 3)).reshape(rows, width), width)
    own = [lax.dynamic_slice_in_dim(w, s_index * mine, mine, 1) for w in (w_q, w_k, w_v)]
    taps = jnp.transpose(
        lax.dynamic_slice_in_dim(conv_weight, s_index * mine, mine, 2).reshape(3, 3, heads, HEAD_DIM), (2, 0, 3, 1)
    ).reshape(heads * part, 3)

    normed_shape, raw_shape = ((length, width), (heads * part, length))

    def sequence_out(first):
        return [
            (normed_shape, BF, pl.BlockSpec((rows, width), lambda i, place: (place[0] ^ (first + i), 0))),
            (raw_shape, BF, pl.BlockSpec((heads * part, rows), lambda i, place: (0, place[0] ^ (first + i)))),
        ]

    flipped, columns_own, normed_in, raw = call(
        functools.partial(near_kernel, heads, cut),
        (2,),
        [full(v) for v in (tokens, toks[1], gain_one, bias_one, *own, columns)],
        [out((heads * part, width), BF), out((width, rows), BF)] + sequence_out(0),
        [],
        4 * rows * width * heads * part,
        8 * rows * width,
        "near",
        place,
        [taps],
    )
    columns_other = to_core(columns_own)
    for k in range(2, ns, 2):
        toks[k] = after(toks[k], [columns_own, codes[k]], place)
        toks[k + 1] = to_core(toks[k])
    normed_in, raw, starts = call(
        functools.partial(far_kernel, ns),
        (ns - 2,),
        [full(v) for v in (*codes, *toks[2:], gain_one, bias_one, flipped)],
        sequence_out(2) + [out((1, length), jnp.int32)],
        [],
        4 * rows * width * heads * part,
        8 * length * width,
        "far",
        place,
        onto=[(normed_in, 0), (raw, 1)],
    )

    fore, hind = ((512, 512), (512, 512))

    def by_head(array, first, columns):
        return (array, pl.BlockSpec((array.shape[0] // heads, columns), lambda i, place: (first + i, 0)))

    def per_head(size, height, columns, dtype):
        return ((size * height, columns), dtype, pl.BlockSpec((height, columns), lambda i, place: (i, 0)))

    for first, size in [(0, heads)]:
        results = call(
            functools.partial(attend_kernel, ns, *fore),
            (size,),
            [full(starts), by_head(raw, first, length), by_head(taps, first, 3)],
            [per_head(size, HEAD_DIM, rows, BF)] * ns
            + [
                per_head(size, HEAD_DIM, length, F32),
                ((size, 1, length), F32, pl.BlockSpec((1, 1, length), lambda i, place: (i, 0, 0))),
                per_head(size, part, length, BF),
            ],
            [],
            2 * length * length * HEAD_DIM * 4 * size,
            part * length * 4,
            "attend",
            place,
            [columns_other],
        )
        attn_pieces = [results[0]] + [swap(results[k], "seq", ns, k) for k in range(1, ns)]
        out_full, lse, conv = results[ns:]

    chunk = 512
    half = units // 2
    steps = half // chunk

    def unit_block(i, place):
        return jnp.where(i < steps, 1 - place[1], place[1]) * steps + lax.rem(i, steps)

    pair = (2, rows, half)
    results = call(
        functools.partial(middle_kernel, ns),
        (2 * steps,),
        [full(v) for v in (*attn_pieces, tokens, w_o, cotangent, gain_two, bias_two)]
        + [
            (w_up, pl.BlockSpec((width, chunk), lambda i, place: (0, unit_block(i, place)))),
            (w_down, pl.BlockSpec((chunk, width), lambda i, place: (unit_block(i, place), 0))),
        ],
        [
            out((rows, width), BF),
            out((rows, width), F32),
            out((rows, width), BF),
            (pair, BF, pl.BlockSpec((2, rows, chunk), lambda i, place: (0, 0, jnp.minimum(i, steps - 1)))),
            (pair, BF, pl.BlockSpec((2, rows, chunk), lambda i, place: (0, 0, jnp.maximum(i - steps, 0)))),
            out((rows, width), BF),
            out((8, width), F32),
            out((width, rows), BF),
            out((width, rows), BF),
        ],
        [pltpu.VMEM((rows, width), F32)] * 3 + [pltpu.VMEM((rows, 128), F32)],
        8 * rows * width * units + 4 * rows * width * width,
        4 * width * units,
        "middle",
        place,
    )
    mixed, grad_middle, grad_low, sent, kept, normed_mid, sums_two, grad_attn, attn = results
    grad_attn = scatter(grad_attn.reshape(ns, mine, rows), "seq")
    normed_other = to_core(normed_mid)
    got = to_core(sent)

    half_width = width // 2
    piece = 128
    steps = half // 4 // piece
    chunk = half // steps
    lanes = width + 128

    rest = half_width + 128
    rest_sent, rest_kept = call(
        rest_kernel,
        (1,),
        [
            full(grad_low),
            (attn, pl.BlockSpec((half_width, rows), lambda i, place: (1 - place[1], 0))),
            (attn, pl.BlockSpec((half_width, rows), lambda i, place: (place[1], 0))),
            full(sums_two),
        ],
        [out((width, rest), BF), out((width, rest), BF)],
        [],
        2 * rows * width * width,
        4 * width * width,
        "rest",
        place,
    )
    rest_got = to_core(rest_sent)
    def weights(phase, rest_parts=(), ties=()):
        def x_half(place):
            return (1 - place[2] if phase == 0 else place[2]) * steps

        return call(
            functools.partial(weight_kernel, phase),
            (steps,),
            [
                (v, pl.BlockSpec((half_width, rows), lambda i, place: (1 - place[3] if phase == 0 else place[3], 0)))
                for v in (columns_own, columns_other)
            ]
            + [(v, pl.BlockSpec((1, rows, chunk), lambda i, place: (0, 0, i))) for v in (kept, got)]
            + [(v, pl.BlockSpec((1, rows, piece), lambda i, place: (1, 0, x_half(place) + i))) for v in (kept, got)]
            + [
                (v, pl.BlockSpec((1, rows, piece), lambda i, place: (1, 0, 2 * steps + x_half(place) + i)))
                for v in (kept, got)
            ]
            + [full(v) for v in (normed_mid, normed_other, *rest_parts)],
            [
                ((half_width, half), BF, pl.BlockSpec((half_width, chunk), lambda i, place: (0, i))),
                ((half // 4, 2 * width), BF, pl.BlockSpec((piece, 2 * width), lambda i, place: (i, 0))),
            ]
            + [out(v.shape, BF) for v in rest_parts[:1]],
            [],
            2 * rows * width * units,
            3 * width * units,
            "weights",
            place,
            ties,
        )

    chips = nb * x_size
    x_index, y_index = (s_index // cores, b_index % y_size)
    z_groups = [[z * y_size + y for z in range(z_size)] for y in range(y_size)]

    down_sent, up_sent = weights(0)
    up_got = swap(up_sent, "seq", ns, cores)
    down_got = swap(down_sent, "batch", nb, 1)
    down_kept, up_kept, rest_sum = weights(1, (rest_kept, rest_got), [grad_attn, up_sent])
    rest_z = scatter(rest_sum.reshape(z_size, width // z_size, rest), "batch", z_groups)

    head_rows = HEAD_DIM // nb

    back_pieces, head_grads, sums_heads = ([], [], [])

    def back(g, ties):
        first, size = groups[g]
        results = call(
            functools.partial(attend_back_kernel, ns, *hind),
            (size,),
            [
                full(starts),
                by_head(conv, first, length),
                by_head(raw, first, length),
                by_head(taps, first, 3),
                by_head(flipped, first, width),
                full(gain_one),
                full(bias_one),
                full(normed_in),
                by_head(out_full, first, length),
                (lse, pl.BlockSpec((1, 1, length), lambda i, place: (first + i, 0, 0))),
            ]
            + [(grad_attn, pl.BlockSpec((ns, HEAD_DIM, rows), lambda i, place: (0, first + i, 0)))],
            [
                ((ns, size * part, rows), BF, pl.BlockSpec((ns, part, rows), lambda i, place: (0, i, 0))),
                per_head(size, part, lanes, BF),
                ((size, 2, width), F32, pl.BlockSpec((1, 2, width), lambda i, place: (i, 0, 0))),
            ],
            [pltpu.VMEM((HEAD_DIM, length), BF), pltpu.VMEM((part, length), F32), pltpu.VMEM((part, length), BF)],
            2 * length * length * HEAD_DIM * 10 * size,
            length * width * 2,
            "attend_back",
            place,
            ties,
            True,
        )
        back_pieces.append(results[0])
        head_grads.append(results[1])
        sums_heads.append(results[2])
        return results[3]

    piece = half // 2 // chips
    token = back(0, [down_kept, up_kept, rest_sum])
    wide = 2 * width + lanes
    times = z_size // x_size

    def fold(values):
        return jnp.stack(jnp.split(values.reshape(x_size, -1, rest), times, -1), 1).reshape(z_size, -1, rest // times)

    def unfold(values):
        values = values.reshape(x_size, times, -1, rest // times)
        return jnp.concatenate([values[:, i] for i in range(times)], -1).reshape(-1, rest)

    aligned = head_rows % 8 == 0 and piece % 16 == 0 and z_size <= 4
    if aligned:
        turned = call(
            functools.partial(turn_y_kernel, heads - 1, head_rows),
            (1,),
            [full(v) for v in (up_kept, up_got, head_grads[0], rest_z, down_kept, down_got)],
            [out((z_size, piece, wide + rest // times), BF)] * 2 + [out((x_size * piece, half), BF)] * z_size,
            [],
            width * units,
            4 * width * units,
            "turn_y",
            place,
        )
        y_sent, y_kept, down_own, down_sent = (turned[0], turned[1], turned[2], turned[3:])
    else:
        up_there, up_here = [
            [v.reshape(z_size, piece, 2 * width) for v in side]
            for side in zip(*[sides(v, 1 - y_index, 0) for v in (up_kept, up_got)])
        ]
        pair = head_grads[0].reshape(-1, y_size, z_size, head_rows, lanes)
        pair = jnp.transpose(pair, (1, 2, 0, 3, 4)).reshape(y_size, z_size, -1, lanes)
        pair_there, pair_here = [v[0] for v in sides(pair, 1 - y_index, 0)]
        rest_there, rest_here = sides(jnp.sum(rest_z.astype(F32), 0).astype(BF), 1 - y_index, 0)
        y_sent = jnp.concatenate([add_low(*up_there), pair_there, fold(rest_there)], -1)
        y_kept = jnp.concatenate([add_low(*up_here), pair_here, fold(rest_here)], -1)
        down_sum = add_low(down_kept, down_got).reshape(z_size, -1, half)
        down_sent = [down_sum]
    y_got = swap(y_sent, "batch", nb, 1)
    if aligned:
        down_got = [swap(v, "batch", nb, (m + 1) * y_size) for m, v in enumerate(down_sent)]
    else:
        down_z = jnp.sum(scatter(down_sum, "batch", z_groups).astype(F32), 0).astype(BF)
    back_pieces[0] = scatter(back_pieces[0], "seq")
    back(1, [y_sent, *down_sent])

    total = jnp.sum(jnp.concatenate(sums_heads, 0), 0).reshape(2, z_size, y_size, ns, 3 * head_rows)
    total = jnp.transpose(total, (2, 1, 4, 0, 3)).reshape(y_size, z_size, 3 * head_rows, 2 * ns)
    last_lanes = width + 256
    total = jnp.pad(total, ((0, 0), (0, 0), (0, 0), (width + 3, last_lanes - width - 3 - 2 * ns)))
    last = jnp.transpose(head_grads[1].reshape(3, y_size, z_size, head_rows, lanes), (1, 2, 0, 3, 4))
    last = jnp.pad(last.reshape(y_size, z_size, -1, lanes), ((0, 0), (0, 0), (0, 0), (0, last_lanes - lanes)))
    last_there, last_kept = [
        add_low(*pair)[0] for pair in zip(*[sides(v, 1 - y_index, 0) for v in (last, total)])
    ]
    last_got = swap(last_there, "batch", nb, 1)
    if aligned:
        turned = call(
            functools.partial(turn_z_kernel, rest),
            (1,),
            [full(v) for v in (y_kept, y_got, last_kept, last_got, down_own, *down_got)],
            [out((piece, half + rest), BF)] * 2 + [out((piece, wide + last_lanes // 2), BF)] * z_size,
            [],
            width * units,
            2 * width * units,
            "turn_z",
            place,
            [back_pieces[0]],
            False,
            [back_pieces[1]],
        )
        x_there, x_here, up_own = turned[:3]
        up_sent, back_pieces[1] = (turned[3:-1], turned[-1])
        up_terms = [up_own] + [swap(v, "batch", nb, (m + 1) * y_size) for m, v in enumerate(up_sent)]
    else:
        last_sum = add_low(last_kept, last_got)
        last_sum = jnp.concatenate([last_sum[..., : last_lanes // 2], last_sum[..., last_lanes // 2 :]], -2)
        up_sum = jnp.concatenate([add_low(y_kept[..., :wide], y_got[..., :wide]), last_sum], -1)
        up_sent = [up_sum]
        up_terms = [jnp.sum(scatter(up_sum, "batch", z_groups).astype(F32), 0)]
        rest_y = unfold(add_low(y_kept[..., wide:], y_got[..., wide:]))
        x_there, x_here = sides(jnp.concatenate([down_z, rest_y], -1), 1 - x_index, 0)
    x_got = swap(x_there, "seq", ns, cores)
    back_pieces[1] = scatter(back_pieces[1], "seq")

    d_tokens, token = call(
        functools.partial(final_kernel, heads, groups),
        (1,),
        [full(v) for v in (*back_pieces, w_q, w_k, w_v, tokens, gain_one, grad_middle)],
        [out((rows, width), BF)],
        [pltpu.VMEM((3, width, rows), BF)],
        6 * rows * width * width,
        8 * width * width,
        "final",
        place,
        up_sent,
        True,
    )
    up_z = add_all([*up_terms, token[0, 0]])
    single = jnp.concatenate(jnp.split(up_z[:, wide:], 2, 0), -1)[:, :lanes].reshape(3, head_rows, lanes)

    devices = [(d // ns, d % ns) for d in range(nb * ns)]
    everywhere = ("batch", "seq")

    pair = up_z[:, 2 * width : wide].astype(BF)
    granules = [*pair.reshape(-1, 3, head_rows, lanes), single.astype(BF)]
    norm_sums = single[:, :, width + 3 : width + 3 + 2 * ns].reshape(3 * head_rows, 2, ns)
    norm_sums = jnp.transpose(norm_sums, (2, 1, 0))
    take = lambda k: lax.dynamic_index_in_dim(norm_sums, s_index ^ k, 0, keepdims=False)
    sums_one = add_all([take(0)] + [swap(take(k), "seq", ns, k) for k in range(1, ns)])

    def position(b):
        return (b % y_size) * z_size + b // y_size

    pieces = []
    for slot in range(heads):
        perm = []
        for d, (b, s) in enumerate(devices):
            for h in range(heads):
                granule = (s * heads + h) * nb + position(b)
                if granule % heads == slot:
                    perm.append((d, granule // heads))
        ours = [(h * nb + position(b_index)) % heads == slot for h in range(heads)]
        sent = granules[-1]
        for h in range(heads - 1):
            sent = jnp.where(ours[h], granules[h], sent)
        pieces.append(lax.ppermute(sent, everywhere, perm))
    grad_qkv = jnp.concatenate(pieces, 1).astype(F32)

    size = piece
    up_value = up_z.astype(BF)
    chip = lambda b, s: ((s // cores) * y_size + b % y_size) * z_size + b // y_size
    got_up = []
    for color in range(2):
        perm = []
        for d, (b, s) in enumerate(devices):
            p = (color + chip(b, s)) % 2
            begin = (s % cores) * half + p * (half // 2) + chip(b, s) * size
            perm.append((d, begin // (2 * size)))
        first = (color + chip(b_index, s_index)) % 2 == 0
        got_up.append(lax.ppermute(jnp.where(first, up_value[:, :width], up_value[:, width : 2 * width]), everywhere, perm))
    first = (b_index * ns + s_index) * 2 * size % half < half // 2
    got_up = [jnp.where(first, got_up[0], got_up[1]), jnp.where(first, got_up[1], got_up[0])]
    got_up = jnp.concatenate(got_up, 0).astype(F32)

    value = add_low(x_here, x_got)
    size = value.shape[0] // cores
    here = lax.dynamic_slice_in_dim(value, core * size, size, 0)
    there = to_core(lax.dynamic_slice_in_dim(value, (1 - core) * size, size, 0))
    by_core = [jnp.where(core == 0, here, there).astype(F32), jnp.where(core == 0, there, here).astype(F32)]
    got_down = jnp.concatenate([v[:, :half] for v in by_core], 1)
    got_rest = jnp.concatenate([v[:, half : half + half_width] for v in by_core], 1)
    sums_two = here[:, half + half_width : half + half_width + 2].astype(F32)

    flat = jnp.swapaxes(grad_qkv[:, :, :width], 1, 2)
    return (
        mixed,
        d_tokens,
        flat[0],
        flat[1],
        flat[2],
        jnp.swapaxes(grad_qkv[:, :, width : width + 3], 1, 2),
        got_rest.T,
        sums_one[0],
        sums_one[1],
        sums_two[:, 0],
        sums_two[:, 1],
        got_up.T,
        got_down.T,
    )


def solution(mesh):
    split = ("batch", "seq")
    in_specs = (P(split, None), P(split), P(split, None)) + (P(),) * 11
    out_specs = (
        P(split, None),
        P(split, None),
        P(None, split),
        P(None, split),
        P(None, split),
        P(None, None, split),
        P(None, split),
        P(split),
        P(split),
        P(split),
        P(split),
        P(None, split),
        P(None, split),
    )
    return jax.shard_map(local, mesh=mesh, in_specs=in_specs, out_specs=out_specs, check_vma=False)
```

```python
import functools
import math

import jax
import jax.numpy as jnp
from jax import lax
from jax.experimental import pallas as pl
from jax.experimental.pallas import tpu as pltpu
from jax.sharding import PartitionSpec as P

HEAD_DIM = 64
EPS = 1e-05
NEG_FILL = -1e30
LONG = 512
ID_ROWS = 16
COST = 1
LOG2E = math.log2(math.e)
BF = jnp.bfloat16
F32 = jnp.float32
VMEM_LIMIT = 60 * 1024 * 1024


def nn(first, second):
    return lax.dot_general(first, second, (((1,), (0,)), ((), ())), preferred_element_type=F32)


def nt(first, second):
    return lax.dot_general(first, second, (((1,), (1,)), ((), ())), preferred_element_type=F32)


def tn(first, second):
    return lax.dot_general(first, second, (((0,), (0,)), ((), ())), preferred_element_type=F32)


def norm_stats(values):
    centred = values - jnp.mean(values, axis=-1, keepdims=True)
    variance = jnp.mean(centred * centred, axis=-1, keepdims=True)
    inv_scale = lax.rsqrt(variance + EPS)
    return (centred * inv_scale, inv_scale)


def norm_back(grad_out, normed, inv_scale, gain):
    grad_norm = grad_out * gain
    projected = (
        grad_norm
        - jnp.mean(grad_norm, -1, keepdims=True)
        - normed * jnp.mean(grad_norm * normed, -1, keepdims=True)
    )
    return (projected * inv_scale, jnp.sum(grad_out * normed, 0, keepdims=True), jnp.sum(grad_out, 0, keepdims=True))


def lag_mask(starts, positions, lag):
    return positions - lag >= starts


def project_rows(tok, gain, bias, flipped):
    normed, _ = norm_stats(tok.astype(F32))
    low = (normed * gain + bias).astype(BF)
    return (low, nn(flipped, jnp.transpose(low)).astype(BF))


def near_kernel(heads, cut, place, own, other, gain, bias, w_q, w_k, w_v, cotangent, flipped, columns, normed, raw):
    rows = normed.shape[0]

    @pl.when(pl.program_id(0) == 0)
    def _():
        for h in range(heads):
            for part, weights in enumerate((w_q, w_k, w_v)):
                row = (h * 3 + part) * HEAD_DIM
                flipped[row : row + HEAD_DIM, :] = jnp.transpose(weights[:, h * HEAD_DIM : (h + 1) * HEAD_DIM])
        normed[...], raw[...] = project_rows(own[...], gain[...], bias[...], flipped[...])

    @pl.when(pl.program_id(0) == 1)
    def _():
        normed[...], raw[...] = project_rows(other[...], gain[...], bias[...], flipped[...])
        flip = jnp.transpose(cotangent[...])
        half = cut // 2
        for i in range(flip.shape[0] // cut):
            for side in range(2):
                to = side * (flip.shape[0] // 2) + i * half
                columns[to : to + half, :] = flip[i * cut + side * half : i * cut + (side + 1) * half]


def far_kernel(ns, place, *refs):
    codes, toks = (refs[:ns], refs[ns : 2 * ns - 2])
    gain, bias, flipped, normed, raw, starts = refs[2 * ns - 2 :]
    rows = normed.shape[0]

    @pl.when(pl.program_id(0) == 0)
    def _():
        for k in range(ns):
            begin = pl.multiple_of((place[0] ^ k) * rows, rows)
            code = codes[k][:, :rows].astype(F32)
            starts[:, pl.ds(begin, rows)] = (code[0:1, :] * 256.0 + code[1:2, :]).astype(jnp.int32)

    for k, tok in enumerate(toks):
        @pl.when(pl.program_id(0) == k)
        def _():
            normed[...], raw[...] = project_rows(tok[...], gain[...], bias[...], flipped[...])


def conv_rows(raw, taps, starts, conv):
    positions = lax.broadcasted_iota(jnp.int32, starts.shape, 1)
    step = HEAD_DIM
    for r in range(0, raw.shape[0], step):
        values = raw[r : r + step, :].astype(F32)
        result = taps[r : r + step, 0:1] * values
        for lag in (1, 2):
            moved = jnp.where(lag_mask(starts, positions, lag), pltpu.roll(values, lag, 1), 0.0)
            result = result + taps[r : r + step, lag : lag + 1] * moved
        conv[r : r + step, :] = result.astype(BF)


def masked_scores(scores, starts, key_begin, query_begin, length):
    keys, queries = scores.shape
    diagonal = key_begin + keys > query_begin
    inside = key_begin >= LONG and query_begin + queries <= length - LONG
    if inside and not diagonal:
        return scores
    key_pos = key_begin + lax.broadcasted_iota(jnp.int32, scores.shape, 0)
    allowed = None
    if not inside:
        allowed = key_pos >= starts
    if diagonal:
        query_pos = query_begin + lax.broadcasted_iota(jnp.int32, scores.shape, 1)
        causal = key_pos <= query_pos
        allowed = causal if allowed is None else allowed & causal
    return jnp.where(allowed, scores, NEG_FILL)


def attend_kernel(ns, block, step, place, starts_ref, raw, taps, *refs):
    pieces, (out_full, lse_out, qkv) = (refs[:ns], refs[ns:])
    conv_rows(raw, taps, starts_ref[...], qkv)
    length = qkv.shape[1]
    rows = length // ns
    keys = jnp.transpose(qkv[HEAD_DIM : 2 * HEAD_DIM, :])
    factor = LOG2E * HEAD_DIM ** (-0.5)
    half = block // 2
    for q in range(0, length, block):
        queries = qkv[0:HEAD_DIM, q : q + block]
        starts = starts_ref[:, q : q + block]
        spans = [(u, step) for u in range(0, q, step)] + [(q, half)]
        scores = [
            masked_scores(nn(keys[u : u + size], queries), starts, u, q, length) * factor for u, size in spans
        ]
        u = q + half
        corner = masked_scores(nn(keys[u : u + half], queries[:, half:]), starts[:, half:], u, u, length) * factor
        top = jnp.max(scores[-1], 0, keepdims=True)
        for one in scores[:-1]:
            top = jnp.maximum(top, jnp.max(one, 0, keepdims=True))
        top_late = jnp.maximum(top[:, half:], jnp.max(corner, 0, keepdims=True))
        top = jnp.concatenate([top[:, :half], top_late], 1)
        total = jnp.zeros((8, block), F32)
        result = jnp.zeros((HEAD_DIM, block), F32)
        for (v, size), one in zip(spans, scores):
            prob = jnp.exp2(one - top)
            total = total + jnp.sum(prob.reshape(size // 8, 8, block), 0)
            result = result + nn(qkv[2 * HEAD_DIM :, v : v + size], prob.astype(BF))
        prob = jnp.exp2(corner - top_late)
        late = total[:, half:] + jnp.sum(prob.reshape(half // 8, 8, half), 0)
        total = jnp.concatenate([total[:, :half], late], 1)
        late = result[:, half:] + nn(qkv[2 * HEAD_DIM :, u : u + half], prob.astype(BF))
        result = jnp.concatenate([result[:, :half], late], 1)
        total = jnp.sum(total, 0, keepdims=True)
        lse_out[0, :, q : q + block] = top + jnp.log2(total)
        out_full[:, q : q + block] = result / total
    for k in range(ns):
        begin = pl.multiple_of((place[0] ^ k) * rows, rows)
        pieces[k][...] = out_full[:, pl.ds(begin, rows)].astype(BF)


def attend_back_kernel(ns, block, step, place, starts_ref, conv, raw, taps, flipped, gain, bias, normed, out_full, lse, *refs):
    grads_in, grads_out, grad_w, norm_sums, grad_attn, grad_conv, grad_raw = refs
    length = conv.shape[1]
    rows = length // ns
    head_scale = HEAD_DIM ** (-0.5)
    factor = LOG2E * head_scale
    for k in range(ns):
        grad_attn[:, k * rows : (k + 1) * rows] = grads_in[k]
    delta = jnp.sum(grad_attn[...].astype(F32) * out_full[...], 0, keepdims=True)
    keys = jnp.transpose(conv[HEAD_DIM : 2 * HEAD_DIM, :])
    values = jnp.transpose(conv[2 * HEAD_DIM :, :])
    grad_conv[HEAD_DIM:, :] = jnp.zeros((2 * HEAD_DIM, length), F32)
    half = block // 2

    def one_span(q, count, spans):
        queries = conv[0:HEAD_DIM, q : q + count]
        grad_block = grad_attn[:, q : q + count]
        starts = starts_ref[:, q : q + count]
        grad_query = jnp.zeros((HEAD_DIM, count), F32)
        for u, size in spans:
            scores = masked_scores(nn(keys[u : u + size], queries), starts, u, q, length)
            prob = jnp.exp2(scores * factor - lse[0, :, q : q + count])
            grad_prob = nn(values[u : u + size], grad_block)
            grad_scores = (prob * (grad_prob - delta[:, q : q + count])).astype(BF)
            grad_query = grad_query + nn(conv[HEAD_DIM : 2 * HEAD_DIM, u : u + size], grad_scores)
            grad_conv[HEAD_DIM : 2 * HEAD_DIM, u : u + size] += nt(queries, grad_scores)
            grad_conv[2 * HEAD_DIM :, u : u + size] += nt(grad_block, prob.astype(BF))
        return grad_query

    for q in range(0, length, block):
        grad_conv[0:HEAD_DIM, q : q + block] = one_span(q, block, [(u, step) for u in range(0, q, step)] + [(q, half)])
        grad_conv[0:HEAD_DIM, q + half : q + block] += one_span(q + half, half, [(q + half, half)])
    starts = starts_ref[...]
    positions = lax.broadcasted_iota(jnp.int32, starts.shape, 1)
    tap_columns = []
    for part in range(3):
        at = slice(part * HEAD_DIM, (part + 1) * HEAD_DIM)
        grad = grad_conv[at, :] * (head_scale if part < 2 else 1.0)
        inputs = raw[at, :].astype(F32)
        result = taps[at, 0:1] * grad
        sums = [jnp.sum(grad * inputs, 1, keepdims=True)]
        for lag in (1, 2):
            kept = jnp.where(lag_mask(starts, positions, lag), grad, 0.0)
            result = result + taps[at, lag : lag + 1] * pltpu.roll(kept, length - lag, 1)
            sums.append(jnp.sum(kept * pltpu.roll(inputs, lag, 1), 1, keepdims=True))
        grad_raw[at, :] = result.astype(BF)
        lane = lax.broadcasted_iota(jnp.int32, (HEAD_DIM, grad_w.shape[1] - normed.shape[1]), 1)
        tap_columns.append(
            jnp.where(lane == 0, sums[0], jnp.where(lane == 1, sums[1], jnp.where(lane == 2, sums[2], 0.0)))
        )
    width = normed.shape[1]
    grads = nn(grad_raw[...], normed[...])
    grad_w[:, :width] = grads.astype(BF)
    weights = flipped[...].astype(F32)
    column = jnp.sum(grad_raw[...].astype(F32), 1, keepdims=True)
    norm_sums[0, 0:1, :] = jnp.sum(weights * (grads - bias[...] * column), 0, keepdims=True) / gain[...]
    norm_sums[0, 1:2, :] = jnp.sum(weights * column, 0, keepdims=True)
    for part in range(3):
        grad_w[part * HEAD_DIM : (part + 1) * HEAD_DIM, width:] = tap_columns[part].astype(BF)
    for k in range(ns):
        grads_out[k] = grad_raw[:, k * rows : (k + 1) * rows]


def middle_kernel(ns, place, *refs):
    pieces = refs[:ns]
    tokens, w_o, cotangent, gain, bias, w_up, w_down = refs[ns : ns + 7]
    mixed, grad_middle, grad_low, sent, kept, normed_low, sums, grad_attn, attn = refs[ns + 7 : ns + 16]
    middle, normed_two, grad_normed, scale = refs[ns + 16 :]
    step = pl.program_id(0)
    steps = pl.num_programs(0)

    @pl.when(step == 0)
    def _():
        for k in range(ns):
            part = pieces[k].shape[0]
            attn[pl.ds(pl.multiple_of((place[0] ^ k) * part, part), part), :] = pieces[k][...]
        value = tokens[...].astype(F32) + tn(attn[...], w_o[...])
        normed, inv_scale = norm_stats(value)
        middle[...] = value
        normed_two[...] = normed
        scale[...] = jnp.broadcast_to(inv_scale, scale.shape)
        normed_low[...] = (normed * gain[...] + bias[...]).astype(BF)
        grad_normed[...] = jnp.zeros_like(grad_normed)

    positive = jnp.maximum(nn(normed_low[...], w_up[...]), 0.0)
    hidden = (positive * positive).astype(BF)
    grad_pre = (nt(cotangent[...], w_down[...]) * (2.0 * positive)).astype(BF)

    @pl.when(step < steps // 2)
    def _():
        sent[0] = hidden
        sent[1] = grad_pre

    @pl.when(step >= steps // 2)
    def _():
        kept[0] = hidden
        kept[1] = grad_pre

    middle[...] += nn(hidden, w_down[...])
    grad_normed[...] += nt(grad_pre, w_up[...])

    @pl.when(step == steps - 1)
    def _():
        mixed[...] = middle[...].astype(BF)
        back, grad_gain, grad_bias = norm_back(grad_normed[...], normed_two[...], scale[:, 0:1], gain[...])
        total = cotangent[...].astype(F32) + back
        grad_middle[...] = total
        low = total.astype(BF)
        grad_low[...] = low
        row = lax.broadcasted_iota(jnp.int32, sums.shape, 0)
        sums[...] = jnp.where(row == 0, grad_gain, jnp.where(row == 1, grad_bias, 0.0))
        grad_attn[...] = nt(w_o[...], low).astype(BF)


def grad_units(pre_low, pre_high, normed):
    both = jnp.concatenate([jnp.transpose(pre_low[0]), jnp.transpose(pre_high[0])], 0)
    grads = nn(both, normed[...])
    rows = grads.shape[0] // 2
    return jnp.concatenate([grads[:rows], grads[rows:]], 1)


def rest_kernel(place, grad_low, attn_sent, attn_kept, sums, sent, kept):
    columns = jnp.transpose(grad_low[...])
    width = columns.shape[0]
    filled = jnp.transpose(jnp.concatenate([sums[...], jnp.zeros((128 - sums.shape[0], width), F32)], 0)).astype(BF)
    for attn, rest in ((attn_sent, sent), (attn_kept, kept)):
        half = attn.shape[0]
        rest[:, :half] = nt(columns, attn[...]).astype(BF)
        rest[:, half:] = filled


def weight_kernel(phase, place, *refs):
    g_own, g_got, hidden_own, hidden_got, low_own, low_got, high_own, high_got, n_own, n_got = refs[:10]
    grad_down, grad_up = refs[10 + 2 * phase : 12 + 2 * phase]

    if phase == 1:
        @pl.when(pl.program_id(0) == 0)
        def _():
            refs[14][...] = (refs[10][...].astype(F32) + refs[11][...].astype(F32)).astype(BF)

    grad_down[...] = (nn(g_own[...], hidden_own[0]) + nn(g_got[...], hidden_got[0])).astype(BF)
    pre_own = jnp.concatenate([jnp.transpose(low_own[0]), jnp.transpose(high_own[0])], 0)
    pre_got = jnp.concatenate([jnp.transpose(low_got[0]), jnp.transpose(high_got[0])], 0)
    grads = (nn(pre_own, n_own[...]) + nn(pre_got, n_got[...])).astype(BF)
    rows, width = (grads.shape[0] // 2, grads.shape[1])
    grad_up[:, :width] = grads[:rows]
    grad_up[:, width:] = grads[rows:]


def sum_refs(refs, index):
    total = refs[0][index].astype(F32)
    for ref in refs[1:]:
        total = total + ref[index].astype(F32)
    return total


def turn_y_kernel(heads, head_rows, place, up_kept, up_got, pair, rest_z, down_kept, down_got, y_sent, y_kept, *downs):
    y, z = (place[3], place[4])
    z_size, piece, _ = y_sent.shape
    wide, lanes = (up_kept.shape[1], pair.shape[1])
    rest = rest_z.shape[2]
    x_size = rest_z.shape[1] // (2 * piece)
    times = z_size // x_size
    cut = rest // times
    parts = heads * 3
    for side, result in ((1 - y, y_sent), (y, y_kept)):
        block = z_size * piece
        at = pl.ds(pl.multiple_of(side * block, block), block)
        result[:, :, :wide] = sum_refs((up_kept, up_got), (at, slice(None))).astype(BF).reshape(z_size, piece, wide)
        run = z_size * head_rows
        taken = [
            pair[pl.ds(pl.multiple_of(p * HEAD_DIM + side * run, run), run), :].astype(F32) for p in range(parts)
        ]
        for i in range(z_size):
            rows = jnp.concatenate([v[i * head_rows : (i + 1) * head_rows] for v in taken], 0)
            result[i, :, wide : wide + lanes] = rows.astype(BF)
        for x in range(x_size):
            at = pl.ds(pl.multiple_of((side * x_size + x) * piece, piece), piece)
            total = rest_z[0, at, :].astype(F32)
            for i in range(1, rest_z.shape[0]):
                total = total + rest_z[i, at, :].astype(F32)
            for i in range(times):
                result[x * times + i, :, wide + lanes :] = total[:, i * cut : (i + 1) * cut].astype(BF)
    block = downs[0].shape[0]
    for m, result in enumerate(downs):
        at = pl.ds(pl.multiple_of((z ^ m) * block, block), block)
        result[...] = sum_refs((down_kept, down_got), (at, slice(None))).astype(BF)


def turn_z_kernel(rest, place, *refs):
    y_kept, y_got, last_kept, last_got, own, one, two, three, sent, kept = refs[:10]
    ups = refs[10:]
    x, z = (place[2], place[4])
    last_lanes = last_kept.shape[2]
    wide = ups[0].shape[1] - last_lanes // 2
    z_size, piece, lanes = y_kept.shape
    last_rows = last_kept.shape[1]
    for m, result in enumerate(ups):
        result[:, :wide] = sum_refs((y_kept, y_got), (z ^ m, slice(None), slice(0, wide))).astype(BF)
        last = sum_refs((last_kept, last_got), z ^ m)
        last = jnp.concatenate([last[:, : last_lanes // 2], last[:, last_lanes // 2 :]], 0)
        result[:, wide:] = last.astype(BF)
    cut = lanes - wide
    times = rest // cut
    half = own.shape[1]
    for side, result in ((1 - x, sent), (x, kept)):
        at = pl.ds(pl.multiple_of(side * piece, piece), piece)
        result[:, :half] = sum_refs((own, one, two, three), (at, slice(None))).astype(BF)
        for i in range(times):
            both = sum_refs((y_kept, y_got), (side * times + i, slice(None), slice(wide, lanes)))
            result[:, half + i * cut : half + (i + 1) * cut] = both.astype(BF)


def final_kernel(heads, groups, place, *refs):
    pieces, weights, (tokens, gain, grad_middle, d_tokens, stacked) = (refs[: len(groups)], refs[len(groups) : -5], refs[-5:])
    for (first, size), piece in zip(groups, pieces):
        for k in range(piece.shape[0]):
            for h in range(size):
                begin = (k * heads + first + h) * HEAD_DIM
                for part in range(3):
                    row = (h * 3 + part) * HEAD_DIM
                    stacked[part, begin : begin + HEAD_DIM, :] = piece[k, row : row + HEAD_DIM, :]
    grad_normed = nt(jnp.transpose(stacked[0]), weights[0][...])
    for part in (1, 2):
        grad_normed = grad_normed + nt(jnp.transpose(stacked[part]), weights[part][...])
    normed, inv_scale = norm_stats(tokens[...].astype(F32))
    back, _, _ = norm_back(grad_normed, normed, inv_scale, gain[...])
    d_tokens[...] = (grad_middle[...] + back).astype(BF)


def whole(shape):
    return pl.BlockSpec(shape, lambda *_: (0,) * len(shape))


def shaped(shape, dtype):
    return jax.ShapeDtypeStruct(shape, dtype)


def call(kernel, grid, inputs, outputs, scratch, flops, moved, name, place, ties=(), token=False, through=(), onto=()):
    count = len(inputs)
    held = len(ties) + len(through) + len(onto)
    end = count + held + len(outputs)

    def body(place, *refs):
        kernel(place, *refs[:count], *refs[count + held : end], *refs[end + token + len(through) :])
        if token:
            refs[end][...] = jnp.zeros_like(refs[end])

    aliases = {}
    for i, (_, result) in enumerate(onto):
        aliases[1 + count + len(ties) + len(through) + i] = result
    if token:
        outputs = [*outputs, out((8, 128), F32)]
    for array in through:
        aliases[1 + count + len(ties) + len(aliases) - len(onto)] = len(outputs)
        outputs = [*outputs, (array.shape, array.dtype, pl.BlockSpec(memory_space=pl.ANY))]

    return pl.pallas_call(
        body,
        grid_spec=pltpu.PrefetchScalarGridSpec(
            num_scalar_prefetch=1,
            grid=grid,
            in_specs=[spec for _, spec in inputs] + [pl.BlockSpec(memory_space=pl.ANY)] * held,
            out_specs=[spec for _, _, spec in outputs],
            scratch_shapes=scratch,
        ),
        out_shape=[jax.ShapeDtypeStruct(shape, dtype) for shape, dtype, _ in outputs],
        compiler_params=pltpu.CompilerParams(vmem_limit_bytes=VMEM_LIMIT),
        cost_estimate=pl.CostEstimate(flops=flops // COST, bytes_accessed=moved // COST, transcendentals=0),
        name=name,
        input_output_aliases=aliases,
    )(place, *[array for array, _ in inputs], *ties, *through, *[array for array, _ in onto])


def full(array):
    return (array, whole(array.shape))


def out(shape, dtype):
    return (shape, dtype, whole(shape))


def swap(values, axis, count, mask):
    return lax.ppermute(values, axis, [(i, i ^ mask) for i in range(count)])


def add_all(terms):
    total = terms[0].astype(F32)
    for one in terms[1:]:
        total = total + jnp.asarray(one, F32)
    return total


def after(values, ties, place):
    anywhere = pl.BlockSpec(memory_space=pl.ANY)
    return pl.pallas_call(
        lambda *refs: None,
        in_specs=[pl.BlockSpec(memory_space=pltpu.SMEM)] + [anywhere] * (1 + len(ties)),
        out_specs=anywhere,
        out_shape=jax.ShapeDtypeStruct(values.shape, values.dtype),
        input_output_aliases={1: 0},
        name="after",
    )(place, values, *ties)


def add_low(*terms):
    return add_all(terms).astype(BF)


def sides(values, index, dim):
    block = values.shape[dim] // 2
    return [lax.dynamic_slice_in_dim(values, i * block, block, dim) for i in (index, 1 - index)]


def scatter(values, axis, groups=None):
    return lax.all_to_all(values, axis, split_axis=0, concat_axis=0, tiled=True, axis_index_groups=groups)


def zero_of(values):
    return jnp.minimum(jnp.abs(values[(0,) * values.ndim].astype(F32)), 0.0)


def local(tokens, segment_ids, cotangent, w_q, w_k, w_v, conv_weight, w_o, gain_one, bias_one, gain_two, bias_two, w_up, w_down):
    ns, nb = (lax.axis_size("seq"), lax.axis_size("batch"))
    s_index, b_index = (lax.axis_index("seq"), lax.axis_index("batch"))
    cores, y_size = (2, 2)
    x_size, z_size = (ns // cores, nb // y_size)
    rows, width = tokens.shape
    units = w_up.shape[1]
    heads = width // HEAD_DIM // ns
    length = rows * ns
    part = 3 * HEAD_DIM
    mine = heads * HEAD_DIM
    core = s_index % cores
    place = jnp.stack([s_index, core, s_index // cores, b_index % y_size, b_index // y_size]).astype(jnp.int32)
    gain_one, bias_one, gain_two, bias_two = (v.reshape(1, width) for v in (gain_one, bias_one, gain_two, bias_two))
    groups = [(0, heads - 1), (heads - 1, 1)]

    def to_core(values):
        return swap(values, "seq", ns, 1)

    toks = [tokens] + [None] * (ns - 1)
    for k in range(2, ns, 2):
        toks[k] = swap(tokens, "seq", ns, k)
    toks[1] = to_core(tokens)
    codes = jnp.stack([segment_ids // 256, segment_ids % 256]).astype(BF)
    codes = [jnp.pad(codes, ((0, ID_ROWS - 2), (0, width - rows)))] + [None] * (ns - 1)
    for k in range(2, ns, 2):
        codes[k] = swap(codes[0], "seq", ns, k)
    for k in range(1, ns, 2):
        codes[k] = to_core(codes[k - 1])
    columns, cut = (cotangent, width // z_size)
    if cut // 2 % 16:
        columns = columns.reshape(rows, z_size, y_size, width // nb)
        columns, cut = (jnp.transpose(columns, (0, 2, 1, 3)).reshape(rows, width), width)
    own = [lax.dynamic_slice_in_dim(w, s_index * mine, mine, 1) for w in (w_q, w_k, w_v)]
    taps = jnp.transpose(
        lax.dynamic_slice_in_dim(conv_weight, s_index * mine, mine, 2).reshape(3, 3, heads, HEAD_DIM), (2, 0, 3, 1)
    ).reshape(heads * part, 3)

    normed_shape, raw_shape = ((length, width), (heads * part, length))

    def sequence_out(first):
        return [
            (normed_shape, BF, pl.BlockSpec((rows, width), lambda i, place: (place[0] ^ (first + i), 0))),
            (raw_shape, BF, pl.BlockSpec((heads * part, rows), lambda i, place: (0, place[0] ^ (first + i)))),
        ]

    flipped, columns_own, normed_in, raw = call(
        functools.partial(near_kernel, heads, cut),
        (2,),
        [full(v) for v in (tokens, toks[1], gain_one, bias_one, *own, columns)],
        [out((heads * part, width), BF), out((width, rows), BF)] + sequence_out(0),
        [],
        4 * rows * width * heads * part,
        8 * rows * width,
        "near",
        place,
        [taps],
    )
    columns_other = to_core(columns_own)
    for k in range(2, ns, 2):
        toks[k] = after(toks[k], [columns_own, codes[k]], place)
        toks[k + 1] = to_core(toks[k])
    normed_in, raw, starts = call(
        functools.partial(far_kernel, ns),
        (ns - 2,),
        [full(v) for v in (*codes, *toks[2:], gain_one, bias_one, flipped)],
        sequence_out(2) + [out((1, length), jnp.int32)],
        [],
        4 * rows * width * heads * part,
        8 * length * width,
        "far",
        place,
        onto=[(normed_in, 0), (raw, 1)],
    )

    fore, hind = ((512, 512), (512, 512))

    def by_head(array, first, columns):
        return (array, pl.BlockSpec((array.shape[0] // heads, columns), lambda i, place: (first + i, 0)))

    def per_head(size, height, columns, dtype):
        return ((size * height, columns), dtype, pl.BlockSpec((height, columns), lambda i, place: (i, 0)))

    for first, size in [(0, heads)]:
        results = call(
            functools.partial(attend_kernel, ns, *fore),
            (size,),
            [full(starts), by_head(raw, first, length), by_head(taps, first, 3)],
            [per_head(size, HEAD_DIM, rows, BF)] * ns
            + [
                per_head(size, HEAD_DIM, length, F32),
                ((size, 1, length), F32, pl.BlockSpec((1, 1, length), lambda i, place: (i, 0, 0))),
                per_head(size, part, length, BF),
            ],
            [],
            2 * length * length * HEAD_DIM * 4 * size,
            part * length * 4,
            "attend",
            place,
            [columns_other],
        )
        attn_pieces = [results[0]] + [swap(results[k], "seq", ns, k) for k in range(1, ns)]
        out_full, lse, conv = results[ns:]

    chunk = 512
    half = units // 2
    steps = half // chunk

    def unit_block(i, place):
        return jnp.where(i < steps, 1 - place[1], place[1]) * steps + lax.rem(i, steps)

    pair = (2, rows, half)
    results = call(
        functools.partial(middle_kernel, ns),
        (2 * steps,),
        [full(v) for v in (*attn_pieces, tokens, w_o, cotangent, gain_two, bias_two)]
        + [
            (w_up, pl.BlockSpec((width, chunk), lambda i, place: (0, unit_block(i, place)))),
            (w_down, pl.BlockSpec((chunk, width), lambda i, place: (unit_block(i, place), 0))),
        ],
        [
            out((rows, width), BF),
            out((rows, width), F32),
            out((rows, width), BF),
            (pair, BF, pl.BlockSpec((2, rows, chunk), lambda i, place: (0, 0, jnp.minimum(i, steps - 1)))),
            (pair, BF, pl.BlockSpec((2, rows, chunk), lambda i, place: (0, 0, jnp.maximum(i - steps, 0)))),
            out((rows, width), BF),
            out((8, width), F32),
            out((width, rows), BF),
            out((width, rows), BF),
        ],
        [pltpu.VMEM((rows, width), F32)] * 3 + [pltpu.VMEM((rows, 128), F32)],
        8 * rows * width * units + 4 * rows * width * width,
        4 * width * units,
        "middle",
        place,
    )
    mixed, grad_middle, grad_low, sent, kept, normed_mid, sums_two, grad_attn, attn = results
    grad_attn = scatter(grad_attn.reshape(ns, mine, rows), "seq")
    normed_other = to_core(normed_mid)
    got = to_core(sent)

    half_width = width // 2
    piece = 128
    steps = half // 4 // piece
    chunk = half // steps
    lanes = width + 128

    rest = half_width + 128
    rest_sent, rest_kept = call(
        rest_kernel,
        (1,),
        [
            full(grad_low),
            (attn, pl.BlockSpec((half_width, rows), lambda i, place: (1 - place[1], 0))),
            (attn, pl.BlockSpec((half_width, rows), lambda i, place: (place[1], 0))),
            full(sums_two),
        ],
        [out((width, rest), BF), out((width, rest), BF)],
        [],
        2 * rows * width * width,
        4 * width * width,
        "rest",
        place,
    )
    rest_got = to_core(rest_sent)
    def weights(phase, rest_parts=(), ties=()):
        def x_half(place):
            return (1 - place[2] if phase == 0 else place[2]) * steps

        return call(
            functools.partial(weight_kernel, phase),
            (steps,),
            [
                (v, pl.BlockSpec((half_width, rows), lambda i, place: (1 - place[3] if phase == 0 else place[3], 0)))
                for v in (columns_own, columns_other)
            ]
            + [(v, pl.BlockSpec((1, rows, chunk), lambda i, place: (0, 0, i))) for v in (kept, got)]
            + [(v, pl.BlockSpec((1, rows, piece), lambda i, place: (1, 0, x_half(place) + i))) for v in (kept, got)]
            + [
                (v, pl.BlockSpec((1, rows, piece), lambda i, place: (1, 0, 2 * steps + x_half(place) + i)))
                for v in (kept, got)
            ]
            + [full(v) for v in (normed_mid, normed_other, *rest_parts)],
            [
                ((half_width, half), BF, pl.BlockSpec((half_width, chunk), lambda i, place: (0, i))),
                ((half // 4, 2 * width), BF, pl.BlockSpec((piece, 2 * width), lambda i, place: (i, 0))),
            ]
            + [out(v.shape, BF) for v in rest_parts[:1]],
            [],
            2 * rows * width * units,
            3 * width * units,
            "weights",
            place,
            ties,
        )

    chips = nb * x_size
    x_index, y_index = (s_index // cores, b_index % y_size)
    z_groups = [[z * y_size + y for z in range(z_size)] for y in range(y_size)]

    down_sent, up_sent = weights(0)
    up_got = swap(up_sent, "seq", ns, cores)
    down_got = swap(down_sent, "batch", nb, 1)
    down_kept, up_kept, rest_sum = weights(1, (rest_kept, rest_got), [grad_attn, up_sent])
    rest_z = scatter(rest_sum.reshape(z_size, width // z_size, rest), "batch", z_groups)

    head_rows = HEAD_DIM // nb

    back_pieces, head_grads, sums_heads = ([], [], [])

    def back(g, ties):
        first, size = groups[g]
        results = call(
            functools.partial(attend_back_kernel, ns, *hind),
            (size,),
            [
                full(starts),
                by_head(conv, first, length),
                by_head(raw, first, length),
                by_head(taps, first, 3),
                by_head(flipped, first, width),
                full(gain_one),
                full(bias_one),
                full(normed_in),
                by_head(out_full, first, length),
                (lse, pl.BlockSpec((1, 1, length), lambda i, place: (first + i, 0, 0))),
            ]
            + [(grad_attn, pl.BlockSpec((ns, HEAD_DIM, rows), lambda i, place: (0, first + i, 0)))],
            [
                ((ns, size * part, rows), BF, pl.BlockSpec((ns, part, rows), lambda i, place: (0, i, 0))),
                per_head(size, part, lanes, BF),
                ((size, 2, width), F32, pl.BlockSpec((1, 2, width), lambda i, place: (i, 0, 0))),
            ],
            [pltpu.VMEM((HEAD_DIM, length), BF), pltpu.VMEM((part, length), F32), pltpu.VMEM((part, length), BF)],
            2 * length * length * HEAD_DIM * 10 * size,
            length * width * 2,
            "attend_back",
            place,
            ties,
            True,
        )
        back_pieces.append(results[0])
        head_grads.append(results[1])
        sums_heads.append(results[2])
        return results[3]

    piece = half // 2 // chips
    token = back(0, [down_kept, up_kept, rest_sum])
    wide = 2 * width + lanes
    times = z_size // x_size

    def fold(values):
        return jnp.stack(jnp.split(values.reshape(x_size, -1, rest), times, -1), 1).reshape(z_size, -1, rest // times)

    def unfold(values):
        values = values.reshape(x_size, times, -1, rest // times)
        return jnp.concatenate([values[:, i] for i in range(times)], -1).reshape(-1, rest)

    aligned = head_rows % 8 == 0 and piece % 16 == 0 and z_size <= 4
    if aligned:
        turned = call(
            functools.partial(turn_y_kernel, heads - 1, head_rows),
            (1,),
            [full(v) for v in (up_kept, up_got, head_grads[0], rest_z, down_kept, down_got)],
            [out((z_size, piece, wide + rest // times), BF)] * 2 + [out((x_size * piece, half), BF)] * z_size,
            [],
            width * units,
            4 * width * units,
            "turn_y",
            place,
        )
        y_sent, y_kept, down_own, down_sent = (turned[0], turned[1], turned[2], turned[3:])
    else:
        up_there, up_here = [
            [v.reshape(z_size, piece, 2 * width) for v in side]
            for side in zip(*[sides(v, 1 - y_index, 0) for v in (up_kept, up_got)])
        ]
        pair = head_grads[0].reshape(-1, y_size, z_size, head_rows, lanes)
        pair = jnp.transpose(pair, (1, 2, 0, 3, 4)).reshape(y_size, z_size, -1, lanes)
        pair_there, pair_here = [v[0] for v in sides(pair, 1 - y_index, 0)]
        rest_there, rest_here = sides(jnp.sum(rest_z.astype(F32), 0).astype(BF), 1 - y_index, 0)
        y_sent = jnp.concatenate([add_low(*up_there), pair_there, fold(rest_there)], -1)
        y_kept = jnp.concatenate([add_low(*up_here), pair_here, fold(rest_here)], -1)
        down_sum = add_low(down_kept, down_got).reshape(z_size, -1, half)
        down_sent = [down_sum]
    y_got = swap(y_sent, "batch", nb, 1)
    if aligned:
        down_got = [swap(v, "batch", nb, (m + 1) * y_size) for m, v in enumerate(down_sent)]
    else:
        down_z = jnp.sum(scatter(down_sum, "batch", z_groups).astype(F32), 0).astype(BF)
    back_pieces[0] = scatter(back_pieces[0], "seq")
    back(1, [y_sent, *down_sent])

    total = jnp.sum(jnp.concatenate(sums_heads, 0), 0).reshape(2, z_size, y_size, ns, 3 * head_rows)
    total = jnp.transpose(total, (2, 1, 4, 0, 3)).reshape(y_size, z_size, 3 * head_rows, 2 * ns)
    last_lanes = width + 256
    total = jnp.pad(total, ((0, 0), (0, 0), (0, 0), (width + 3, last_lanes - width - 3 - 2 * ns)))
    last = jnp.transpose(head_grads[1].reshape(3, y_size, z_size, head_rows, lanes), (1, 2, 0, 3, 4))
    last = jnp.pad(last.reshape(y_size, z_size, -1, lanes), ((0, 0), (0, 0), (0, 0), (0, last_lanes - lanes)))
    last_there, last_kept = [
        add_low(*pair)[0] for pair in zip(*[sides(v, 1 - y_index, 0) for v in (last, total)])
    ]
    last_got = swap(last_there, "batch", nb, 1)
    if aligned:
        turned = call(
            functools.partial(turn_z_kernel, rest),
            (1,),
            [full(v) for v in (y_kept, y_got, last_kept, last_got, down_own, *down_got)],
            [out((piece, half + rest), BF)] * 2 + [out((piece, wide + last_lanes // 2), BF)] * z_size,
            [],
            width * units,
            2 * width * units,
            "turn_z",
            place,
            [back_pieces[0]],
            False,
            [back_pieces[1]],
        )
        x_there, x_here, up_own = turned[:3]
        up_sent, back_pieces[1] = (turned[3:-1], turned[-1])
        up_terms = [up_own] + [swap(v, "batch", nb, (m + 1) * y_size) for m, v in enumerate(up_sent)]
    else:
        last_sum = add_low(last_kept, last_got)
        last_sum = jnp.concatenate([last_sum[..., : last_lanes // 2], last_sum[..., last_lanes // 2 :]], -2)
        up_sum = jnp.concatenate([add_low(y_kept[..., :wide], y_got[..., :wide]), last_sum], -1)
        up_sent = [up_sum]
        up_terms = [jnp.sum(scatter(up_sum, "batch", z_groups).astype(F32), 0)]
        rest_y = unfold(add_low(y_kept[..., wide:], y_got[..., wide:]))
        x_there, x_here = sides(jnp.concatenate([down_z, rest_y], -1), 1 - x_index, 0)
    x_got = swap(x_there, "seq", ns, cores)
    back_pieces[1] = scatter(back_pieces[1], "seq")

    d_tokens, token = call(
        functools.partial(final_kernel, heads, groups),
        (1,),
        [full(v) for v in (*back_pieces, w_q, w_k, w_v, tokens, gain_one, grad_middle)],
        [out((rows, width), BF)],
        [pltpu.VMEM((3, width, rows), BF)],
        6 * rows * width * width,
        8 * width * width,
        "final",
        place,
        up_sent,
        True,
    )
    up_z = add_all([*up_terms, token[0, 0]])
    single = jnp.concatenate(jnp.split(up_z[:, wide:], 2, 0), -1)[:, :lanes].reshape(3, head_rows, lanes)

    devices = [(d // ns, d % ns) for d in range(nb * ns)]
    everywhere = ("batch", "seq")

    pair = up_z[:, 2 * width : wide].astype(BF)
    granules = [*pair.reshape(-1, 3, head_rows, lanes), single.astype(BF)]
    norm_sums = single[:, :, width + 3 : width + 3 + 2 * ns].reshape(3 * head_rows, 2, ns)
    norm_sums = jnp.transpose(norm_sums, (2, 1, 0))
    take = lambda k: lax.dynamic_index_in_dim(norm_sums, s_index ^ k, 0, keepdims=False)
    sums_one = add_all([take(0)] + [swap(take(k), "seq", ns, k) for k in range(1, ns)])

    def position(b):
        return (b % y_size) * z_size + b // y_size

    pieces = []
    for slot in range(heads):
        perm = []
        for d, (b, s) in enumerate(devices):
            for h in range(heads):
                granule = (s * heads + h) * nb + position(b)
                if granule % heads == slot:
                    perm.append((d, granule // heads))
        ours = [(h * nb + position(b_index)) % heads == slot for h in range(heads)]
        sent = granules[-1]
        for h in range(heads - 1):
            sent = jnp.where(ours[h], granules[h], sent)
        pieces.append(lax.ppermute(sent, everywhere, perm))
    grad_qkv = jnp.concatenate(pieces, 1).astype(F32)

    size = piece
    up_value = up_z.astype(BF)
    chip = lambda b, s: ((s // cores) * y_size + b % y_size) * z_size + b // y_size
    got_up = []
    for color in range(2):
        perm = []
        for d, (b, s) in enumerate(devices):
            p = (color + chip(b, s)) % 2
            begin = (s % cores) * half + p * (half // 2) + chip(b, s) * size
            perm.append((d, begin // (2 * size)))
        first = (color + chip(b_index, s_index)) % 2 == 0
        got_up.append(lax.ppermute(jnp.where(first, up_value[:, :width], up_value[:, width : 2 * width]), everywhere, perm))
    first = (b_index * ns + s_index) * 2 * size % half < half // 2
    got_up = [jnp.where(first, got_up[0], got_up[1]), jnp.where(first, got_up[1], got_up[0])]
    got_up = jnp.concatenate(got_up, 0).astype(F32)

    value = add_low(x_here, x_got)
    size = value.shape[0] // cores
    here = lax.dynamic_slice_in_dim(value, core * size, size, 0)
    there = to_core(lax.dynamic_slice_in_dim(value, (1 - core) * size, size, 0))
    by_core = [jnp.where(core == 0, here, there).astype(F32), jnp.where(core == 0, there, here).astype(F32)]
    got_down = jnp.concatenate([v[:, :half] for v in by_core], 1)
    got_rest = jnp.concatenate([v[:, half : half + half_width] for v in by_core], 1)
    sums_two = here[:, half + half_width : half + half_width + 2].astype(F32)

    flat = jnp.swapaxes(grad_qkv[:, :, :width], 1, 2)
    return (
        mixed,
        d_tokens,
        flat[0],
        flat[1],
        flat[2],
        jnp.swapaxes(grad_qkv[:, :, width : width + 3], 1, 2),
        got_rest.T,
        sums_one[0],
        sums_one[1],
        sums_two[:, 0],
        sums_two[:, 1],
        got_up.T,
        got_down.T,
    )


def solution(mesh):
    split = ("batch", "seq")
    in_specs = (P(split, None), P(split), P(split, None)) + (P(),) * 11
    out_specs = (
        P(split, None),
        P(split, None),
        P(None, split),
        P(None, split),
        P(None, split),
        P(None, None, split),
        P(None, split),
        P(split),
        P(split),
        P(split),
        P(split),
        P(None, split),
        P(None, split),
    )
    return jax.shard_map(local, mesh=mesh, in_specs=in_specs, out_specs=out_specs, check_vma=False)
```
